32 devices in a mesh: dp: 8 (over z, y), fsdp: 4 (over x, core).
Axes of the slice: x: 2, y: 2, z: 4, core: 2. Of those that a mesh axis runs over, the one named last changes fastest.
Arguments:
- tokens: bfloat16 [512, 128, 768], P(('dp', 'fsdp')), may hold values from -6 to 6
- input_weight: bfloat16 [768, 2304], P(('dp', 'fsdp')), may hold values from -0.21875 to 0.21875
- query_bias: bfloat16 [768], P(('dp', 'fsdp')), may hold values from -1.75 to 1.75
- value_bias: bfloat16 [768], P(('dp', 'fsdp')), may hold values from -1.75 to 1.75
- output_weight: bfloat16 [768, 768], P(('dp', 'fsdp')), may hold values from -0.875 to 0.875
- output_bias: bfloat16 [768], P(('dp', 'fsdp')), may hold values from -1.75 to 1.75
- first_gain: bfloat16 [768], P(('dp', 'fsdp')), may hold values from 0.5 to 1.5
- first_shift: bfloat16 [768], P(('dp', 'fsdp')), may hold values from -1.75 to 1.75
- up_weight: bfloat16 [768, 3072], P(('dp', 'fsdp')), may hold values from -0.21875 to 0.21875
- up_bias: bfloat16 [3072], P(('dp', 'fsdp')), may hold values from -1.75 to 1.75
- down_weight: bfloat16 [3072, 768], P(('dp', 'fsdp')), may hold values from -0.109375 to 0.109375
- down_bias: bfloat16 [768], P(('dp', 'fsdp')), may hold values from -1.75 to 1.75
- second_gain: bfloat16 [768], P(('dp', 'fsdp')), may hold values from 0.5 to 1.5
- second_shift: bfloat16 [768], P(('dp', 'fsdp')), may hold values from -1.75 to 1.75
- student_weight: bfloat16 [768, 128], P(('dp', 'fsdp')), may hold values from -0.21875 to 0.21875
- student_bias: bfloat16 [128], P(('dp', 'fsdp')), may hold values from -1.75 to 1.75
- pool_query: bfloat16 [128], P(('dp', 'fsdp')), may hold values from -12 to 12
- pool_weight: bfloat16 [128, 128], P(('dp', 'fsdp')), may hold values from -0.5 to 0.5
- pool_bias: bfloat16 [128], P(('dp', 'fsdp')), may hold values from -1.75 to 1.75
- class_weight: bfloat16 [128, 14], P(('dp', 'fsdp')), may hold values from -0.5 to 0.5
- class_bias: bfloat16 [14], replicated, may hold values from -3 to 3
- lengths: int32 [512], P(('dp', 'fsdp')), may hold values from 1 to 128, 40960 in all
- exit_layer: int32 [512], P(('dp', 'fsdp')), may hold values from 6 to 9
- destination: int32 [512], replicated, may hold values from 0 to 511, as said below
- repacked_grad: bfloat16 [512, 128, 768], P(('dp', 'fsdp')), may hold values from -6 to 6
- logits_grad: bfloat16 [512, 14], P(('dp', 'fsdp')), may hold values from -6 to 6
Outputs:
- repacked: bfloat16 [512, 128, 768], P(('dp', 'fsdp'))
- student_logits: float32 [512, 14], P(('dp', 'fsdp'))
- tokens_grad: float32 [512, 128, 768], P(('dp', 'fsdp'))
- input_weight_grad: float32 [768, 2304], P(('dp', 'fsdp'))
- query_bias_grad: float32 [768], P(('dp', 'fsdp'))
- value_bias_grad: float32 [768], P(('dp', 'fsdp'))
- output_weight_grad: float32 [768, 768], P(('dp', 'fsdp'))
- output_bias_grad: float32 [768], P(('dp', 'fsdp'))
- first_gain_grad: float32 [768], P(('dp', 'fsdp'))
- first_shift_grad: float32 [768], P(('dp', 'fsdp'))
- up_weight_grad: float32 [768, 3072], P(('dp', 'fsdp'))
- up_bias_grad: float32 [3072], P(('dp', 'fsdp'))
- down_weight_grad: float32 [3072, 768], P(('dp', 'fsdp'))
- down_bias_grad: float32 [768], P(('dp', 'fsdp'))
- second_gain_grad: float32 [768], P(('dp', 'fsdp'))
- second_shift_grad: float32 [768], P(('dp', 'fsdp'))
- student_weight_grad: float32 [768, 128], P(('dp', 'fsdp'))
- student_bias_grad: float32 [128], P(('dp', 'fsdp'))
- pool_query_grad: float32 [128], P(('dp', 'fsdp'))
- pool_weight_grad: float32 [128, 128], P(('dp', 'fsdp'))
- pool_bias_grad: float32 [128], P(('dp', 'fsdp'))
- class_weight_grad: float32 [128, 14], P(('dp', 'fsdp'))
- class_bias_grad: float32 [14], replicated
The draws below stay inside these ranges and needn't reach their ends.
Inputs may be any that keep to these rules, and one draw needn't show every extreme that they name: destination is a permutation of 0 to 511 that keeps every sample inside its aligned block of 16 times (devices along fsdp) samples; of the 16 samples of one device at most 6 go to any one device, and in every draw some device sends exactly 6 to some device.
All inputs are finite; a program needn't handle non-finite values. No bound on the sum of `lengths` on one device may be relied on, other than what follows from the above.
Results may differ from the reference program's by a relative error of at most 0.025.
Values may be sent and summed in bfloat16 or wider, within the bound.
No kernel may reach another device: no remote copies, remote signals or barrier semaphores. Data moves between devices by JAX's collectives and lax.ppermute only.
A program may use at most 320 MiB of HBM per device.

```python
import math
import jax
import jax.numpy as jnp
import numpy as np
from jax import lax

D = 768
HEADS = 12
HEAD_DIM = 64
FF = 3072
STU = 128
STU_HEADS = 2
CLASSES = 14
SEQ = 128
SAMP_DEV = 16
LAYER = 6
SAMPLES = 512
N_FSDP = 4


def draw_destination(key, part):
    key = jax.random.fold_in(key, 11)
    groups = SAMPLES // (SAMP_DEV * N_FSDP)
    capacity = 3 * SAMP_DEV // (2 * N_FSDP)
    lower = 2 * SAMP_DEV // N_FSDP - capacity
    half = N_FSDP // 2
    pattern = jnp.concatenate([jnp.full((half,), capacity, jnp.int32), jnp.full((N_FSDP - half,), lower, jnp.int32)])
    count_key, order_key, slot_key = jax.random.split(key, 3)
    counts = jax.vmap(lambda subkey: pattern[jax.random.permutation(subkey, N_FSDP)])(jax.random.split(count_key, groups))
    shifts = jax.vmap(lambda row: jnp.repeat(jnp.arange(N_FSDP, dtype=jnp.int32), row, total_repeat_length=SAMP_DEV))(counts)
    order = jax.vmap(lambda subkey: jax.random.permutation(subkey, SAMP_DEV))(jax.random.split(order_key, groups * N_FSDP))
    order = order.reshape(groups, N_FSDP, SAMP_DEV).astype(jnp.int32)
    slots = jax.vmap(lambda subkey: jax.random.permutation(subkey, SAMP_DEV))(jax.random.split(slot_key, groups * N_FSDP))
    slots = slots.reshape(groups, N_FSDP, SAMP_DEV).astype(jnp.int32)
    group_ids = jnp.arange(groups, dtype=jnp.int32)[:, None, None]
    source = jnp.arange(N_FSDP, dtype=jnp.int32)[None, :, None]
    shift = shifts[group_ids, order]
    target = (source + shift) % N_FSDP
    slot = slots[group_ids, target, order]
    return ((group_ids * N_FSDP + target) * SAMP_DEV + slot).reshape(-1).astype(jnp.int32)


def plant(result, key, smallest, high):
    shape = result.shape
    spot = [jax.random.randint(jax.random.fold_in(key, axis), (), 0, shape[axis]) for axis in range(len(shape))]
    result = result.at[tuple(spot)].set(smallest)
    longest = shape.index(max(shape))
    spot[longest] = (spot[longest] + 1) % shape[longest]
    return result.at[tuple(spot)].set(high)


def shard_levels(stream_key, dims, pieces, smallest, largest):
    def one(position, shards_of):
        draws = jax.random.uniform(jax.random.fold_in(jax.random.fold_in(stream_key, 6), position), (shards_of,), jnp.float32, smallest / len(pieces), largest / len(pieces))
        return jnp.repeat(jnp.exp(draws), dims[position] // shards_of).reshape((-1,) + (1,) * (len(dims) - position - 1))

    level = one(*pieces[0])
    for cut in pieces[1:]:
        level = level * one(*cut)
    return level


def split_up(number_of, total, limit, lean):
    weights = [(1 << 20) // math.isqrt(grade ** lean) + 1 for grade in range(2, number_of + 1)]
    rest, given = total - limit - (number_of - 1), [1] * (number_of - 1)
    while rest > 0:
        candidates = [i for i in range(number_of - 1) if given[i] < limit]
        pool, left = sum([weights[i] for i in candidates]), rest
        for i in candidates:
            addition = min(limit - given[i], max(1, left * weights[i] // pool), rest)
            given[i] = given[i] + addition
            rest = rest - addition
    return np.array([limit] + given)


def uneven_parts(rng, number_of, total, bound, skew):
    if number_of == 2:
        one = jax.random.randint(rng, (), max(1, total - bound), min(bound, total - 1) + 1)
        return jnp.stack([one, total - one])
    sizes = jnp.asarray(split_up(number_of, total, bound, skew), jnp.int32)
    couples = (number_of - 1) // 2
    source_of, receiver = sizes[1:1 + 2 * couples:2], sizes[2:2 + 2 * couples:2]
    margin = jnp.minimum(source_of - 1, bound - receiver)
    shifted = jax.random.randint(jax.random.fold_in(rng, 1), (couples,), 0, 1 << 20) % (margin + 1)
    sizes = sizes.at[1:1 + 2 * couples:2].set(source_of - shifted).at[2:2 + 2 * couples:2].set(receiver + shifted)
    return sizes[jax.random.permutation(jax.random.fold_in(rng, 2), number_of)]


def bell_draw(rng, dims, spread, limit, pieces=(), kind=jnp.bfloat16):
    result = spread * jax.random.normal(rng, dims, jnp.float32)
    if pieces:
        result = result * shard_levels(rng, dims, pieces, -0.22, 0.18)
    return jnp.clip(result, -limit, limit).astype(kind)


def setup_inputs(seed: int = 0) -> dict:
    streams_of = jax.random.split(jax.random.key(seed), 27)
    return {
        "tokens": bell_draw(streams_of[0], (SAMPLES, SEQ, D), 1.0, 6.0, ((0, 32),)),
        "input_weight": bell_draw(streams_of[1], (D, 3 * D), D ** -0.5, 0.21875, ((0, 32),)),
        "query_bias": bell_draw(streams_of[2], (D,), 0.3, 1.75, ((0, 32),)),
        "value_bias": bell_draw(streams_of[3], (D,), 0.3, 1.75, ((0, 32),)),
        "output_weight": bell_draw(streams_of[4], (D, D), (D // 16) ** -0.5, 0.875, ((0, 32),)),
        "output_bias": bell_draw(streams_of[5], (D,), 0.3, 1.75, ((0, 32),)),
        "first_gain": jnp.clip(1.0 + 0.1 * jax.random.normal(streams_of[6], (D,), jnp.float32), 0.5, 1.5).astype(jnp.bfloat16),
        "first_shift": bell_draw(streams_of[7], (D,), 0.3, 1.75, ((0, 32),)),
        "up_weight": bell_draw(streams_of[8], (D, FF), D ** -0.5, 0.21875, ((0, 32),)),
        "up_bias": bell_draw(streams_of[9], (FF,), 0.3, 1.75, ((0, 32),)),
        "down_weight": bell_draw(streams_of[10], (FF, D), FF ** -0.5, 0.109375, ((0, 32),)),
        "down_bias": bell_draw(streams_of[11], (D,), 0.3, 1.75, ((0, 32),)),
        "second_gain": jnp.clip(1.0 + 0.1 * jax.random.normal(streams_of[12], (D,), jnp.float32), 0.5, 1.5).astype(jnp.bfloat16),
        "second_shift": bell_draw(streams_of[13], (D,), 0.3, 1.75, ((0, 32),)),
        "student_weight": bell_draw(streams_of[14], (D, STU), D ** -0.5, 0.21875, ((0, 32),)),
        "student_bias": bell_draw(streams_of[15], (STU,), 0.3, 1.75, ((0, 32),)),
        "pool_query": bell_draw(streams_of[16], (STU,), 2.0, 12.0, ((0, 32),)),
        "pool_weight": bell_draw(streams_of[17], (STU, STU), STU ** -0.5, 0.5, ((0, 32),)),
        "pool_bias": bell_draw(streams_of[18], (STU,), 0.3, 1.75, ((0, 32),)),
        "class_weight": bell_draw(streams_of[19], (STU, CLASSES), STU ** -0.5, 0.5, ((0, 32),)),
        "class_bias": bell_draw(streams_of[20], (CLASSES,), 0.5, 3.0),
        "lengths": uneven_parts(streams_of[21], SAMPLES, SAMPLES * SEQ * 5 // 8, SEQ, 1).astype(jnp.int32),
        "exit_layer": plant(jax.random.randint(streams_of[22], (SAMPLES,), LAYER, LAYER + 4), jax.random.fold_in(streams_of[22], 1), LAYER, (LAYER + 4) - 1).astype(jnp.int32),
        "destination": draw_destination(jax.random.fold_in(streams_of[26], 71), 0),
        "repacked_grad": bell_draw(streams_of[24], (SAMPLES, SEQ, D), 1.0, 6.0, ((0, 32),)),
        "logits_grad": bell_draw(streams_of[25], (SAMPLES, CLASSES), 1.0, 6.0, ((0, 32),)),
    }


EPS = 1e-06
MASKED = -1e+30
EXACT = lax.Precision.HIGHEST

@jax.custom_vjp
def low(v):
    return lax.optimization_barrier(v.astype(jnp.bfloat16)).astype(jnp.float32)

@jax.custom_vjp
def low_back(v):
    return v

def low_keep(v):
    return (low(v), None)

def low_pass(kept, grad):
    return (grad,)

def back_keep(v):
    return (v, None)

def back_low(kept, grad):
    return (low(grad),)
low.defvjp(low_keep, low_pass)
low_back.defvjp(back_keep, back_low)

def matmul(left, right):
    return jnp.dot(left, right, precision=EXACT, preferred_element_type=jnp.float32)

def layer_norm(total, gain, shift):
    mean = lax.optimization_barrier(jnp.mean(total, axis=-1, keepdims=True))
    centered = total - mean
    return centered * lax.rsqrt(lax.optimization_barrier(jnp.mean(centered * centered, axis=-1, keepdims=True)) + EPS) * gain + shift

def forward(params, block, block_lengths):
    input_weight, query_bias, value_bias, output_weight, output_bias, first_gain, first_shift, up_weight, up_bias, down_weight, down_bias, second_gain, second_shift, student_weight, student_bias, pool_query, pool_weight, pool_bias, class_weight, class_bias = params
    count = block.shape[0]
    rows = block.reshape(count * SEQ, D)
    projected = matmul(rows, input_weight)
    query = low_back(low(projected[:, :D] + query_bias)).reshape(count, SEQ, HEADS, HEAD_DIM)
    key = low_back(low(projected[:, D:2 * D])).reshape(count, SEQ, HEADS, HEAD_DIM)
    value = low_back(low(projected[:, 2 * D:] + value_bias)).reshape(count, SEQ, HEADS, HEAD_DIM)
    scores = low_back(jnp.einsum('bqhd,bkhd->bhqk', query, key, precision=EXACT) / math.sqrt(HEAD_DIM))
    valid = jnp.arange(SEQ, dtype=jnp.int32)[None, :] < block_lengths[:, None]
    attention = low(jax.nn.softmax(jnp.where(valid[:, None, None, :], scores, MASKED), axis=-1))
    mixed = jnp.einsum('bhqk,bkhd->bqhd', attention, value, precision=EXACT).reshape(count * SEQ, D)
    mixed = low_back(low(mixed))
    attended = low_back(matmul(mixed, output_weight) + output_bias)
    first = layer_norm(rows + attended, first_gain, first_shift)
    up = low_back(matmul(low(first), up_weight) + up_bias)
    activated = low(jax.nn.gelu(up, approximate=False))
    down = low_back(matmul(activated, down_weight) + down_bias)
    second = low(layer_norm(first + down, second_gain, second_shift))
    pool_width = STU // STU_HEADS
    reduced = low_back(low(matmul(second, student_weight) + student_bias)).reshape(count, SEQ, STU_HEADS, pool_width)
    query_pool = pool_query.reshape(STU_HEADS, pool_width)
    pool_scores = jnp.einsum('bshd,hd->bhs', reduced, query_pool, precision=EXACT) / math.sqrt(pool_width)
    pool_share = jax.nn.softmax(jnp.where(valid[:, None, :], pool_scores, MASKED), axis=-1)
    pooled = jnp.einsum('bhs,bshd->bhd', pool_share, reduced, precision=EXACT).reshape(count, STU)
    pooled = low_back(low(pooled))
    hidden = low_back(matmul(pooled, pool_weight) + pool_bias)
    logits = matmul(low(jnp.tanh(hidden)), class_weight) + class_bias
    return (second.reshape(count, SEQ, D), logits)

def reference(tokens, input_weight, query_bias, value_bias, output_weight, output_bias, first_gain, first_shift, up_weight, up_bias, down_weight, down_bias, second_gain, second_shift, student_weight, student_bias, pool_query, pool_weight, pool_bias, class_weight, class_bias, lengths, exit_layer, destination, repacked_grad, logits_grad):
    params = tuple((piece.astype(jnp.float32) for piece in (input_weight, query_bias, value_bias, output_weight, output_bias, first_gain, first_shift, up_weight, up_bias, down_weight, down_bias, second_gain, second_shift, student_weight, student_bias, pool_query, pool_weight, pool_bias, class_weight, class_bias)))
    group = min(SAMPLES, max(1, 4096 // SEQ))
    blocks = SAMPLES // group
    survives = exit_layer > LAYER

    def step(carry, index):
        start = (index * group).astype(jnp.int32)
        block = lax.dynamic_slice_in_dim(tokens, start, group).astype(jnp.float32)
        block_lengths = lax.dynamic_slice_in_dim(lengths, start, group)
        block_slots = lax.dynamic_slice_in_dim(destination, start, group)
        block_alive = lax.dynamic_slice_in_dim(survives, start, group)
        second_cot = jnp.where(block_alive[:, None, None], repacked_grad[block_slots].astype(jnp.float32), 0.0)
        logits_cot = lax.dynamic_slice_in_dim(logits_grad, start, group).astype(jnp.float32)
        outputs, backward = jax.vjp(lambda weights, inputs: forward(weights, inputs, block_lengths), params, block)
        param_grads, block_grad = backward((second_cot, logits_cot))
        carry = jax.tree.map(jnp.add, carry, param_grads)
        kept_rows = jnp.where(block_alive[:, None, None], outputs[0], 0.0).astype(jnp.bfloat16)
        return (carry, (kept_rows, outputs[1], block_grad))
    zeros = jax.tree.map(jnp.zeros_like, params)
    totals, (kept_rows, logits, token_grads) = lax.scan(step, zeros, jnp.arange(blocks, dtype=jnp.int32))
    kept_rows = kept_rows.reshape(SAMPLES, SEQ, D)
    repacked = jnp.zeros_like(kept_rows).at[destination].set(kept_rows)
    return (repacked, logits.reshape(SAMPLES, CLASSES), token_grads.reshape(SAMPLES, SEQ, D), totals[0], totals[1], totals[2], totals[3], totals[4], totals[5], totals[6], totals[7], totals[8], totals[9], totals[10], totals[11], totals[12], totals[13], totals[14], totals[15], totals[16], totals[17], totals[18], totals[19])
```

```python
import functools
import itertools
import math

import jax
import jax.numpy as jnp
from jax import lax
from jax.experimental import pallas as pl
from jax.experimental.pallas import tpu as pltpu
from jax.sharding import PartitionSpec as P

HEADS = 12
HEAD_DIM = 64
STU_HEADS = 2
LAYER = 6
EPS = 1e-06
MASKED = -1e30
AXES = ("dp", "fsdp")
F32 = jnp.float32
BF16 = jnp.bfloat16
VMEM_LIMIT = 60 * 1024 * 1024

QB, VB, OB, G1, S1, DB, G2, S2 = range(8)


def dot(left, right):
    return jnp.dot(left, right, preferred_element_type=F32)


def dot_nt(left, right):
    return lax.dot_general(left, right, (((1,), (1,)), ((), ())), preferred_element_type=F32)


def dot_tn(left, right):
    return lax.dot_general(left, right, (((0,), (0,)), ((), ())), preferred_element_type=F32)


def params(limit=VMEM_LIMIT):
    return pltpu.CompilerParams(vmem_limit_bytes=limit, dimension_semantics=("arbitrary",))


def cost(flops, nbytes):
    return pl.CostEstimate(flops=int(flops), bytes_accessed=int(nbytes), transcendentals=0)


def whole(shape, index=None):
    index = index or (0,) * len(shape)
    return pl.BlockSpec(shape, lambda i, *_: index, pipeline_mode=pl.Buffered(1))


def rows_spec(rows, width):
    return pl.BlockSpec((rows, width), lambda i, *_: (i, 0))


def kept(shape):
    return pl.BlockSpec(shape, lambda i, *_: (0,) * len(shape))


def layer_norm(total):
    mean = jnp.mean(total, axis=-1, keepdims=True)
    centered = total - mean
    factor = lax.rsqrt(jnp.mean(centered * centered, axis=-1, keepdims=True) + EPS)
    return centered * factor, factor


def layer_norm_back(cot, gain, normed, factor):
    scaled = cot * gain
    inner = (
        scaled
        - jnp.mean(scaled, axis=-1, keepdims=True)
        - normed * jnp.mean(scaled * normed, axis=-1, keepdims=True)
    )
    return factor * inner


def gelu_parts(up):
    size = jnp.abs(up) * (1.0 / math.sqrt(2.0))
    near = 1.0 / (1.0 + 0.3275911 * size)
    bell = jnp.exp(-(size * size))
    series = near * (
        0.5 * 0.254829592
        + near
        * (
            0.5 * -0.284496736
            + near * (0.5 * 1.421413741 + near * (0.5 * -1.453152027 + near * (0.5 * 1.061405429)))
        )
    )
    tail = series * bell
    phi = jnp.where(up >= 0.0, 1.0 - tail, tail)
    slope = phi + up * (bell * (1.0 / math.sqrt(2.0 * math.pi)))
    return up * phi, slope


def column_sum(matrix):
    return jnp.sum(matrix, axis=0, keepdims=True)


def stack_rows(rows, count):
    width = rows[0].shape[1]
    pad = count - len(rows)
    if pad:
        rows = list(rows) + [jnp.zeros((pad, width), F32)]
    return jnp.concatenate(rows, axis=0)


def one_hot_rows(count, width, group, stride, skip):
    row = lax.broadcasted_iota(jnp.int32, (count, width), 0)
    column = lax.broadcasted_iota(jnp.int32, (count, width), 1)
    shift = group.bit_length() - 1
    wanted = (row >> shift) * stride + skip + (row & (group - 1))
    return jnp.where(column == wanted, 1.0, 0.0).astype(BF16)


def turn_lanes(matrix):
    return pltpu.roll(matrix, 64, 1)


def read_small(block, vec_ref, sv_ref, pw_ref, cw_ref, ub_ref, stu, classes, devices):
    width = block.shape[0]
    shard = width // devices
    group = stu // devices
    lane = lax.broadcasted_iota(jnp.int32, (stu, 128), 1)
    left, right, rest = (
        dot(one_hot_rows(stu, width, group, shard, n * group), block) for n in range(3)
    )
    pw_ref[...] = jnp.where(lane < 64, turn_lanes(left), right).astype(BF16)
    rest = turn_lanes(rest)
    cw_ref[...] = jnp.where(lane < classes, rest, 0.0).astype(BF16)
    sv_ref[...] = rest.T[classes : classes + 8]
    low, high = (
        dot(one_hot_rows(devices, width, 1, shard, 3 * group + n), block) for n in range(2)
    )
    lane = lax.broadcasted_iota(jnp.int32, (devices, 128), 1)
    ub_ref[...] = jnp.where(lane < 64, turn_lanes(low), high)
    vec_ref[...] = block.astype(F32).T[:8]


def pack_small(vectors, up_bias, pool_weight, class_weight, columns):
    shard = vectors[0].shape[0]
    group = pool_weight.shape[0]
    rest = jnp.concatenate([class_weight] + [c[:, None] for c in columns], axis=1)
    up = jnp.pad(up_bias, (0, -up_bias.shape[0] % 64)).reshape(-1, 64)
    right = jnp.concatenate(
        [
            pool_weight[:, :64],
            pool_weight[:, 64:],
            jnp.pad(rest, ((0, 0), (0, 64 - rest.shape[1]))),
            up,
        ],
        axis=0,
    )
    right = jnp.pad(right, ((0, shard - right.shape[0]), (0, 0)))
    left = jnp.stack(vectors + (jnp.zeros_like(vectors[0]),) * (64 - len(vectors)), axis=1)
    return jnp.concatenate([left, right], axis=1)


def attend_kernel(lens, table, *refs, seq, width, stu, classes, devices):
    x_ref = refs[0]
    pieces = refs[1:-11]
    qkv_ref, prob_ref, mixed_ref, vec_ref, sv_ref, pw_ref, cw_ref, ub_ref, ws_ref, w_ref, sem = refs[-11:]
    step = pl.program_id(0)
    half = w_ref.shape[1] // 2
    cut = half - 128

    @pl.when(step == 0)
    def _():
        fetch_pieces(table, pieces, w_ref, sem, True, True)
        ws_ref[...] = w_ref[:, cut:half]
        read_small(
            w_ref[:, half + cut :], vec_ref, sv_ref, pw_ref, cw_ref, ub_ref, stu, classes, devices
        )

    rows = x_ref.shape[0]
    x = x_ref[...]
    vec = vec_ref[...]
    query = dot(x, w_ref[:, :width]) + vec[QB : QB + 1]
    qkv_ref[:, :width] = query.astype(BF16)
    split = 2 * width - cut
    qkv_ref[:, width:cut] = dot(x, w_ref[:, width:cut]).astype(BF16)
    qkv_ref[:, cut : 2 * width] = dot(x, w_ref[:, half : half + split]).astype(BF16)
    value = dot(x, w_ref[:, half + split : half + cut]) + vec[VB : VB + 1]
    qkv_ref[:, 2 * width :] = value.astype(BF16)
    lane = lax.broadcasted_iota(jnp.int32, (seq, 128), 1)
    first_head = lane < HEAD_DIM
    place = lax.broadcasted_iota(jnp.int32, (seq, 2 * seq), 0)
    scale = jnp.asarray(1.0 / math.sqrt(HEAD_DIM), BF16)
    for s in range(rows // seq):
        valid = place < lens[step * (rows // seq) + s]
        at = slice(s * seq, (s + 1) * seq)
        for pair in range(width // 128):
            low = pair * 128
            q = qkv_ref[at, low : low + 128] * scale
            k = qkv_ref[at, width + low : width + low + 128]
            v = qkv_ref[at, 2 * width + low : 2 * width + low + 128]
            zero = jnp.zeros_like(q)
            both = jnp.concatenate(
                [jnp.where(first_head, q, zero), jnp.where(first_head, zero, q)], axis=0
            )
            scores = jnp.where(valid, dot_nt(k, both), MASKED)
            raised = jnp.exp(scores - jnp.max(scores, axis=0, keepdims=True))
            share = raised * (1.0 / jnp.sum(raised, axis=0, keepdims=True))
            share = share.astype(BF16)
            prob_ref[s, pair] = share
            out = dot_tn(share, v)
            mixed_ref[at, low : low + 128] = jnp.where(first_head, out[:seq], out[seq:]).astype(BF16)


def attend(lens, table, rows, pieces, seq, block, stu, classes, devices):
    count, width = rows.shape
    pairs = width // 128
    samples = block // seq
    columns = 2 * pieces[0].shape[1]
    small = [
        jax.ShapeDtypeStruct((8, width), F32),
        jax.ShapeDtypeStruct((8, stu), F32),
        jax.ShapeDtypeStruct((stu, stu), BF16),
        jax.ShapeDtypeStruct((stu, 128), BF16),
        jax.ShapeDtypeStruct((devices, 128), F32),
        jax.ShapeDtypeStruct((width, stu), BF16),
    ]
    return pl.pallas_call(
        functools.partial(
            attend_kernel, seq=seq, width=width, stu=stu, classes=classes, devices=devices
        ),
        grid_spec=pltpu.PrefetchScalarGridSpec(
            num_scalar_prefetch=2,
            grid=(count // block,),
            in_specs=[rows_spec(block, width)] + [pl.BlockSpec(memory_space=pl.ANY)] * len(pieces),
            out_specs=[
                rows_spec(block, 3 * width),
                pl.BlockSpec((samples, pairs, seq, 2 * seq), lambda i, *_: (i, 0, 0, 0)),
                rows_spec(block, width),
            ]
            + [kept(s.shape) for s in small],
            scratch_shapes=[
                pltpu.VMEM((width, columns), BF16),
                pltpu.SemaphoreType.DMA((2 * len(pieces),)),
            ],
        ),
        out_shape=[
            jax.ShapeDtypeStruct((count, 3 * width), BF16),
            jax.ShapeDtypeStruct((count // seq, pairs, seq, 2 * seq), BF16),
            jax.ShapeDtypeStruct((count, width), BF16),
        ]
        + small,
        compiler_params=params(),
        cost_estimate=cost(2 * count * width * 3 * width * 2, 30e6),
        name="attend",
    )(lens, table, rows, *pieces)


def up_kernel(
    mixed_ref, x_ref, w_ref, vec_ref, ub_ref, norm_ref, factor_ref, low_ref, act_ref, slope_ref, *, chunk
):
    width = x_ref.shape[1]
    vec = vec_ref[...]
    total = dot(mixed_ref[...], w_ref[:, :width]) + vec[OB : OB + 1] + x_ref[...].astype(F32)
    normed, factor = layer_norm(total)
    norm_ref[...] = normed
    factor_ref[...] = jnp.broadcast_to(factor, factor_ref.shape)
    low_ref[...] = (normed * vec[G1 : G1 + 1] + vec[S1 : S1 + 1]).astype(BF16)
    low = low_ref[...]
    for begin in range(0, act_ref.shape[1], chunk):
        at = slice(begin, begin + chunk)
        up = dot(low, w_ref[:, width + begin : width + begin + chunk]) + ub_ref[0:1, at]
        act, slope = gelu_parts(up)
        act_ref[:, at] = act.astype(BF16)
        slope_ref[:, at] = slope.astype(BF16)


def up_part(mixed, rows, large, vec, ub, block):
    count, width = rows.shape
    ff = large.shape[1] - width
    return pl.pallas_call(
        functools.partial(up_kernel, chunk=256),
        grid_spec=pltpu.PrefetchScalarGridSpec(
            num_scalar_prefetch=0,
            grid=(count // block,),
            in_specs=[
                rows_spec(block, width),
                rows_spec(block, width),
                pl.BlockSpec(large.shape, lambda i: (0, 0), pipeline_mode=pl.Buffered(1)),
                whole(vec.shape),
                whole(ub.shape),
            ],
            out_specs=[
                rows_spec(block, width),
                rows_spec(block, 128),
                rows_spec(block, width),
                rows_spec(block, ff),
                rows_spec(block, ff),
            ],
        ),
        out_shape=[
            jax.ShapeDtypeStruct((count, width), F32),
            jax.ShapeDtypeStruct((count, 128), F32),
            jax.ShapeDtypeStruct((count, width), BF16),
            jax.ShapeDtypeStruct((count, ff), BF16),
            jax.ShapeDtypeStruct((count, ff), BF16),
        ],
        compiler_params=params(),
        cost_estimate=cost(2 * count * width * (ff + width) * 2, 50e6),
        name="up_part",
    )(mixed, rows, large, vec, ub)


def down_kernel(lens, alive, table, *refs, seq):
    act_ref, norm_ref, cot_ref, lg_ref, vec_ref, ws_ref, sv_ref, pw_ref, cw_ref = refs[:9]
    pieces = refs[9:-11]
    second_ref, sum_ref, dcot_ref, logits_ref, vgrad_ref, sgrad_ref = refs[-11:-5]
    wsgrad_ref, pwgrad_ref, cwgrad_ref, wd_ref, sem = refs[-5:]
    step = pl.program_id(0)
    rows = act_ref.shape[0]
    samples = rows // seq
    vec = vec_ref[...]
    sv = sv_ref[...]
    stu = sv.shape[1]
    pool_width = stu // STU_HEADS
    pool_scale = 1.0 / math.sqrt(pool_width)

    @pl.when(step == 0)
    def _():
        fetch_pieces(table, pieces, wd_ref, sem, True, True)
        vgrad_ref[...] = jnp.zeros_like(vgrad_ref)
        sgrad_ref[...] = jnp.zeros_like(sgrad_ref)
        wsgrad_ref[...] = jnp.zeros_like(wsgrad_ref)
        pwgrad_ref[...] = jnp.zeros_like(pwgrad_ref)
        cwgrad_ref[...] = jnp.zeros_like(cwgrad_ref)

    first = norm_ref[...] * vec[G1 : G1 + 1] + vec[S1 : S1 + 1]
    down = dot(act_ref[...], wd_ref[...]) + vec[DB : DB + 1]
    normed, factor = layer_norm(first + down)
    second = (normed * vec[G2 : G2 + 1] + vec[S2 : S2 + 1]).astype(BF16)
    reduced = (dot(second, ws_ref[...]) + sv[0:1]).astype(BF16)
    head_of = lax.broadcasted_iota(jnp.int32, (stu, stu), 0) // pool_width
    same = head_of == lax.broadcasted_iota(jnp.int32, (stu, stu), 1) // pool_width
    pool_query = sv[1:2]
    query_table = jnp.where(same, jnp.broadcast_to(pool_query, (stu, stu)), 0.0).astype(BF16)
    scores = dot_nt(reduced, query_table) * pool_scale
    place = lax.broadcasted_iota(jnp.int32, (seq, stu), 0)
    shares = []
    pooled_rows = []
    for s in range(samples):
        at = slice(s * seq, (s + 1) * seq)
        part = jnp.where(place < lens[step * samples + s], scores[at], MASKED)
        raised = jnp.exp(part - jnp.max(part, axis=0, keepdims=True))
        share = raised / jnp.sum(raised, axis=0, keepdims=True)
        shares.append(share)
        pooled_rows.append(column_sum(share * reduced[at].astype(F32)))
    pooled = stack_rows(pooled_rows, 8).astype(BF16)
    squashed = jnp.tanh(dot(pooled, pw_ref[...]) + sv[2:3])
    squashed_low = squashed.astype(BF16)
    logits_ref[...] = dot(squashed_low, cw_ref[...])
    lg = lg_ref[...]
    cwgrad_ref[...] += dot_tn(squashed_low, lg)
    hidden_cot = (dot_nt(lg, cw_ref[...]) * (1.0 - squashed * squashed)).astype(BF16)
    pwgrad_ref[...] += dot_tn(pooled, hidden_cot)
    pooled_cot = dot_nt(hidden_cot, pw_ref[...]).astype(BF16).astype(F32)
    query_grad = jnp.zeros((1, stu), F32)
    cots = []
    for s in range(samples):
        at = slice(s * seq, (s + 1) * seq)
        row = pooled_cot[s : s + 1]
        table = jnp.where(same, jnp.broadcast_to(row, (stu, stu)), 0.0).astype(BF16)
        share_cot = dot_nt(reduced[at], table)
        share = shares[s]
        score_cot = share * (share_cot - column_sum(share * share_cot))
        query_grad += column_sum(score_cot * reduced[at].astype(F32)) * pool_scale
        cots.append((share * row + score_cot * (pool_query * pool_scale)).astype(BF16))
    reduced_cot = jnp.concatenate(cots, axis=0)
    sgrad_ref[...] += stack_rows(
        [
            column_sum(reduced_cot.astype(F32)),
            query_grad,
            column_sum(hidden_cot.astype(F32)),
        ],
        8,
    )
    wsgrad_ref[...] += dot_tn(reduced_cot, second)
    back = dot_nt(reduced_cot, ws_ref[...])
    parts = []
    for s in range(samples):
        at = slice(s * seq, (s + 1) * seq)
        live = alive[step * samples + s] > 0
        parts.append(back[at] + jnp.where(live, cot_ref[at].astype(F32), 0.0))
        second_ref[at] = jnp.where(live, second[at], jnp.zeros_like(second[at]))
    total = jnp.concatenate(parts, axis=0)
    sum_cot = layer_norm_back(total, vec[G2 : G2 + 1], normed, factor)
    sum_ref[...] = sum_cot
    down_cot = sum_cot.astype(BF16)
    dcot_ref[...] = down_cot
    vgrad_ref[...] += stack_rows(
        [column_sum(total * normed), column_sum(total), column_sum(down_cot.astype(F32))], 8
    )


def down_part(lens, alive, table, act, normed, cot, lg, pieces, vec, ws, sv, pw, cw, seq, block):
    count, ff = act.shape
    width = normed.shape[1]
    stu = ws.shape[1]
    steps = count // block
    return pl.pallas_call(
        functools.partial(down_kernel, seq=seq),
        grid_spec=pltpu.PrefetchScalarGridSpec(
            num_scalar_prefetch=3,
            grid=(steps,),
            in_specs=[
                rows_spec(block, ff),
                rows_spec(block, width),
                rows_spec(block, width),
                rows_spec(8, 128),
                whole(vec.shape),
                whole(ws.shape),
                whole(sv.shape),
                whole(pw.shape),
                whole(cw.shape),
            ]
            + [pl.BlockSpec(memory_space=pl.ANY)] * len(pieces),
            out_specs=[
                rows_spec(block, width),
                rows_spec(block, width),
                rows_spec(block, width),
                rows_spec(8, 128),
                kept((8, width)),
                kept((8, stu)),
                kept((stu, width)),
                kept((stu, stu)),
                kept((stu, 128)),
            ],
            scratch_shapes=[
                pltpu.VMEM((ff, width), BF16),
                pltpu.SemaphoreType.DMA((2 * len(pieces),)),
            ],
        ),
        out_shape=[
            jax.ShapeDtypeStruct((count, width), BF16),
            jax.ShapeDtypeStruct((count, width), F32),
            jax.ShapeDtypeStruct((count, width), BF16),
            jax.ShapeDtypeStruct((steps * 8, 128), F32),
            jax.ShapeDtypeStruct((8, width), F32),
            jax.ShapeDtypeStruct((8, stu), F32),
            jax.ShapeDtypeStruct((stu, width), F32),
            jax.ShapeDtypeStruct((stu, stu), F32),
            jax.ShapeDtypeStruct((stu, 128), F32),
        ],
        compiler_params=params(),
        cost_estimate=cost(2 * count * width * ff * 2, 40e6),
        name="down_part",
    )(lens, alive, table, act, normed, cot, lg, vec, ws, sv, pw, cw, *pieces)


def up_back_kernel(table, *refs, chunk):
    dcot_ref, slope_ref, sum_ref, norm_ref, factor_ref, w_ref, vec_ref = refs[:7]
    pieces = refs[7:-8]
    ucot_ref, one_ref, acot_ref, mcot_ref, vgrad_ref, ugrad_ref, wd_ref, sem = refs[-8:]
    step = pl.program_id(0)
    width = dcot_ref.shape[1]
    vec = vec_ref[...]

    @pl.when(step == 0)
    def _():
        fetch_pieces(table, pieces, wd_ref, sem, True, True)
        vgrad_ref[...] = jnp.zeros_like(vgrad_ref)
        ugrad_ref[...] = jnp.zeros_like(ugrad_ref)

    down_cot = dcot_ref[...]
    for begin in range(0, slope_ref.shape[1], chunk):
        at = slice(begin, begin + chunk)
        up_cot = dot_nt(down_cot, wd_ref[at, :]) * slope_ref[:, at].astype(F32)
        up_cot = up_cot.astype(BF16)
        ucot_ref[:, at] = up_cot
        ugrad_ref[0:1, at] += column_sum(up_cot.astype(F32))
    cot = sum_ref[...] + dot_nt(ucot_ref[...], w_ref[:, width:])
    normed = norm_ref[...]
    one_cot = layer_norm_back(cot, vec[G1 : G1 + 1], normed, factor_ref[:, 0:1])
    one_ref[...] = one_cot
    low = one_cot.astype(BF16)
    acot_ref[...] = low
    mcot_ref[...] = dot_nt(low, w_ref[:, :width]).astype(BF16)
    vgrad_ref[...] += stack_rows(
        [column_sum(cot * normed), column_sum(cot), column_sum(low.astype(F32))], 8
    )


def up_back(table, dcot, slope, sum_two, normed, factor, pieces, large, vec, block):
    count, width = dcot.shape
    ff = slope.shape[1]
    return pl.pallas_call(
        functools.partial(up_back_kernel, chunk=512),
        grid_spec=pltpu.PrefetchScalarGridSpec(
            num_scalar_prefetch=1,
            grid=(count // block,),
            in_specs=[
                rows_spec(block, width),
                rows_spec(block, ff),
                rows_spec(block, width),
                rows_spec(block, width),
                rows_spec(block, 128),
                whole(large.shape),
                whole(vec.shape),
            ]
            + [pl.BlockSpec(memory_space=pl.ANY)] * len(pieces),
            out_specs=[
                rows_spec(block, ff),
                rows_spec(block, width),
                rows_spec(block, width),
                rows_spec(block, width),
                kept((8, width)),
                kept((8, ff)),
            ],
            scratch_shapes=[
                pltpu.VMEM((ff, width), BF16),
                pltpu.SemaphoreType.DMA((2 * len(pieces),)),
            ],
        ),
        out_shape=[
            jax.ShapeDtypeStruct((count, ff), BF16),
            jax.ShapeDtypeStruct((count, width), F32),
            jax.ShapeDtypeStruct((count, width), BF16),
            jax.ShapeDtypeStruct((count, width), BF16),
            jax.ShapeDtypeStruct((8, width), F32),
            jax.ShapeDtypeStruct((8, ff), F32),
        ],
        compiler_params=params(),
        cost_estimate=cost(2 * count * width * ff * 2.5, 60e6),
        name="up_back",
    )(table, dcot, slope, sum_two, normed, factor, large, vec, *pieces)


def attend_back_kernel(mcot_ref, qkv_ref, prob_ref, pcot_ref, vgrad_ref, *, seq, width):
    step = pl.program_id(0)
    rows = mcot_ref.shape[0]

    @pl.when(step == 0)
    def _():
        vgrad_ref[...] = jnp.zeros_like(vgrad_ref)

    lane = lax.broadcasted_iota(jnp.int32, (seq, 128), 1)
    first_head = lane < HEAD_DIM
    scale = 1.0 / math.sqrt(HEAD_DIM)

    def split(part):
        zero = jnp.zeros_like(part)
        return jnp.concatenate(
            [jnp.where(first_head, part, zero), jnp.where(first_head, zero, part)], axis=0
        )

    for s in range(rows // seq):
        at = slice(s * seq, (s + 1) * seq)
        for pair in range(width // 128):
            low = pair * 128
            q = split(qkv_ref[at, low : low + 128])
            k = qkv_ref[at, width + low : width + low + 128]
            v = qkv_ref[at, 2 * width + low : 2 * width + low + 128]
            cot = split(mcot_ref[at, low : low + 128])
            share = prob_ref[s, pair]
            share_cot = dot_nt(v, cot)
            pcot_ref[at, 2 * width + low : 2 * width + low + 128] = dot(share, cot).astype(BF16)
            wide = share.astype(F32)
            product = wide * share_cot
            score_cot = (product - wide * column_sum(product)).astype(BF16)
            pcot_ref[at, width + low : width + low + 128] = (dot(score_cot, q) * scale).astype(BF16)
            query_cot = dot_tn(score_cot, k) * scale
            pcot_ref[at, low : low + 128] = jnp.where(
                first_head, query_cot[:seq], query_cot[seq:]
            ).astype(BF16)
    vgrad_ref[...] += stack_rows(
        [
            column_sum(pcot_ref[:, :width].astype(F32)),
            column_sum(pcot_ref[:, 2 * width :].astype(F32)),
        ],
        8,
    )


def attend_back(mcot, qkv, prob, seq, block):
    count, width = mcot.shape
    pairs = width // 128
    return pl.pallas_call(
        functools.partial(attend_back_kernel, seq=seq, width=width),
        grid_spec=pltpu.PrefetchScalarGridSpec(
            num_scalar_prefetch=0,
            grid=(count // block,),
            in_specs=[
                rows_spec(block, width),
                rows_spec(block, 3 * width),
                pl.BlockSpec((block // seq, pairs, seq, 2 * seq), lambda i, *_: (i, 0, 0, 0)),
            ],
            out_specs=[rows_spec(block, 3 * width), kept((8, width))],
        ),
        out_shape=[
            jax.ShapeDtypeStruct((count, 3 * width), BF16),
            jax.ShapeDtypeStruct((8, width), F32),
        ],
        compiler_params=params(),
        cost_estimate=cost(2 * count * width * 3 * width * 2, 30e6),
        name="attend_back",
    )(mcot, qkv, prob)


def token_kernel(table, *refs):
    pcot_ref, one_ref = refs[:2]
    pieces = refs[2:-3]
    out_ref, w_ref, sem = refs[-3:]

    @pl.when(pl.program_id(0) == 0)
    def _():
        fetch_pieces(table, pieces, w_ref, sem, True, True)

    half = w_ref.shape[1] // 2
    cut = half - 128
    out_ref[...] = (
        one_ref[...]
        + dot_nt(pcot_ref[:, :cut], w_ref[:, :cut])
        + dot_nt(pcot_ref[:, cut:], w_ref[:, half : half + cut])
    )


def token_part(table, pcot, one_cot, pieces, block):
    count, width = one_cot.shape
    return pl.pallas_call(
        token_kernel,
        grid_spec=pltpu.PrefetchScalarGridSpec(
            num_scalar_prefetch=1,
            grid=(count // block,),
            in_specs=[rows_spec(block, 3 * width), rows_spec(block, width)]
            + [pl.BlockSpec(memory_space=pl.ANY)] * len(pieces),
            out_specs=rows_spec(block, width),
            scratch_shapes=[
                pltpu.VMEM((width, 2 * pieces[0].shape[1]), BF16),
                pltpu.SemaphoreType.DMA((2 * len(pieces),)),
            ],
        ),
        out_shape=jax.ShapeDtypeStruct((count, width), F32),
        compiler_params=params(),
        cost_estimate=cost(2 * count * width * 3 * width, 25e6),
        name="token_part",
    )(table, pcot, one_cot, *pieces)


def weight_kernel(left_ref, right_ref, out_ref, turned):
    @pl.when(pl.program_id(0) == 0)
    def _():
        turned[...] = left_ref[...].T

    out_ref[...] = dot(turned[...], right_ref[...]).astype(out_ref.dtype)


def weight_part(left, right, tile, name):
    count, height = left.shape
    width = right.shape[1]
    return pl.pallas_call(
        weight_kernel,
        grid_spec=pltpu.PrefetchScalarGridSpec(
            num_scalar_prefetch=0,
            grid=(width // tile,),
            in_specs=[
                whole((count, height)),
                pl.BlockSpec((count, tile), lambda i, *_: (0, i)),
            ],
            out_specs=pl.BlockSpec((height, tile), lambda i, *_: (0, i)),
            scratch_shapes=[pltpu.VMEM((height, count), BF16)],
        ),
        out_shape=jax.ShapeDtypeStruct((height, width), BF16),
        compiler_params=params(),
        cost_estimate=cost(2 * count * width * height, 2 * (count + height) * width),
        name=name,
    )(left, right)


def weight_pieces_kernel(table, left_ref, right_ref, *refs, steps):
    other_ref, planes, flat, turned = refs[0], refs[1:-2], refs[-2], refs[-1]
    step = pl.program_id(0)
    lines = table.shape[0] - 1
    rows = turned.shape[0] // lines

    @pl.when(step == 0)
    def _():
        flat[...] = left_ref[...].T
        for n in range(lines):
            at = pl.ds(pl.multiple_of(table[n], 16), rows)
            turned[n * rows : (n + 1) * rows] = flat[at]

    out = dot(turned[...], right_ref[...]).astype(BF16)

    @pl.when(step < steps)
    def _():
        other_ref[...] = out

    @pl.when(step >= steps)
    def _():
        for n, plane in enumerate(planes):
            height = plane.shape[0]
            plane[...] = out[n * height : (n + 1) * height]


def weight_pieces(table, left, right, tile, planes, name):
    count, height = left.shape
    half = right.shape[1] // 2
    steps = half // tile
    core_at = table.shape[0] - 1

    def columns(i, t):
        core = t[core_at]
        return (0, jnp.where(i < steps, (1 - core) * steps + i, core * steps + i - steps))

    last = steps - 1
    return pl.pallas_call(
        functools.partial(weight_pieces_kernel, steps=steps),
        grid_spec=pltpu.PrefetchScalarGridSpec(
            num_scalar_prefetch=1,
            grid=(2 * steps,),
            in_specs=[whole((count, height)), pl.BlockSpec((count, tile), columns)],
            out_specs=[pl.BlockSpec((height, tile), lambda i, t: (0, jnp.minimum(i, last)))]
            + [
                pl.BlockSpec((height // planes, tile), lambda i, t: (0, jnp.maximum(i - steps, 0)))
            ]
            * planes,
            scratch_shapes=[pltpu.VMEM((height, count), BF16)] * 2,
        ),
        out_shape=[jax.ShapeDtypeStruct((height, half), BF16)]
        + [jax.ShapeDtypeStruct((height // planes, half), BF16)] * planes,
        compiler_params=params(),
        cost_estimate=cost(2 * count * 2 * half * height, 4 * (count + height) * half),
        name=name,
    )(table, left, right)


def small_kernel(table, *refs, classes, devices):
    vin_ref, vone_ref, vtwo_ref, ugrad_ref, sgrad_ref, wsgrad_ref, pwgrad_ref, cwgrad_ref = refs[:8]
    other_ref, planes, halves = refs[8], refs[9:-1], refs[-1]
    width = vin_ref.shape[1]
    stu = sgrad_ref.shape[1]
    shard = width // devices
    group = stu // devices
    halves[0] = wsgrad_ref[...].T
    vin, vone, vtwo = vin_ref[...], vone_ref[...], vtwo_ref[...]
    rows = [vin[0:1], vin[1:2], vone[2:3], vone[0:1], vone[1:2], vtwo[2:3], vtwo[0:1], vtwo[1:2]]
    block = stack_rows(rows, 128).T
    lane = lax.broadcasted_iota(jnp.int32, (stu, 128), 1)
    high = lane >= 64
    pwgrad = pwgrad_ref[...]
    spare = jnp.zeros((classes, stu), F32)
    rest = jnp.concatenate(
        [spare, sgrad_ref[0:3], jnp.zeros((128 - classes - 3, stu), F32)], axis=0
    ).T
    rest = rest + jnp.where(lane < classes, cwgrad_ref[...], 0.0)
    for n, part in enumerate((turn_lanes(pwgrad), pwgrad, turn_lanes(rest))):
        part = jnp.where(high, part, 0.0).astype(BF16)
        block = block + dot_tn(one_hot_rows(stu, width, group, shard, n * group), part)
    ugrad = ugrad_ref[...]
    high = lax.broadcasted_iota(jnp.int32, ugrad.shape, 1) >= 64
    for n, part in enumerate((turn_lanes(ugrad), ugrad)):
        part = jnp.where(high, part, 0.0).astype(BF16)
        block = block + dot_tn(one_hot_rows(devices, width, 1, shard, 3 * group + n), part)
    halves[1] = block
    lines = table.shape[0] - 1
    core = table[lines]
    rows = width // lines
    per = lines // len(planes)
    for n in range(lines):
        at = pl.ds(pl.multiple_of(table[n], 16), rows)
        other_ref[n * rows : (n + 1) * rows] = halves[1 - core, at].astype(BF16)
        begin = (n % per) * rows
        planes[n // per][begin : begin + rows] = halves[core, at].astype(BF16)


def small_pieces(table, grads, planes, classes, devices):
    width = grads[0].shape[1]
    return pl.pallas_call(
        functools.partial(small_kernel, classes=classes, devices=devices),
        grid_spec=pltpu.PrefetchScalarGridSpec(
            num_scalar_prefetch=1,
            grid=(1,),
            in_specs=[whole(g.shape) for g in grads],
            out_specs=[kept((width, 128))] + [kept((width // planes, 128))] * planes,
            scratch_shapes=[pltpu.VMEM((2, width, 128), F32)],
        ),
        out_shape=[jax.ShapeDtypeStruct((width, 128), BF16)]
        + [jax.ShapeDtypeStruct((width // planes, 128), BF16)] * planes,
        compiler_params=params(),
        cost_estimate=cost(1e8, 2e6),
        name="small_pieces",
    )(table, *grads)


def finish_kernel(block_ref, *outs, group, classes, up_size):
    block = block_ref[...]
    shard = block.shape[0]
    columns = jnp.concatenate([block, jnp.zeros((128 - shard, 128), F32)], axis=0).T
    for n in range(8):
        outs[n][...] = columns[n : n + 1, :shard]
    outs[8][...] = block[:group, 64:]
    outs[9][...] = block[group : 2 * group, 64:]
    outs[10][...] = block[2 * group : 3 * group, 64 : 64 + classes]
    for n in range(3):
        row = columns[64 + classes + n : 64 + classes + n + 1]
        outs[11 + n][...] = row[:, 2 * group : 3 * group]
    first = min(64, up_size)
    outs[14][:, :first] = block[3 * group : 3 * group + 1, 64 : 64 + first]
    if up_size > first:
        outs[14][:, first:] = block[3 * group + 1 : 3 * group + 2, 64 : 64 + up_size - first]


def pick_kernel(table, source_ref, *refs, count):
    outs, held, sem_in, sem_out = refs[:-3], refs[-3], refs[-2], refs[-1]
    reads, writes = [], []
    for o, out in enumerate(outs):
        for j in range(count):
            n = o * count + j
            reads.append(pltpu.make_async_copy(source_ref.at[table[o, j]], held.at[n], sem_in.at[n]))
            writes.append(pltpu.make_async_copy(held.at[n], out.at[j], sem_out.at[n]))
    for copy in reads:
        copy.start()
    for read, write in zip(reads, writes):
        read.wait()
        write.start()
    for copy in writes:
        copy.wait()


def pick(table, source, outs, count):
    total = outs * count
    return pl.pallas_call(
        functools.partial(pick_kernel, count=count),
        grid_spec=pltpu.PrefetchScalarGridSpec(
            num_scalar_prefetch=1,
            grid=(1,),
            in_specs=[pl.BlockSpec(memory_space=pl.ANY)],
            out_specs=[pl.BlockSpec(memory_space=pl.ANY)] * outs,
            scratch_shapes=[
                pltpu.VMEM((total,) + source.shape[1:], source.dtype),
                pltpu.SemaphoreType.DMA((total,)),
                pltpu.SemaphoreType.DMA((total,)),
            ],
        ),
        out_shape=[jax.ShapeDtypeStruct((count,) + source.shape[1:], source.dtype)] * outs,
        compiler_params=params(),
        cost_estimate=cost(0, 2 * total * source[0].size * 2),
        name="pick",
    )(table, source)


def place_kernel(origin, position, *refs, samples):
    sources, out_ref, held, sem_in, sem_out = refs[:-4], refs[-4], refs[-3], refs[-2], refs[-1]
    for j in range(samples):
        for o, source in enumerate(sources):

            @pl.when(origin[j] == o)
            def _():
                pltpu.make_async_copy(source.at[position[j]], held.at[j], sem_in.at[j]).start()

    writes = []
    for j in range(samples):
        pltpu.make_async_copy(sources[0].at[0], held.at[j], sem_in.at[j]).wait()
        writes.append(pltpu.make_async_copy(held.at[j], out_ref.at[j], sem_out.at[j]))
        writes[-1].start()
    for copy in writes:
        copy.wait()


def place(origin, position, sources):
    samples = origin.shape[0]
    shape = sources[0].shape[1:]
    return pl.pallas_call(
        functools.partial(place_kernel, samples=samples),
        grid_spec=pltpu.PrefetchScalarGridSpec(
            num_scalar_prefetch=2,
            grid=(1,),
            in_specs=[pl.BlockSpec(memory_space=pl.ANY)] * len(sources),
            out_specs=pl.BlockSpec(memory_space=pl.ANY),
            scratch_shapes=[
                pltpu.VMEM((samples,) + shape, sources[0].dtype),
                pltpu.SemaphoreType.DMA((samples,)),
                pltpu.SemaphoreType.DMA((samples,)),
            ],
        ),
        out_shape=jax.ShapeDtypeStruct((samples,) + shape, sources[0].dtype),
        compiler_params=params(),
        cost_estimate=cost(0, 4 * samples * shape[0] * shape[1]),
        name="place",
    )(origin, position, *sources)


def routes(destination, samples, fsdp):
    group = lax.axis_index("dp")
    me = lax.axis_index("fsdp")
    capacity = 3 * samples // (2 * fsdp)
    span = fsdp * samples
    slots = lax.dynamic_slice_in_dim(destination, group * span, span).reshape(fsdp, samples)
    target = slots // samples - group * fsdp
    slot = slots % samples
    order = jnp.arange(samples, dtype=jnp.int32)
    before = order[None, :] < order[:, None]
    rank = jnp.sum(
        jnp.where((target[:, :, None] == target[:, None, :]) & before[None], 1, 0), axis=2
    ).astype(jnp.int32)
    offsets = (me + jnp.arange(1, fsdp, dtype=jnp.int32)) % fsdp
    places = jnp.arange(capacity, dtype=jnp.int32)

    def mine(table):
        return lax.dynamic_index_in_dim(table, me, 0, keepdims=False)

    my_target, my_slot, my_rank = mine(target), mine(slot), mine(rank)
    hit = (my_target[None, None, :] == offsets[:, None, None]) & (
        my_rank[None, None, :] == places[None, :, None]
    )
    out_pick = jnp.sum(jnp.where(hit, order[None, None, :], 0), axis=2).astype(jnp.int32)
    lands = (target == me)[:, :, None] & (slot[:, :, None] == order[None, None, :])
    origin_table = ((me - jnp.arange(fsdp, dtype=jnp.int32)) % fsdp)[:, None, None]
    in_origin = jnp.sum(jnp.where(lands, origin_table, 0), axis=(0, 1)).astype(jnp.int32)
    entry = jnp.where(origin_table == 0, order[None, :, None], rank[:, :, None])
    in_place = jnp.sum(jnp.where(lands, entry, 0), axis=(0, 1)).astype(jnp.int32)
    their_target = jnp.take(target, offsets, axis=0)
    their_slot = jnp.take(slot, offsets, axis=0)
    their_rank = jnp.take(rank, offsets, axis=0)
    hit = (their_target[:, None, :] == me) & (their_rank[:, None, :] == places[None, :, None])
    back_pick = jnp.sum(jnp.where(hit, their_slot[:, None, :], 0), axis=2).astype(jnp.int32)
    back_origin = ((me - my_target) % fsdp).astype(jnp.int32)
    back_place = jnp.where(back_origin == 0, my_slot, my_rank).astype(jnp.int32)
    return capacity, out_pick, in_origin, in_place, back_pick, back_origin, back_place


class Grid:
    def __init__(self, dp, fsdp):
        self.size = {"c": 2, "x": fsdp // 2}
        self.size["z"] = 4 if dp % 4 == 0 else dp
        self.size["y"] = dp // self.size["z"]
        d, f = lax.axis_index("dp"), lax.axis_index("fsdp")
        self.at = {"z": d // self.size["y"], "y": d % self.size["y"], "x": f // 2, "c": f % 2}

    def number(self, at):
        dp = at["z"] * self.size["y"] + at["y"]
        return (dp * self.size["x"] + at["x"]) * 2 + at["c"]

    def send(self, array, axis, offset):
        pairs = []
        spans = [range(self.size[a]) for a in "zyxc"]
        for place in itertools.product(*spans):
            here = dict(zip("zyxc", place))
            there = dict(here)
            there[axis] = (here[axis] + offset) % self.size[axis]
            pairs.append((self.number(here), self.number(there)))
        return lax.ppermute(array, AXES, pairs)

    def spread(self, array, axis):
        return [array] + [self.send(array, axis, o) for o in range(1, self.size[axis])]

    def ordered(self, parts, axis):
        n, at = self.size[axis], self.at[axis]
        out = []
        for j in range(n):
            pick = parts[0]
            for o in range(1, n):
                pick = jnp.where((at - o) % n == j, parts[o], pick)
            out.append(pick)
        return jnp.concatenate(out, axis=0)


def gather_pieces(grid, shard):
    half = shard.shape[1] // 2
    c = grid.at["c"]
    mine = lax.dynamic_slice_in_dim(shard, c * half, half, 1)
    other = lax.dynamic_slice_in_dim(shard, (1 - c) * half, half, 1)
    chip = grid.ordered([mine, grid.send(other, "c", 1)], "c")
    line = grid.ordered(grid.spread(chip, "x"), "x")
    columns = grid.spread(line, "z")
    planes = [[] for _ in range(grid.size["y"])]
    for part in columns:
        for o, got in enumerate(grid.spread(part, "y")):
            planes[o].append(got)
    own = [part for plane in planes for part in plane]
    far = [grid.send(jnp.concatenate(plane, axis=0), "c", 1) for plane in planes]
    return own, far


def piece_table(grid, rows, sign):
    oy, oz = jnp.meshgrid(jnp.arange(grid.size["y"]), jnp.arange(grid.size["z"]), indexing="ij")
    z = (grid.at["z"] + sign * oz.reshape(-1)) % grid.size["z"]
    y = (grid.at["y"] + sign * oy.reshape(-1)) % grid.size["y"]
    lines = (z * grid.size["y"] + y) * rows
    return jnp.concatenate([lines, jnp.reshape(grid.at["c"], (1,))]).astype(jnp.int32)


def fetch_pieces(table, pieces, w_ref, sem, begin, finish):
    own_count = sum(1 for p in pieces if p.shape[0] == pieces[0].shape[0])
    own, far = pieces[:own_count], pieces[own_count:]
    rows, half = own[0].shape
    per = own_count // len(far)
    core = table[own_count]
    copies = []
    for n in range(own_count):
        at = pl.ds(pl.multiple_of(table[n], 16), rows)
        near = pl.ds(pl.multiple_of(core * half, 128), half)
        away = pl.ds(pl.multiple_of((1 - core) * half, 128), half)
        copies.append(pltpu.make_async_copy(own[n], w_ref.at[at, near], sem.at[2 * n]))
        source = far[n // per].at[pl.ds((n % per) * rows, rows)]
        copies.append(pltpu.make_async_copy(source, w_ref.at[at, away], sem.at[2 * n + 1]))
    for copy in copies:
        if begin:
            copy.start()
    for copy in copies:
        if finish:
            copy.wait()


def add(*parts):
    total = parts[0].astype(F32)
    for part in parts[1:]:
        total = total + part.astype(F32)
    return total


def scatter_pieces(grid, other, planes):
    rows, half = planes[0].shape
    nz, nx = grid.size["z"], grid.size["x"]
    got = grid.send(other, "c", 1)
    came = []
    for o in range(1, grid.size["y"]):
        part = add(planes[o], got[o * rows : (o + 1) * rows]).astype(BF16)
        came.append(grid.send(part, "y", o))
    line = rows // nz
    terms = [planes[0], got[:rows]] + came
    cut = [add(*(t[o * line : (o + 1) * line] for t in terms)) for o in range(nz)]
    came = [grid.send(cut[o].astype(BF16), "z", o) for o in range(1, nz)]
    chip = line // nx
    line_sum = add(cut[0], *came)
    at = [(grid.at["x"] + o) % nx * chip for o in range(nx)]
    cut = [lax.dynamic_slice_in_dim(line_sum, a, chip, 0) for a in at]
    total = add(cut[0], *(grid.send(cut[o].astype(BF16), "x", o) for o in range(1, nx)))
    c = grid.at["c"]
    share = chip // 2
    mine = lax.dynamic_slice_in_dim(total, c * share, share, 0)
    far = lax.dynamic_slice_in_dim(total, (1 - c) * share, share, 0).astype(BF16)
    far = grid.send(far, "c", 1).astype(F32)
    return jnp.concatenate([jnp.where(c == 0, mine, far), jnp.where(c == 0, far, mine)], axis=1)


def exchange(parts, fsdp):
    out = []
    for o, part in enumerate(parts):
        pairs = [(m, (m + o + 1) % fsdp) for m in range(fsdp)]
        out.append(lax.ppermute(part, "fsdp", pairs))
    return out


def body(
    tokens,
    input_weight,
    query_bias,
    value_bias,
    output_weight,
    output_bias,
    first_gain,
    first_shift,
    up_weight,
    up_bias,
    down_weight,
    down_bias,
    second_gain,
    second_shift,
    student_weight,
    student_bias,
    pool_query,
    pool_weight,
    pool_bias,
    class_weight,
    class_bias,
    lengths,
    exit_layer,
    destination,
    repacked_grad,
    logits_grad,
):
    samples, seq, width = tokens.shape
    count = samples * seq
    devices = lax.axis_size("dp") * lax.axis_size("fsdp")
    fsdp = lax.axis_size("fsdp")
    ff = up_weight.shape[1]
    stu = student_weight.shape[1]
    classes = class_weight.shape[1]
    block = min(count, 256)
    wide_block = min(count, 512)
    shard = width // devices
    grid = Grid(lax.axis_size("dp"), fsdp)
    line = grid.size["x"] * 2 * shard
    table_in = piece_table(grid, line, -1)
    table_down = piece_table(grid, line * ff // width, -1)
    table_out = piece_table(grid, line, 1)
    planes = grid.size["y"]
    vectors = (
        query_bias,
        value_bias,
        output_bias,
        first_gain,
        first_shift,
        down_bias,
        second_gain,
        second_shift,
    )
    small = pack_small(vectors, up_bias, pool_weight, class_weight, (student_bias, pool_query, pool_bias))
    cut = 3 * width // 2
    own, far = gather_pieces(
        grid,
        jnp.concatenate([input_weight[:, :cut], student_weight, input_weight[:, cut:], small], axis=1),
    )
    pieces = own + far
    large = lax.all_gather(
        jnp.concatenate([output_weight, up_weight], axis=1), AXES, axis=0, tiled=True
    )
    own, far = gather_pieces(grid, down_weight)
    down_pieces = own + far

    capacity, out_pick, in_origin, in_place, back_pick, back_origin, back_place = routes(
        destination, samples, fsdp
    )
    alive = (exit_layer > LAYER).astype(jnp.int32)
    outgoing = pick(back_pick, repacked_grad, fsdp - 1, capacity)
    returned = exchange(outgoing, fsdp)
    second_cot = place(back_origin, back_place, [repacked_grad] + returned)

    rows = tokens.reshape(count, width)
    qkv, prob, mixed, vec, sv, pw, cw, ubm, ws = attend(
        lengths, table_in, rows, pieces, seq, block, stu, classes, devices
    )
    ub = jnp.broadcast_to(ubm[:, : ff // devices].reshape(1, ff), (8, ff))
    normed, factor, low, act, slope = up_part(mixed, rows, large, vec, ub, block)
    steps = count // wide_block
    lg = jnp.pad(
        logits_grad.reshape(steps, samples // steps, classes),
        ((0, 0), (0, 8 - samples // steps), (0, 128 - classes)),
    ).reshape(steps * 8, 128)
    second, sum_two, dcot, logits, vgrad_two, sgrad, wsgrad, pwgrad, cwgrad = down_part(
        lengths,
        alive,
        table_down,
        act,
        normed,
        second_cot.reshape(count, width),
        lg,
        down_pieces,
        vec,
        ws,
        sv,
        pw,
        cw,
        seq,
        wide_block,
    )
    student_logits = logits.reshape(steps, 8, 128)[:, : samples // steps, :classes].reshape(
        samples, classes
    ) + class_bias.astype(F32)
    second = second.reshape(samples, seq, width)
    leaving = pick(out_pick, second, fsdp - 1, capacity)
    arrived = exchange(leaving, fsdp)

    wd_grad = weight_part(act, dcot, 256, "down_grad")
    wd_share = lax.psum_scatter(wd_grad, AXES, scatter_dimension=0, tiled=True)
    ucot, one_cot, acot, mcot, vgrad_one, ugrad = up_back(
        table_down, dcot, slope, sum_two, normed, factor, down_pieces, large, vec, wide_block
    )
    wo_grad = weight_pieces(table_out, mixed, acot, 128, planes, "output_grad")
    wu_grad = weight_pieces(table_out, low, ucot, 512, planes, "up_grad")
    ff_grad = [jnp.concatenate(pair, axis=1) for pair in zip(wu_grad, wo_grad)]
    ff_share = scatter_pieces(grid, ff_grad[0], ff_grad[1:])
    pcot, vgrad_in = attend_back(mcot, qkv, prob, seq, block)
    ugm = jnp.pad(ugrad[0].reshape(devices, -1), ((0, 0), (0, 128 - ff // devices)))
    small_grad = small_pieces(
        table_out,
        (vgrad_in, vgrad_one, vgrad_two, ugm, sgrad, wsgrad, pwgrad, cwgrad),
        planes,
        classes,
        devices,
    )
    wi_grad = weight_pieces(table_out, rows, pcot, 384, planes, "input_grad")
    in_grad = [jnp.concatenate(pair, axis=1) for pair in zip(wi_grad, small_grad)]
    in_share = scatter_pieces(grid, in_grad[0], in_grad[1:])
    tokens_grad = token_part(table_in, pcot, one_cot, pieces, wide_block).reshape(samples, seq, width)
    repacked = place(in_origin, in_place, [second] + arrived)
    class_bias_grad = lax.psum(jnp.sum(logits_grad.astype(F32), axis=0), AXES)

    half = cut + 128
    input_share = jnp.concatenate([in_share[:, :cut], in_share[:, half : half + cut]], axis=1)
    flat = lambda size: jax.ShapeDtypeStruct((1, size), F32)
    group = stu // devices
    outs = pl.pallas_call(
        functools.partial(finish_kernel, group=group, classes=classes, up_size=ff // devices),
        out_shape=[flat(shard)] * 8
        + [
            jax.ShapeDtypeStruct((group, 64), F32),
            jax.ShapeDtypeStruct((group, 64), F32),
            jax.ShapeDtypeStruct((group, classes), F32),
        ]
        + [flat(group)] * 3
        + [flat(ff // devices)],
        name="finish",
    )(in_share[:, half + cut :])
    qb, vb, ob, g1, s1, db, g2, s2 = (o.reshape(-1) for o in outs[:8])
    up_half = ff // 2
    wu_share = jnp.concatenate(
        [ff_share[:, :up_half], ff_share[:, up_half + width // 2 : ff + width // 2]], axis=1
    )
    wo_share = jnp.concatenate(
        [ff_share[:, up_half : up_half + width // 2], ff_share[:, ff + width // 2 :]], axis=1
    )
    return (
        repacked,
        student_logits,
        tokens_grad,
        input_share,
        qb,
        vb,
        wo_share,
        ob,
        g1,
        s1,
        wu_share,
        outs[14].reshape(-1),
        wd_share.astype(F32),
        db,
        g2,
        s2,
        in_share[:, cut:half],
        outs[11].reshape(-1),
        outs[12].reshape(-1),
        jnp.concatenate(outs[8:10], axis=1),
        outs[13].reshape(-1),
        outs[10],
        class_bias_grad,
    )


def solution(mesh):
    both = P(AXES)
    matrix = P(AXES, None)
    cube = P(AXES, None, None)
    return jax.shard_map(
        body,
        mesh=mesh,
        in_specs=(
            cube,
            matrix,
            both,
            both,
            matrix,
            both,
            both,
            both,
            matrix,
            both,
            matrix,
            both,
            both,
            both,
            matrix,
            both,
            both,
            matrix,
            both,
            matrix,
            P(),
            both,
            both,
            P(),
            cube,
            matrix,
        ),
        out_specs=(
            cube,
            matrix,
            cube,
            matrix,
            both,
            both,
            matrix,
            both,
            both,
            both,
            matrix,
            both,
            matrix,
            both,
            both,
            both,
            matrix,
            both,
            both,
            matrix,
            both,
            matrix,
            P(),
        ),
        check_vma=False,
    )
```

```python
import functools
import itertools
import math

import jax
import jax.numpy as jnp
from jax import lax
from jax.experimental import pallas as pl
from jax.experimental.pallas import tpu as pltpu
from jax.sharding import PartitionSpec as P

HEADS = 12
HEAD_DIM = 64
STU_HEADS = 2
LAYER = 6
EPS = 1e-06
MASKED = -1e30
AXES = ("dp", "fsdp")
F32 = jnp.float32
BF16 = jnp.bfloat16
VMEM_LIMIT = 60 * 1024 * 1024

QB, VB, OB, G1, S1, DB, G2, S2 = range(8)


def dot(left, right):
    return jnp.dot(left, right, preferred_element_type=F32)


def dot_nt(left, right):
    return lax.dot_general(left, right, (((1,), (1,)), ((), ())), preferred_element_type=F32)


def dot_tn(left, right):
    return lax.dot_general(left, right, (((0,), (0,)), ((), ())), preferred_element_type=F32)


def params(limit=VMEM_LIMIT):
    return pltpu.CompilerParams(vmem_limit_bytes=limit, dimension_semantics=("arbitrary",))


def cost(flops, nbytes):
    return pl.CostEstimate(
        flops=int(0.3 * flops), bytes_accessed=int(0.3 * nbytes), transcendentals=0
    )


def whole(shape, index=None):
    index = index or (0,) * len(shape)
    return pl.BlockSpec(shape, lambda i, *_: index, pipeline_mode=pl.Buffered(1))


def rows_spec(rows, width):
    return pl.BlockSpec((rows, width), lambda i, *_: (i, 0))


def kept(shape):
    return pl.BlockSpec(shape, lambda i, *_: (0,) * len(shape))


def layer_norm(total):
    mean = jnp.mean(total, axis=-1, keepdims=True)
    centered = total - mean
    factor = lax.rsqrt(jnp.mean(centered * centered, axis=-1, keepdims=True) + EPS)
    return centered * factor, factor


def layer_norm_back(cot, gain, normed, factor):
    scaled = cot * gain
    inner = (
        scaled
        - jnp.mean(scaled, axis=-1, keepdims=True)
        - normed * jnp.mean(scaled * normed, axis=-1, keepdims=True)
    )
    return factor * inner


def gelu_parts(up):
    phi = 0.5 + 0.5 * lax.erf(up * (1.0 / math.sqrt(2.0)))
    bell = jnp.exp(up * up * -0.5) * (1.0 / math.sqrt(2.0 * math.pi))
    return up * phi, phi + up * bell


def column_sum(matrix):
    return jnp.sum(matrix, axis=0, keepdims=True)


def stack_rows(rows, count):
    width = rows[0].shape[1]
    pad = count - len(rows)
    if pad:
        rows = list(rows) + [jnp.zeros((pad, width), F32)]
    return jnp.concatenate(rows, axis=0)


def one_hot_rows(count, width, group, stride, skip):
    row = lax.broadcasted_iota(jnp.int32, (count, width), 0)
    column = lax.broadcasted_iota(jnp.int32, (count, width), 1)
    shift = group.bit_length() - 1
    wanted = (row >> shift) * stride + skip + (row & (group - 1))
    return jnp.where(column == wanted, 1.0, 0.0).astype(BF16)


def turn_lanes(matrix):
    return pltpu.roll(matrix, 64, 1)


def read_small(block, vec_ref, sv_ref, pw_ref, cw_ref, ub_ref, cb_ref, stu, classes, devices, up_size):
    width = block.shape[0]
    shard = width // devices
    group = stu // devices
    lane = lax.broadcasted_iota(jnp.int32, (stu, 128), 1)
    left, right, rest = (
        dot(one_hot_rows(stu, width, group, shard, n * group), block) for n in range(3)
    )
    pw_ref[...] = jnp.where(lane < 64, turn_lanes(left), right).astype(BF16)
    rest = turn_lanes(rest)
    cw_ref[...] = jnp.where(lane < classes, rest, 0.0).astype(BF16)
    sv_ref[...] = rest.T[classes : classes + 8]
    low, high = (
        dot(one_hot_rows(devices, width, 1, shard, 3 * group + n), block) for n in range(2)
    )
    lane = lax.broadcasted_iota(jnp.int32, (devices, 128), 1)
    ub_ref[...] = jnp.where(lane < 64, turn_lanes(low), high)
    vec_ref[...] = block.astype(F32).T[:8]
    skip = 3 * group + pl.cdiv(up_size, 64)
    high, low = (dot(one_hot_rows(devices, width, 1, shard, skip + n), block) for n in range(2))
    cb_ref[...] = jnp.broadcast_to(turn_lanes(column_sum(high + low)), cb_ref.shape)


def pack_kernel(here, *refs, classes, group):
    wi_ref, ws_ref, wo_ref, wu_ref, ub_ref, pw_ref, cw_ref, lg_ref = refs[:8]
    columns, vectors = refs[8:11], refs[11:19]
    in_mine, in_other, ff_mine, ff_other, held = refs[19:]
    shard = wi_ref.shape[0]
    held[...] = jnp.zeros_like(held)
    for n, vector in enumerate(vectors):
        held[n : n + 1, :shard] = vector[...].astype(F32)
    left = held[:128].T[:shard]
    held[:8] = jnp.zeros((8, 128), F32)
    for n, column in enumerate(columns):
        held[classes + n : classes + n + 1, :group] = column[...].astype(F32)
    held[128 : 128 + group, :classes] = cw_ref[...].astype(F32)
    rest = held[128 : 128 + group] + held[:128].T[:group]
    up_size = ub_ref.shape[1]
    held[136:137, :up_size] = ub_ref[...].astype(F32)
    up = held[136:137]
    total = column_sum(lg_ref[...].astype(F32))
    high = total.astype(BF16).astype(F32)
    held[144:145, :classes] = high
    held[145:146, :classes] = total - high
    pool = pw_ref[...].astype(F32)
    rows = [turn_lanes(pool), pool, turn_lanes(rest), turn_lanes(up)]
    if up_size > 64:
        rows.append(up)
    rows.append(turn_lanes(held[144:146]))
    spare = shard - sum(r.shape[0] for r in rows)
    if spare:
        rows.append(jnp.zeros((spare, 128), F32))
    lane = lax.broadcasted_iota(jnp.int32, (shard, 128), 1)
    small = jnp.where(lane < 64, left, jnp.concatenate(rows, axis=0)).astype(BF16)
    cut = wi_ref.shape[1] // 2
    width = wo_ref.shape[1]
    part = ff_mine.shape[1] - width
    for core, (a, b, c, d) in enumerate(
        ((in_mine, in_other, ff_mine, ff_other), (in_other, in_mine, ff_other, ff_mine))
    ):

        @pl.when(here[3] == core)
        def _():
            a[:, :cut] = wi_ref[:, :cut]
            a[:, cut:] = ws_ref[...]
            b[:, :cut] = wi_ref[:, cut:]
            b[:, cut:] = small
            c[:, :width] = wo_ref[...]
            c[:, width:] = wu_ref[:, :part]
            d[...] = wu_ref[:, part:]


def pack(here, wi, ws, wo, wu, ub, pw, cw, lg, columns, vectors):
    shard = wi.shape[0]
    group, classes = cw.shape
    flat = lambda v: v.reshape(1, -1)
    first = jax.ShapeDtypeStruct((shard, wi.shape[1] // 2 + 128), BF16)
    second = jax.ShapeDtypeStruct((shard, (wo.shape[1] + wu.shape[1]) // 2), BF16)
    args = (wi, ws, wo, wu, flat(ub), pw, cw, lg, *map(flat, columns), *map(flat, vectors))
    return pl.pallas_call(
        functools.partial(pack_kernel, classes=classes, group=group),
        grid_spec=pltpu.PrefetchScalarGridSpec(
            num_scalar_prefetch=1,
            grid=(1,),
            in_specs=[whole(a.shape) for a in args],
            out_specs=[kept(o.shape) for o in (first, first, second, second)],
            scratch_shapes=[pltpu.VMEM((152, 128), F32)],
        ),
        out_shape=[first, first, second, second],
        compiler_params=params(),
        cost_estimate=cost(1e6, 1e6),
        name="pack",
    )(here, *args)


def attend_kernel(lens, here, *refs, copies, size, seq, width, stu, classes, devices, up_size):
    x_ref = refs[0]
    pieces = refs[1:-14]
    qkv_ref, prob_ref, mixed_ref, turned_ref, vec_ref, sv_ref, pw_ref = refs[-14:-7]
    cw_ref, ub_ref, cb_ref, ws_ref, w_ref, held, sem = refs[-7:]
    step = pl.program_id(0)
    half = w_ref.shape[1] // 2
    cut = half - 128

    @pl.when(step == 0)
    def _():
        fetch(copies, here, size, pieces, w_ref, sem)
        ws_ref[...] = w_ref[:, cut:half]
        read_small(
            w_ref[:, half + cut :],
            vec_ref,
            sv_ref,
            pw_ref,
            cw_ref,
            ub_ref,
            cb_ref,
            stu,
            classes,
            devices,
            up_size,
        )

    rows = x_ref.shape[0]
    lines = line_rows(here, size, width // (size["y"] * size["z"]))
    turn_lines(x_ref[...], lines, held, turned_ref, slice(0, rows))
    x = x_ref[...]
    vec = vec_ref[...]
    query = dot(x, w_ref[:, :width]) + vec[QB : QB + 1]
    qkv_ref[:, :width] = query.astype(BF16)
    split = 2 * width - cut
    qkv_ref[:, width:cut] = dot(x, w_ref[:, width:cut]).astype(BF16)
    qkv_ref[:, cut : 2 * width] = dot(x, w_ref[:, half : half + split]).astype(BF16)
    value = dot(x, w_ref[:, half + split : half + cut]) + vec[VB : VB + 1]
    qkv_ref[:, 2 * width :] = value.astype(BF16)
    lane = lax.broadcasted_iota(jnp.int32, (seq, 128), 1)
    first_head = lane < HEAD_DIM
    place = lax.broadcasted_iota(jnp.int32, (seq, 2 * seq), 0)
    scale = jnp.asarray(1.0 / math.sqrt(HEAD_DIM), BF16)
    for s in range(rows // seq):
        valid = place < lens[step * (rows // seq) + s]
        at = slice(s * seq, (s + 1) * seq)
        for pair in range(width // 128):
            low = pair * 128
            q = qkv_ref[at, low : low + 128] * scale
            k = qkv_ref[at, width + low : width + low + 128]
            v = qkv_ref[at, 2 * width + low : 2 * width + low + 128]
            zero = jnp.zeros_like(q)
            both = jnp.concatenate(
                [jnp.where(first_head, q, zero), jnp.where(first_head, zero, q)], axis=0
            )
            scores = jnp.where(valid, dot_nt(k, both), MASKED)
            raised = jnp.exp(scores - jnp.max(scores, axis=0, keepdims=True))
            share = raised * (1.0 / jnp.sum(raised, axis=0, keepdims=True))
            share = share.astype(BF16)
            prob_ref[s, pair] = share
            out = dot_tn(share, v)
            mixed_ref[at, low : low + 128] = jnp.where(first_head, out[:seq], out[seq:]).astype(BF16)


def attend(lens, gather, rows, seq, block, stu, classes, devices, up_size):
    copies, here, size = gather.plan(), gather.grid.here, gather.grid.size
    pieces = gather.parts
    count, width = rows.shape
    pairs = width // 128
    samples = block // seq
    columns = gather.columns
    small = [
        jax.ShapeDtypeStruct((8, width), F32),
        jax.ShapeDtypeStruct((8, stu), F32),
        jax.ShapeDtypeStruct((stu, stu), BF16),
        jax.ShapeDtypeStruct((stu, 128), BF16),
        jax.ShapeDtypeStruct((devices, 128), F32),
        jax.ShapeDtypeStruct((8, 128), F32),
        jax.ShapeDtypeStruct((width, stu), BF16),
    ]
    return pl.pallas_call(
        functools.partial(
            attend_kernel,
            copies=copies,
            size=size,
            seq=seq,
            width=width,
            stu=stu,
            classes=classes,
            devices=devices,
            up_size=up_size,
        ),
        grid_spec=pltpu.PrefetchScalarGridSpec(
            num_scalar_prefetch=2,
            grid=(count // block,),
            in_specs=[rows_spec(block, width)] + [pl.BlockSpec(memory_space=pl.ANY)] * len(pieces),
            out_specs=[
                rows_spec(block, 3 * width),
                pl.BlockSpec((samples, pairs, seq, 2 * seq), lambda i, *_: (i, 0, 0, 0)),
                rows_spec(block, width),
                pl.BlockSpec((width, block), lambda i, *_: (0, i)),
            ]
            + [kept(s.shape) for s in small],
            scratch_shapes=[
                pltpu.VMEM((width, columns), BF16),
                pltpu.VMEM((width, block), BF16),
                pltpu.SemaphoreType.DMA((len(copies),)),
            ],
        ),
        out_shape=[
            jax.ShapeDtypeStruct((count, 3 * width), BF16),
            jax.ShapeDtypeStruct((count // seq, pairs, seq, 2 * seq), BF16),
            jax.ShapeDtypeStruct((count, width), BF16),
            jax.ShapeDtypeStruct((width, count), BF16),
        ]
        + small,
        compiler_params=params(),
        cost_estimate=cost(2 * count * width * 3 * width * 2, 30e6),
        name="attend",
    )(lens, here, rows, *pieces)


def up_kernel(here, *refs, copies, size, chunk):
    mixed_ref, x_ref, vec_ref, ub_ref = refs[:4]
    pieces = refs[4:-7]
    norm_ref, factor_ref, low_ref, act_ref, slope_ref, w_ref, sem = refs[-7:]
    width = x_ref.shape[1]

    @pl.when(pl.program_id(0) == 0)
    def _():
        fetch(copies, here, size, pieces, w_ref, sem)

    vec = vec_ref[...]
    total = dot(mixed_ref[...], w_ref[:, :width]) + vec[OB : OB + 1] + x_ref[...].astype(F32)
    normed, factor = layer_norm(total)
    norm_ref[...] = normed
    factor_ref[...] = jnp.broadcast_to(factor, factor_ref.shape)
    low_ref[...] = (normed * vec[G1 : G1 + 1] + vec[S1 : S1 + 1]).astype(BF16)
    low = low_ref[...]
    for begin in range(0, act_ref.shape[1], chunk):
        at = slice(begin, begin + chunk)
        for first in range(0, low.shape[0], 128):
            rows = slice(first, first + 128)
            up = dot(low[rows], w_ref[:, width + begin : width + begin + chunk]) + ub_ref[0:1, at]
            act, slope = gelu_parts(up)
            act_ref[rows, at] = act.astype(BF16)
            slope_ref[rows, at] = slope.astype(BF16)


def up_part(gather, mixed, rows, vec, ub, block):
    copies, here, size = gather.plan(), gather.grid.here, gather.grid.size
    pieces = gather.parts
    count, width = rows.shape
    ff = gather.columns - width
    return pl.pallas_call(
        functools.partial(up_kernel, copies=copies, size=size, chunk=256),
        grid_spec=pltpu.PrefetchScalarGridSpec(
            num_scalar_prefetch=1,
            grid=(count // block,),
            in_specs=[
                rows_spec(block, width),
                rows_spec(block, width),
                whole(vec.shape),
                whole(ub.shape),
            ]
            + [pl.BlockSpec(memory_space=pl.ANY)] * len(pieces),
            out_specs=[
                rows_spec(block, width),
                rows_spec(block, 128),
                rows_spec(block, width),
                rows_spec(block, ff),
                rows_spec(block, ff),
            ],
            scratch_shapes=[
                pltpu.VMEM((width, gather.columns), BF16),
                pltpu.SemaphoreType.DMA((len(copies),)),
            ],
        ),
        out_shape=[
            jax.ShapeDtypeStruct((count, width), F32),
            jax.ShapeDtypeStruct((count, 128), F32),
            jax.ShapeDtypeStruct((count, width), BF16),
            jax.ShapeDtypeStruct((count, ff), BF16),
            jax.ShapeDtypeStruct((count, ff), BF16),
        ],
        compiler_params=params(),
        cost_estimate=cost(2 * count * width * (ff + width) * 2, 50e6),
        name="up_part",
    )(here, mixed, rows, vec, ub, *pieces)


def down_kernel(lens, alive, *refs, seq, steps, tile):
    act_hbm, norm_ref, cot_ref, lg_ref, wd_ref, vec_ref, ws_ref, sv_ref, pw_ref, cw_ref = refs[:10]
    second_ref, sum_ref, dcot_ref, logits_ref, vgrad_ref, sgrad_ref = refs[10:16]
    wsgrad_ref, pwgrad_ref, cwgrad_ref, grad_ref, act_all, turned, sem = refs[16:]
    step = pl.program_id(0)
    rows = norm_ref.shape[0]

    def load(n):
        at = pl.ds(pl.multiple_of(n * rows, rows), rows)
        return pltpu.make_async_copy(act_hbm.at[at], act_all.at[at], sem.at[n])

    @pl.when(step == 0)
    def _():
        load(0).start()

    @pl.when(step + 1 < steps)
    def _():
        load(step + 1).start()

    @pl.when(step < steps)
    def _():
        load(step).wait()
        at = pl.ds(pl.multiple_of(step * rows, rows), rows)
        down_rows(
            lens,
            alive,
            (act_all.at[at], norm_ref, cot_ref, lg_ref, wd_ref, vec_ref, ws_ref, sv_ref, pw_ref, cw_ref),
            (second_ref, sum_ref, dcot_ref, logits_ref, vgrad_ref, sgrad_ref),
            (wsgrad_ref, pwgrad_ref, cwgrad_ref),
            seq,
        )
        turned[:, at] = dcot_ref[...].T

    @pl.when(step >= steps)
    def _():
        at = pl.ds(pl.multiple_of((step - steps) * tile, tile), tile)
        grad_ref[...] = dot(turned[...], act_all[:, at]).astype(BF16).T


def down_rows(lens, alive, ins, outs, sums, seq):
    act_ref, norm_ref, cot_ref, lg_ref, wd_ref, vec_ref, ws_ref, sv_ref, pw_ref, cw_ref = ins
    second_ref, sum_ref, dcot_ref, logits_ref, vgrad_ref, sgrad_ref = outs
    wsgrad_ref, pwgrad_ref, cwgrad_ref = sums
    step = pl.program_id(0)
    rows = norm_ref.shape[0]
    samples = rows // seq
    vec = vec_ref[...]
    sv = sv_ref[...]
    stu = sv.shape[1]
    pool_width = stu // STU_HEADS
    pool_scale = 1.0 / math.sqrt(pool_width)

    @pl.when(step == 0)
    def _():
        vgrad_ref[...] = jnp.zeros_like(vgrad_ref)
        sgrad_ref[...] = jnp.zeros_like(sgrad_ref)
        wsgrad_ref[...] = jnp.zeros_like(wsgrad_ref)
        pwgrad_ref[...] = jnp.zeros_like(pwgrad_ref)
        cwgrad_ref[...] = jnp.zeros_like(cwgrad_ref)

    first = norm_ref[...] * vec[G1 : G1 + 1] + vec[S1 : S1 + 1]
    down = dot(act_ref[...], wd_ref[...]) + vec[DB : DB + 1]
    normed, factor = layer_norm(first + down)
    second = (normed * vec[G2 : G2 + 1] + vec[S2 : S2 + 1]).astype(BF16)
    reduced = (dot(second, ws_ref[...]) + sv[0:1]).astype(BF16)
    head_of = lax.broadcasted_iota(jnp.int32, (stu, stu), 0) // pool_width
    same = head_of == lax.broadcasted_iota(jnp.int32, (stu, stu), 1) // pool_width
    pool_query = sv[1:2]
    query_table = jnp.where(same, jnp.broadcast_to(pool_query, (stu, stu)), 0.0).astype(BF16)
    scores = dot_nt(reduced, query_table) * pool_scale
    place = lax.broadcasted_iota(jnp.int32, (seq, stu), 0)
    shares = []
    pooled_rows = []
    for s in range(samples):
        at = slice(s * seq, (s + 1) * seq)
        part = jnp.where(place < lens[step * samples + s], scores[at], MASKED)
        raised = jnp.exp(part - jnp.max(part, axis=0, keepdims=True))
        share = raised / jnp.sum(raised, axis=0, keepdims=True)
        shares.append(share)
        pooled_rows.append(column_sum(share * reduced[at].astype(F32)))
    pooled = stack_rows(pooled_rows, 8).astype(BF16)
    squashed = jnp.tanh(dot(pooled, pw_ref[...]) + sv[2:3])
    squashed_low = squashed.astype(BF16)
    logits_ref[...] = dot(squashed_low, cw_ref[...])
    lg = lg_ref[...]
    cwgrad_ref[...] += dot_tn(squashed_low, lg)
    hidden_cot = (dot_nt(lg, cw_ref[...]) * (1.0 - squashed * squashed)).astype(BF16)
    pwgrad_ref[...] += dot_tn(pooled, hidden_cot)
    pooled_cot = dot_nt(hidden_cot, pw_ref[...]).astype(BF16).astype(F32)
    query_grad = jnp.zeros((1, stu), F32)
    cots = []
    for s in range(samples):
        at = slice(s * seq, (s + 1) * seq)
        row = pooled_cot[s : s + 1]
        table = jnp.where(same, jnp.broadcast_to(row, (stu, stu)), 0.0).astype(BF16)
        share_cot = dot_nt(reduced[at], table)
        share = shares[s]
        score_cot = share * (share_cot - column_sum(share * share_cot))
        query_grad += column_sum(score_cot * reduced[at].astype(F32)) * pool_scale
        cots.append((share * row + score_cot * (pool_query * pool_scale)).astype(BF16))
    reduced_cot = jnp.concatenate(cots, axis=0)
    sgrad_ref[...] += stack_rows(
        [
            column_sum(reduced_cot.astype(F32)),
            query_grad,
            column_sum(hidden_cot.astype(F32)),
        ],
        8,
    )
    wsgrad_ref[...] += dot_tn(reduced_cot, second)
    back = dot_nt(reduced_cot, ws_ref[...])
    parts = []
    for s in range(samples):
        at = slice(s * seq, (s + 1) * seq)
        live = alive[step * samples + s] > 0
        parts.append(back[at] + jnp.where(live, cot_ref[at].astype(F32), 0.0))
        second_ref[at] = jnp.where(live, second[at], jnp.zeros_like(second[at]))
    total = jnp.concatenate(parts, axis=0)
    sum_cot = layer_norm_back(total, vec[G2 : G2 + 1], normed, factor)
    sum_ref[...] = sum_cot
    down_cot = sum_cot.astype(BF16)
    dcot_ref[...] = down_cot
    vgrad_ref[...] += stack_rows(
        [column_sum(total * normed), column_sum(total), column_sum(down_cot.astype(F32))], 8
    )


def down_part(lens, alive, act, normed, cot, lg, wd, vec, ws, sv, pw, cw, seq, block, tile):
    count, ff = act.shape
    width = normed.shape[1]
    stu = ws.shape[1]
    steps = count // block

    def block_rows(height, columns):
        return pl.BlockSpec((height, columns), lambda i, *_: (jnp.minimum(i, steps - 1), 0))

    return pl.pallas_call(
        functools.partial(down_kernel, seq=seq, steps=steps, tile=tile),
        grid_spec=pltpu.PrefetchScalarGridSpec(
            num_scalar_prefetch=2,
            grid=(steps + ff // tile,),
            in_specs=[
                pl.BlockSpec(memory_space=pl.ANY),
                block_rows(block, width),
                block_rows(block, width),
                block_rows(8, 128),
                whole(wd.shape),
                whole(vec.shape),
                whole(ws.shape),
                whole(sv.shape),
                whole(pw.shape),
                whole(cw.shape),
            ],
            out_specs=[
                block_rows(block, width),
                block_rows(block, width),
                block_rows(block, width),
                block_rows(8, 128),
                kept((8, width)),
                kept((8, stu)),
                kept((stu, width)),
                kept((stu, stu)),
                kept((stu, 128)),
                pl.BlockSpec((tile, width), lambda i, *_: (jnp.maximum(i - steps, 0), 0)),
            ],
            scratch_shapes=[
                pltpu.VMEM((count, ff), BF16),
                pltpu.VMEM((width, count), BF16),
                pltpu.SemaphoreType.DMA((steps,)),
            ],
        ),
        out_shape=[
            jax.ShapeDtypeStruct((count, width), BF16),
            jax.ShapeDtypeStruct((count, width), F32),
            jax.ShapeDtypeStruct((count, width), BF16),
            jax.ShapeDtypeStruct((steps * 8, 128), F32),
            jax.ShapeDtypeStruct((8, width), F32),
            jax.ShapeDtypeStruct((8, stu), F32),
            jax.ShapeDtypeStruct((stu, width), F32),
            jax.ShapeDtypeStruct((stu, stu), F32),
            jax.ShapeDtypeStruct((stu, 128), F32),
            jax.ShapeDtypeStruct((ff, width), BF16),
        ],
        compiler_params=params(),
        cost_estimate=cost(2 * count * width * ff * 4, 60e6),
        name="down_part",
    )(lens, alive, act, normed, cot, lg, wd, vec, ws, sv, pw, cw)


def turn_lines(block, lines, held, to, at):
    held[...] = block.T
    rows = to.shape[0] // len(lines)
    for n, line in enumerate(lines):
        to[n * rows : (n + 1) * rows, at] = held[pl.ds(line, rows)]


def up_back_kernel(here, *refs, copies, size, steps, chunk, tile):
    dcot_ref, slope_ref, sum_ref, norm_ref, factor_ref, low_ref, mixed_ref, wd_ref, vec_ref = refs[:9]
    pieces = refs[9:-15]
    one_ref, mcot_ref, vgrad_ref, ugrad_ref = refs[-15:-11]
    up_other, up_mine, out_other, out_mine = refs[-11:-7]
    w_ref, ucot_all, acot_all, low_turned, mixed_turned, held, sem = refs[-7:]
    step = pl.program_id(0)
    rows, width = dcot_ref.shape
    ff = slope_ref.shape[1]
    core = here[3]
    lines = line_rows(here, size, width // (size["y"] * size["z"]))

    @pl.when(step == 0)
    def _():
        fetch(copies, here, size, pieces, w_ref, sem)
        vgrad_ref[...] = jnp.zeros_like(vgrad_ref)
        ugrad_ref[...] = jnp.zeros_like(ugrad_ref)

    @pl.when(step < steps)
    def _():
        vec = vec_ref[...]
        at_rows = pl.ds(pl.multiple_of(step * rows, rows), rows)
        down_cot = dcot_ref[...]
        for begin in range(0, ff, chunk):
            at = slice(begin, begin + chunk)
            up_cot = dot_nt(down_cot, wd_ref[at, :]) * slope_ref[:, at].astype(F32)
            ugrad_ref[0:1, at] += column_sum(up_cot)
            ucot_all[at_rows, at] = up_cot.astype(BF16)
        turn_lines(low_ref[...], lines, held, low_turned, at_rows)
        turn_lines(mixed_ref[...], lines, held, mixed_turned, at_rows)
        cot = sum_ref[...] + dot_nt(ucot_all[at_rows, :], w_ref[:, width:])
        normed = norm_ref[...]
        one_cot = layer_norm_back(cot, vec[G1 : G1 + 1], normed, factor_ref[:, 0:1])
        one_ref[...] = one_cot
        low = one_cot.astype(BF16)
        acot_all[at_rows, :] = low
        mcot_ref[...] = dot_nt(low, w_ref[:, :width]).astype(BF16)
        vgrad_ref[...] += stack_rows(
            [column_sum(cot * normed), column_sum(cot), column_sum(one_cot)], 8
        )

    per = ff // 2 // tile

    def up_tile(n, half):
        first = (half * per + n) * tile
        return dot(low_turned[...], ucot_all[:, pl.ds(pl.multiple_of(first, 128), tile)])

    def out_tile(half):
        first = half * (width // 2)
        return dot(mixed_turned[...], acot_all[:, pl.ds(pl.multiple_of(first, 128), width // 2)])

    @pl.when((step >= steps) & (step < steps + per))
    def _():
        up_other[...] = up_tile(step - steps, 1 - core).astype(BF16)

    @pl.when(step == steps + per)
    def _():
        out_other[...] = out_tile(1 - core).astype(BF16)
        out_mine[...] = out_tile(core).astype(BF16)

    @pl.when(step > steps + per)
    def _():
        up_mine[...] = up_tile(step - steps - per - 1, core).astype(BF16)


def up_back(gather, dcot, slope, sum_two, normed, factor, low, mixed, wd, vec, block, tile):
    copies, here, size = gather.plan(), gather.grid.here, gather.grid.size
    pieces = gather.parts
    count, width = dcot.shape
    ff = slope.shape[1]
    steps = count // block
    per = ff // 2 // tile

    def block_rows(columns):
        return pl.BlockSpec((block, columns), lambda i, *_: (jnp.minimum(i, steps - 1), 0))

    def tiles(begin):
        return pl.BlockSpec(
            (width, tile), lambda i, *_: (0, jnp.clip(i - begin, 0, per - 1))
        )

    return pl.pallas_call(
        functools.partial(
            up_back_kernel, copies=copies, size=size, steps=steps, chunk=512, tile=tile
        ),
        grid_spec=pltpu.PrefetchScalarGridSpec(
            num_scalar_prefetch=1,
            grid=(steps + 2 * per + 1,),
            in_specs=[
                block_rows(width),
                block_rows(ff),
                block_rows(width),
                block_rows(width),
                block_rows(128),
                block_rows(width),
                block_rows(width),
                whole(wd.shape),
                whole(vec.shape),
            ]
            + [pl.BlockSpec(memory_space=pl.ANY)] * len(pieces),
            out_specs=[
                block_rows(width),
                block_rows(width),
                kept((8, width)),
                kept((8, ff)),
                tiles(steps),
                tiles(steps + per + 1),
                kept((width, width // 2)),
                kept((width, width // 2)),
            ],
            scratch_shapes=[
                pltpu.VMEM((width, gather.columns), BF16),
                pltpu.VMEM((count, ff), BF16),
                pltpu.VMEM((count, width), BF16),
                pltpu.VMEM((width, count), BF16),
                pltpu.VMEM((width, count), BF16),
                pltpu.VMEM((width, block), BF16),
                pltpu.SemaphoreType.DMA((len(copies),)),
            ],
        ),
        out_shape=[
            jax.ShapeDtypeStruct((count, width), F32),
            jax.ShapeDtypeStruct((count, width), BF16),
            jax.ShapeDtypeStruct((8, width), F32),
            jax.ShapeDtypeStruct((8, ff), F32),
            jax.ShapeDtypeStruct((width, ff // 2), BF16),
            jax.ShapeDtypeStruct((width, ff // 2), BF16),
            jax.ShapeDtypeStruct((width, width // 2), BF16),
            jax.ShapeDtypeStruct((width, width // 2), BF16),
        ],
        compiler_params=params(),
        cost_estimate=cost(2 * count * width * ff * 4, 60e6),
        name="up_back",
    )(here, dcot, slope, sum_two, normed, factor, low, mixed, wd, vec, *pieces)


def attend_back_kernel(mcot_ref, qkv_ref, prob_ref, pcot_ref, vgrad_ref, *, seq, width):
    @pl.when(pl.program_id(0) == 0)
    def _():
        vgrad_ref[...] = jnp.zeros_like(vgrad_ref)

    attend_back_rows(mcot_ref, qkv_ref, prob_ref, pcot_ref, vgrad_ref, seq, width)


def input_grad_kernel(here, turned_ref, pcot_ref, other, mine, *, per):
    step = pl.program_id(0)
    grad = dot(turned_ref[...], pcot_ref[...]).astype(BF16)

    @pl.when(step < per)
    def _():
        other[...] = grad

    @pl.when(step >= per)
    def _():
        mine[...] = grad


def input_grad(here, turned, pcot, tile):
    width, count = turned.shape
    half = pcot.shape[1] // 2
    per = half // tile

    def columns(i, t):
        core = t[3]
        return (0, jnp.where(i < per, (1 - core) * per + i, core * per + i - per))

    return pl.pallas_call(
        functools.partial(input_grad_kernel, per=per),
        grid_spec=pltpu.PrefetchScalarGridSpec(
            num_scalar_prefetch=1,
            grid=(2 * per,),
            in_specs=[whole((width, count)), pl.BlockSpec((count, tile), columns)],
            out_specs=[
                pl.BlockSpec((width, tile), lambda i, t: (0, jnp.minimum(i, per - 1))),
                pl.BlockSpec((width, tile), lambda i, t: (0, jnp.maximum(i - per, 0))),
            ],
        ),
        out_shape=[jax.ShapeDtypeStruct((width, half), BF16)] * 2,
        compiler_params=params(),
        cost_estimate=cost(4 * count * width * half, 20e6),
        name="input_grad",
    )(here, turned, pcot)


def attend_back_rows(mcot_ref, qkv_ref, prob_ref, pcot_ref, vgrad_ref, seq, width):
    rows = mcot_ref.shape[0]
    lane = lax.broadcasted_iota(jnp.int32, (seq, 128), 1)
    first_head = lane < HEAD_DIM
    scale = 1.0 / math.sqrt(HEAD_DIM)

    def split(part):
        zero = jnp.zeros_like(part)
        return jnp.concatenate(
            [jnp.where(first_head, part, zero), jnp.where(first_head, zero, part)], axis=0
        )

    for s in range(rows // seq):
        at = slice(s * seq, (s + 1) * seq)
        for pair in range(width // 128):
            low = pair * 128
            q = split(qkv_ref[at, low : low + 128])
            k = qkv_ref[at, width + low : width + low + 128]
            v = qkv_ref[at, 2 * width + low : 2 * width + low + 128]
            cot = split(mcot_ref[at, low : low + 128])
            share = prob_ref[s, pair]
            share_cot = dot_nt(v, cot)
            pcot_ref[at, 2 * width + low : 2 * width + low + 128] = dot(share, cot).astype(BF16)
            wide = share.astype(F32)
            product = wide * share_cot
            score_cot = (product - wide * column_sum(product)).astype(BF16)
            pcot_ref[at, width + low : width + low + 128] = (dot(score_cot, q) * scale).astype(BF16)
            query_cot = dot_tn(score_cot, k) * scale
            pcot_ref[at, low : low + 128] = jnp.where(
                first_head, query_cot[:seq], query_cot[seq:]
            ).astype(BF16)
    vgrad_ref[...] += stack_rows(
        [
            column_sum(pcot_ref[:, :width].astype(F32)),
            column_sum(pcot_ref[:, 2 * width :].astype(F32)),
        ],
        8,
    )


def attend_back(mcot, qkv, prob, seq, block):
    count, width = mcot.shape
    pairs = width // 128
    return pl.pallas_call(
        functools.partial(attend_back_kernel, seq=seq, width=width),
        grid_spec=pltpu.PrefetchScalarGridSpec(
            num_scalar_prefetch=0,
            grid=(count // block,),
            in_specs=[
                rows_spec(block, width),
                rows_spec(block, 3 * width),
                pl.BlockSpec((block // seq, pairs, seq, 2 * seq), lambda i: (i, 0, 0, 0)),
            ],
            out_specs=[rows_spec(block, 3 * width), kept((8, width))],
        ),
        out_shape=[
            jax.ShapeDtypeStruct((count, 3 * width), BF16),
            jax.ShapeDtypeStruct((8, width), F32),
        ],
        compiler_params=params(),
        cost_estimate=cost(2 * count * width * 3 * width * 2, 30e6),
        name="attend_back",
    )(mcot, qkv, prob)


def token_kernel(here, *refs, copies, size):
    pcot_ref, one_ref = refs[:2]
    pieces = refs[2:-3]
    out_ref, w_ref, sem = refs[-3:]

    @pl.when(pl.program_id(0) == 0)
    def _():
        fetch(copies, here, size, pieces, w_ref, sem)

    half = w_ref.shape[1] // 2
    cut = half - 128
    out_ref[...] = (
        one_ref[...]
        + dot_nt(pcot_ref[:, :cut], w_ref[:, :cut])
        + dot_nt(pcot_ref[:, cut:], w_ref[:, half : half + cut])
    )


def token_part(gather, pcot, one_cot, block):
    copies, here, size = gather.plan(), gather.grid.here, gather.grid.size
    pieces = gather.parts
    count, width = one_cot.shape
    return pl.pallas_call(
        functools.partial(token_kernel, copies=copies, size=size),
        grid_spec=pltpu.PrefetchScalarGridSpec(
            num_scalar_prefetch=1,
            grid=(count // block,),
            in_specs=[rows_spec(block, 3 * width), rows_spec(block, width)]
            + [pl.BlockSpec(memory_space=pl.ANY)] * len(pieces),
            out_specs=rows_spec(block, width),
            scratch_shapes=[
                pltpu.VMEM((width, gather.columns), BF16),
                pltpu.SemaphoreType.DMA((len(copies),)),
            ],
        ),
        out_shape=jax.ShapeDtypeStruct((count, width), F32),
        compiler_params=params(),
        cost_estimate=cost(2 * count * width * 3 * width, 25e6),
        name="token_part",
    )(here, pcot, one_cot, *pieces)


def small_kernel(here, *refs, size, classes, devices):
    vin_ref, vone_ref, vtwo_ref, ugrad_ref, sgrad_ref, wsgrad_ref, pwgrad_ref, cwgrad_ref = refs[:8]
    other_ref, mine_ref, halves = refs[8:]
    width = vin_ref.shape[1]
    stu = sgrad_ref.shape[1]
    shard = width // devices
    group = stu // devices
    halves[0] = wsgrad_ref[...].T
    vin, vone, vtwo = vin_ref[...], vone_ref[...], vtwo_ref[...]
    rows = [vin[0:1], vin[1:2], vone[2:3], vone[0:1], vone[1:2], vtwo[2:3], vtwo[0:1], vtwo[1:2]]
    block = stack_rows(rows, 128).T
    lane = lax.broadcasted_iota(jnp.int32, (stu, 128), 1)
    high = lane >= 64
    pwgrad = pwgrad_ref[...]
    spare = jnp.zeros((classes, stu), F32)
    rest = jnp.concatenate(
        [spare, sgrad_ref[0:3], jnp.zeros((128 - classes - 3, stu), F32)], axis=0
    ).T
    rest = rest + jnp.where(lane < classes, cwgrad_ref[...], 0.0)
    for n, part in enumerate((turn_lanes(pwgrad), pwgrad, turn_lanes(rest))):
        part = jnp.where(high, part, 0.0).astype(BF16)
        block = block + dot_tn(one_hot_rows(stu, width, group, shard, n * group), part)
    ugrad = ugrad_ref[...]
    high = lax.broadcasted_iota(jnp.int32, ugrad.shape, 1) >= 64
    for n, part in enumerate((turn_lanes(ugrad), ugrad)):
        part = jnp.where(high, part, 0.0).astype(BF16)
        block = block + dot_tn(one_hot_rows(devices, width, 1, shard, 3 * group + n), part)
    halves[1] = block
    core = here[3]
    rows = width // (size["y"] * size["z"])
    for n, line in enumerate(line_rows(here, size, rows)):
        at = pl.ds(line, rows)
        other_ref[n * rows : (n + 1) * rows] = halves[1 - core, at].astype(BF16)
        mine_ref[n * rows : (n + 1) * rows] = halves[core, at].astype(BF16)


def small_pieces(grid, grads, classes, devices):
    width = grads[0].shape[1]
    return pl.pallas_call(
        functools.partial(small_kernel, size=grid.size, classes=classes, devices=devices),
        grid_spec=pltpu.PrefetchScalarGridSpec(
            num_scalar_prefetch=1,
            grid=(1,),
            in_specs=[whole(g.shape) for g in grads],
            out_specs=[kept((width, 128))] * 2,
            scratch_shapes=[pltpu.VMEM((2, width, 128), F32)],
        ),
        out_shape=[jax.ShapeDtypeStruct((width, 128), BF16)] * 2,
        compiler_params=params(),
        cost_estimate=cost(1e8, 2e6),
        name="small_pieces",
    )(grid.here, *grads)


def finish_kernel(block_ref, *outs, group, classes, up_size):
    block = block_ref[...]
    shard = block.shape[0]
    columns = jnp.concatenate([block, jnp.zeros((128 - shard, 128), F32)], axis=0).T
    for n in range(8):
        outs[n][...] = columns[n : n + 1, :shard]
    outs[8][...] = block[:group, 64:]
    outs[9][...] = block[group : 2 * group, 64:]
    outs[10][...] = block[2 * group : 3 * group, 64 : 64 + classes]
    for n in range(3):
        row = columns[64 + classes + n : 64 + classes + n + 1]
        outs[11 + n][...] = row[:, 2 * group : 3 * group]
    first = min(64, up_size)
    outs[14][:, :first] = block[3 * group : 3 * group + 1, 64 : 64 + first]
    if up_size > first:
        outs[14][:, first:] = block[3 * group + 1 : 3 * group + 2, 64 : 64 + up_size - first]


def pick_kernel(table, source_ref, *refs, count):
    outs, held, sem_in, sem_out = refs[:-3], refs[-3], refs[-2], refs[-1]
    reads, writes = [], []
    for o, out in enumerate(outs):
        for j in range(count):
            n = o * count + j
            reads.append(pltpu.make_async_copy(source_ref.at[table[o, j]], held.at[n], sem_in.at[n]))
            writes.append(pltpu.make_async_copy(held.at[n], out.at[j], sem_out.at[n]))
    for copy in reads:
        copy.start()
    for read, write in zip(reads, writes):
        read.wait()
        write.start()
    for copy in writes:
        copy.wait()


def pick(table, source, outs, count):
    total = outs * count
    return pl.pallas_call(
        functools.partial(pick_kernel, count=count),
        grid_spec=pltpu.PrefetchScalarGridSpec(
            num_scalar_prefetch=1,
            grid=(1,),
            in_specs=[pl.BlockSpec(memory_space=pl.ANY)],
            out_specs=[pl.BlockSpec(memory_space=pl.ANY)] * outs,
            scratch_shapes=[
                pltpu.VMEM((total,) + source.shape[1:], source.dtype),
                pltpu.SemaphoreType.DMA((total,)),
                pltpu.SemaphoreType.DMA((total,)),
            ],
        ),
        out_shape=[jax.ShapeDtypeStruct((count,) + source.shape[1:], source.dtype)] * outs,
        compiler_params=params(),
        cost_estimate=cost(0, 2 * total * source[0].size * 2),
        name="pick",
    )(table, source)


def place_kernel(origin, position, *refs, samples):
    sources, out_ref, held, sem_in, sem_out = refs[:-4], refs[-4], refs[-3], refs[-2], refs[-1]
    for j in range(samples):
        for o, source in enumerate(sources):

            @pl.when(origin[j] == o)
            def _():
                pltpu.make_async_copy(source.at[position[j]], held.at[j], sem_in.at[j]).start()

    writes = []
    for j in range(samples):
        pltpu.make_async_copy(sources[0].at[0], held.at[j], sem_in.at[j]).wait()
        writes.append(pltpu.make_async_copy(held.at[j], out_ref.at[j], sem_out.at[j]))
        writes[-1].start()
    for copy in writes:
        copy.wait()


def place(origin, position, sources):
    samples = origin.shape[0]
    shape = sources[0].shape[1:]
    return pl.pallas_call(
        functools.partial(place_kernel, samples=samples),
        grid_spec=pltpu.PrefetchScalarGridSpec(
            num_scalar_prefetch=2,
            grid=(1,),
            in_specs=[pl.BlockSpec(memory_space=pl.ANY)] * len(sources),
            out_specs=pl.BlockSpec(memory_space=pl.ANY),
            scratch_shapes=[
                pltpu.VMEM((samples,) + shape, sources[0].dtype),
                pltpu.SemaphoreType.DMA((samples,)),
                pltpu.SemaphoreType.DMA((samples,)),
            ],
        ),
        out_shape=jax.ShapeDtypeStruct((samples,) + shape, sources[0].dtype),
        compiler_params=params(),
        cost_estimate=cost(0, 4 * samples * shape[0] * shape[1]),
        name="place",
    )(origin, position, *sources)


def routes(destination, samples, fsdp):
    group = lax.axis_index("dp")
    me = lax.axis_index("fsdp")
    capacity = 3 * samples // (2 * fsdp)
    span = fsdp * samples
    slots = lax.dynamic_slice_in_dim(destination, group * span, span).reshape(fsdp, samples)
    target = slots // samples - group * fsdp
    slot = slots % samples
    order = jnp.arange(samples, dtype=jnp.int32)
    before = order[None, :] < order[:, None]
    rank = jnp.sum(
        jnp.where((target[:, :, None] == target[:, None, :]) & before[None], 1, 0), axis=2
    ).astype(jnp.int32)
    offsets = (me + jnp.arange(1, fsdp, dtype=jnp.int32)) % fsdp
    places = jnp.arange(capacity, dtype=jnp.int32)

    def mine(table):
        return lax.dynamic_index_in_dim(table, me, 0, keepdims=False)

    my_target, my_slot, my_rank = mine(target), mine(slot), mine(rank)
    hit = (my_target[None, None, :] == offsets[:, None, None]) & (
        my_rank[None, None, :] == places[None, :, None]
    )
    out_pick = jnp.sum(jnp.where(hit, order[None, None, :], 0), axis=2).astype(jnp.int32)
    lands = (target == me)[:, :, None] & (slot[:, :, None] == order[None, None, :])
    origin_table = ((me - jnp.arange(fsdp, dtype=jnp.int32)) % fsdp)[:, None, None]
    in_origin = jnp.sum(jnp.where(lands, origin_table, 0), axis=(0, 1)).astype(jnp.int32)
    entry = jnp.where(origin_table == 0, order[None, :, None], rank[:, :, None])
    in_place = jnp.sum(jnp.where(lands, entry, 0), axis=(0, 1)).astype(jnp.int32)
    their_target = jnp.take(target, offsets, axis=0)
    their_slot = jnp.take(slot, offsets, axis=0)
    their_rank = jnp.take(rank, offsets, axis=0)
    hit = (their_target[:, None, :] == me) & (their_rank[:, None, :] == places[None, :, None])
    back_pick = jnp.sum(jnp.where(hit, their_slot[:, None, :], 0), axis=2).astype(jnp.int32)
    back_origin = ((me - my_target) % fsdp).astype(jnp.int32)
    back_place = jnp.where(back_origin == 0, my_slot, my_rank).astype(jnp.int32)
    return capacity, out_pick, in_origin, in_place, back_pick, back_origin, back_place


class Grid:
    def __init__(self, dp, fsdp, shard):
        self.size = {"c": 2, "x": fsdp // 2}
        self.size["z"] = 4 if dp % 4 == 0 else dp
        self.size["y"] = dp // self.size["z"]
        d, f = lax.axis_index("dp"), lax.axis_index("fsdp")
        self.at = {"z": d // self.size["y"], "y": d % self.size["y"], "x": f // 2, "c": f % 2}
        self.plain = 2 * shard % 16 != 0 or self.size["x"] != 2 or self.size["y"] != 2
        self.here = jnp.stack([self.at[a] for a in "zyxc"]).astype(jnp.int32)

    def number(self, at):
        dp = at["z"] * self.size["y"] + at["y"]
        return (dp * self.size["x"] + at["x"]) * 2 + at["c"]

    def send(self, array, axis, offset):
        pairs = []
        spans = [range(self.size[a]) for a in "zyxc"]
        for place in itertools.product(*spans):
            here = dict(zip("zyxc", place))
            there = dict(here)
            there[axis] = (here[axis] + offset) % self.size[axis]
            pairs.append((self.number(here), self.number(there)))
        return lax.ppermute(array, AXES, pairs)

    def spread(self, array, axis):
        return [array] + [self.send(array, axis, o) for o in range(1, self.size[axis])]

    def ordered(self, parts, axis):
        n, at = self.size[axis], self.at[axis]
        out = []
        for j in range(n):
            pick = parts[0]
            for o in range(1, n):
                pick = jnp.where((at - o) % n == j, parts[o], pick)
            out.append(pick)
        return jnp.concatenate(out, axis=0)


def tie(*values):
    return lax.optimization_barrier(values)


class Gather:
    def __init__(self, grid, mine, other, split):
        self.grid, self.mine, self.other, self.split = grid, mine, other, split
        self.rows, self.columns = 2 * mine.shape[0], 2 * mine.shape[1]
        self.plain = grid.plain
        self.parts = []

    def along_z(self):
        grid = self.grid
        if self.plain:
            shard = jnp.concatenate([self.mine, self.other], axis=1)
            self.parts = [lax.all_gather(shard, AXES, axis=0, tiled=True)]
            return
        chip = grid.ordered([self.mine, grid.send(self.other, "c", 1)], "c")
        self.stack = jnp.concatenate(grid.spread(chip, "z"), axis=0)

    def along_xy(self):
        if not self.plain:
            self.from_x = self.grid.send(self.stack, "x", 1)
            self.from_y = self.grid.send(self.stack, "y", 1)
            self.near = self.grid.send(self.stack, "c", 1)

    def diagonal(self):
        if not self.plain:
            self.one = self.grid.send(self.from_x[:, : self.split], "y", 1)
            self.two = self.grid.send(self.from_y[:, self.split :], "x", 1)
            self.near_x = self.grid.send(self.from_x, "c", 1)
            self.near_y = self.grid.send(self.from_y, "c", 1)

    def finish(self):
        if not self.plain:
            own = [self.stack, self.from_x, self.from_y, self.one, self.two]
            far = [self.near, self.near_x, self.near_y]
            far += [self.grid.send(self.one, "c", 1), self.grid.send(self.two, "c", 1)]
            self.parts = own + far

    def plan(self):
        if self.plain:
            return [(0, 0, self.parts[0].shape[0], self.columns, None, 0, 0, 0, 0)]
        copies = []
        steps = [(0, 0, 0), (0, 1, 0), (1, 0, 0), (1, 1, 0), (1, 1, self.split)]
        for n, part in enumerate(self.parts):
            dy, dx, begin = steps[n % 5]
            for k in range(self.grid.size["z"]):
                copies.append(
                    (n, k * self.rows, self.rows, part.shape[1], dy, dx, k, n // 5, begin)
                )
        return copies


def fetch(copies, here, size, parts, w_ref, sem):
    z, y, x, c = (here[n] for n in range(4))
    half = w_ref.shape[1] // 2
    started = []
    for n, (part, first, rows, columns, dy, dx, dz, far, begin) in enumerate(copies):
        if dy is None:
            to = w_ref
        else:
            line = (lax.rem(z + size["z"] - dz, size["z"]) * size["y"]) + lax.rem(y + dy, size["y"])
            row = (line * size["x"] + lax.rem(x + dx, size["x"])) * rows
            core = 1 - c if far else c
            to = w_ref.at[
                pl.ds(pl.multiple_of(row, 16), rows),
                pl.ds(pl.multiple_of(core * half + begin, 128), columns),
            ]
        started.append(
            pltpu.make_async_copy(parts[part].at[pl.ds(first, rows)], to, sem.at[n])
        )
    for copy in started:
        copy.start()
    for copy in started:
        copy.wait()


def line_rows(here, size, rows):
    z, y = here[0], here[1]
    return [
        pl.multiple_of(
            (lax.rem(z + oz, size["z"]) * size["y"] + lax.rem(y + oy, size["y"])) * rows, 16
        )
        for oy in range(size["y"])
        for oz in range(size["z"])
    ]


def tie_lists(*lists):
    flat = tie(*[value for part in lists for value in part])
    out = []
    for part in lists:
        out.append(list(flat[: len(part)]))
        flat = flat[len(part) :]
    return out


def add(*parts):
    total = parts[0].astype(F32)
    for part in parts[1:]:
        total = total + part.astype(F32)
    return total


class Scatter:
    def __init__(self, grid, mine, split):
        self.grid, self.mine, self.split = grid, mine, split

    def core(self, others):
        self.got = [self.grid.send(other, "c", 1) for other in others]

    def line(self, array, offset, axis):
        at = (self.grid.at["x"] + offset) % self.grid.size["x"]
        return lax.dynamic_index_in_dim(array, at, axis, keepdims=False)

    def begin(self):
        grid = self.grid
        total = jnp.concatenate([add(m, g) for m, g in zip(self.mine, self.got)], axis=1)
        sizes = [grid.size[a] for a in "yzx"]
        chip = total.shape[0] // math.prod(sizes)
        total = total.reshape(*sizes, chip, total.shape[1])
        left, right = total[..., : self.split], total[..., self.split :]
        self.keep_one, self.keep_two = left[0], self.line(right, 0, 2)
        self.out_one = [left[o].astype(BF16) for o in range(1, grid.size["y"])]
        self.out_two = [self.line(right, o, 2).astype(BF16) for o in range(1, grid.size["x"])]

    def first(self):
        grid = self.grid
        self.in_one = [grid.send(p, "y", o + 1) for o, p in enumerate(self.out_one)]
        self.in_two = [grid.send(p, "x", o + 1) for o, p in enumerate(self.out_two)]

    def second(self):
        grid = self.grid
        one, two = add(self.keep_one, *self.in_one), add(self.keep_two, *self.in_two)
        self.keep_one, self.keep_two = self.line(one, 0, 1), two[0]
        self.in_one = [
            grid.send(self.line(one, o, 1).astype(BF16), "x", o) for o in range(1, grid.size["x"])
        ]
        self.in_two = [grid.send(two[o].astype(BF16), "y", o) for o in range(1, grid.size["y"])]

    def third(self):
        grid = self.grid
        total = jnp.concatenate(
            [add(self.keep_one, *self.in_one), add(self.keep_two, *self.in_two)], axis=2
        )
        self.keep = total[0]
        self.came = [grid.send(total[o].astype(BF16), "z", o) for o in range(1, grid.size["z"])]

    def last(self):
        grid = self.grid
        total = add(self.keep, *self.came)
        c = grid.at["c"]
        share = total.shape[0] // 2
        mine = lax.dynamic_slice_in_dim(total, c * share, share, 0)
        far = lax.dynamic_slice_in_dim(total, (1 - c) * share, share, 0).astype(BF16)
        far = grid.send(far, "c", 1).astype(F32)
        return jnp.concatenate([jnp.where(c == 0, mine, far), jnp.where(c == 0, far, mine)], axis=1)


def exchange(part, fsdp, offset):
    return lax.ppermute(part, "fsdp", [(m, (m + offset) % fsdp) for m in range(fsdp)])


def body(
    tokens,
    input_weight,
    query_bias,
    value_bias,
    output_weight,
    output_bias,
    first_gain,
    first_shift,
    up_weight,
    up_bias,
    down_weight,
    down_bias,
    second_gain,
    second_shift,
    student_weight,
    student_bias,
    pool_query,
    pool_weight,
    pool_bias,
    class_weight,
    class_bias,
    lengths,
    exit_layer,
    destination,
    repacked_grad,
    logits_grad,
):
    samples, seq, width = tokens.shape
    count = samples * seq
    devices = lax.axis_size("dp") * lax.axis_size("fsdp")
    fsdp = lax.axis_size("fsdp")
    ff = up_weight.shape[1]
    stu = student_weight.shape[1]
    classes = class_weight.shape[1]
    block = min(count, 256)
    wide_block = min(count, 512)
    shard = width // devices
    grid = Grid(lax.axis_size("dp"), fsdp, shard)
    vectors = (
        query_bias,
        value_bias,
        output_bias,
        first_gain,
        first_shift,
        down_bias,
        second_gain,
        second_shift,
    )
    cut = 3 * width // 2
    here = grid.here
    if grid.plain:
        here = here * jnp.array([1, 1, 1, 0], jnp.int32)
    in_mine, in_other, ff_mine, ff_other = pack(
        here,
        input_weight,
        student_weight,
        output_weight,
        up_weight,
        up_bias,
        pool_weight,
        class_weight,
        logits_grad,
        (student_bias, pool_query, pool_bias),
        vectors,
    )
    capacity, out_pick, in_origin, in_place, back_pick, back_origin, back_place = routes(
        destination, samples, fsdp
    )
    alive = (exit_layer > LAYER).astype(jnp.int32)

    wd = lax.all_gather(down_weight, AXES, axis=0, tiled=True)
    g_in = Gather(grid, in_mine, in_other, (cut + 128) // 256 * 128)
    g_in.along_z()
    outgoing = pick(back_pick, repacked_grad, fsdp - 1, capacity)
    returned = [exchange(outgoing[0], fsdp, 1)]
    if not grid.plain:
        g_in.stack, ff_mine, returned[0] = tie(g_in.stack, ff_mine, returned[0])
    g_ff = Gather(grid, ff_mine, ff_other, (ff + width) // 512 * 128 + 128)
    g_in.along_xy()
    g_in.diagonal()
    g_ff.along_z()
    g_in.finish()
    if not grid.plain:
        *g_in.parts, g_ff.stack = tie(*g_in.parts, g_ff.stack)
    g_ff.along_xy()
    rows = tokens.reshape(count, width)
    qkv, prob, mixed, turned, vec, sv, pw, cw, ubm, cb, ws = attend(
        lengths, g_in, rows, seq, wide_block, stu, classes, devices, ff // devices
    )
    rest = list(outgoing[1:])
    if not grid.plain:
        mixed, g_ff.from_x, g_ff.from_y, g_ff.near, *rest = tie(
            mixed, g_ff.from_x, g_ff.from_y, g_ff.near, *rest
        )
    g_ff.diagonal()
    returned += [exchange(part, fsdp, o + 2) for o, part in enumerate(rest)]
    g_ff.finish()
    ub = jnp.broadcast_to(ubm[:, : ff // devices].reshape(1, ff), (8, ff))
    normed, factor, low, act, slope = up_part(g_ff, mixed, rows, vec, ub, block)
    act, *returned = tie(act, *returned)
    second_cot = place(back_origin, back_place, [repacked_grad] + returned)
    steps = count // wide_block
    lg = jnp.pad(
        logits_grad.reshape(steps, samples // steps, classes),
        ((0, 0), (0, 8 - samples // steps), (0, 128 - classes)),
    ).reshape(steps * 8, 128)
    second, sum_two, dcot, logits, vgrad_two, sgrad, wsgrad, pwgrad, cwgrad, wd_grad = down_part(
        lengths,
        alive,
        act,
        normed,
        second_cot.reshape(count, width),
        lg,
        wd,
        vec,
        ws,
        sv,
        pw,
        cw,
        seq,
        wide_block,
        ff // 6,
    )
    student_logits = logits.reshape(steps, 8, 128)[:, : samples // steps, :classes].reshape(
        samples, classes
    ) + class_bias.astype(F32)
    second = second.reshape(samples, seq, width)
    wd_share = lax.psum_scatter(wd_grad, AXES, scatter_dimension=0, tiled=True)
    leaving = pick(out_pick, second, fsdp - 1, capacity)
    dcot, *leaving = tie(dcot, *leaving)
    arrived = [exchange(part, fsdp, o + 1) for o, part in enumerate(leaving)]
    one_cot, mcot, vgrad_one, ugrad, wu_other, wu_mine, wo_other, wo_mine = up_back(
        g_ff, dcot, slope, sum_two, normed, factor, low, mixed, wd, vec, block, ff // 6
    )
    mcot, wu_other, wo_other, *arrived = tie(mcot, wu_other, wo_other, *arrived)
    s_ff = Scatter(grid, [wo_mine, wu_mine], (ff + width) // 512 * 128 + 128)
    s_ff.core([wo_other, wu_other])
    s_ff.begin()
    mcot, *out = tie(mcot, *s_ff.out_one, *s_ff.out_two)
    s_ff.out_one, s_ff.out_two = out[: len(s_ff.out_one)], out[len(s_ff.out_one) :]
    s_ff.first()
    pcot, vgrad_in = attend_back(mcot, qkv, prob, seq, wide_block)
    (pcot, vgrad_in), s_ff.in_one, s_ff.in_two = tie_lists(
        (pcot, vgrad_in), s_ff.in_one, s_ff.in_two
    )
    s_ff.second()
    ugm = jnp.pad(ugrad[0].reshape(devices, -1), ((0, 0), (0, 128 - ff // devices)))
    small_other, small_mine = small_pieces(
        grid,
        (vgrad_in, vgrad_one, vgrad_two, ugm, sgrad, wsgrad, pwgrad, cwgrad),
        classes,
        devices,
    )
    wi_other, wi_mine = input_grad(grid.here, turned, pcot, width // 2)
    (wi_other, small_other, wd_share), s_ff.in_one, s_ff.in_two, arrived = tie_lists(
        (wi_other, small_other, wd_share), s_ff.in_one, s_ff.in_two, arrived
    )
    s_in = Scatter(grid, [wi_mine, small_mine], (cut + 128) // 2)
    s_in.core([wi_other, small_other])
    s_ff.third()
    repacked = place(in_origin, in_place, [second] + arrived)
    s_in.begin()
    (pcot, repacked), s_in.out_one, s_in.out_two = tie_lists(
        (pcot, repacked), s_in.out_one, s_in.out_two
    )
    s_in.first()
    tokens_grad = token_part(g_in, pcot, one_cot, wide_block)
    (tokens_grad,), s_in.in_one, s_in.in_two, s_ff.came = tie_lists(
        (tokens_grad,), s_in.in_one, s_in.in_two, s_ff.came
    )
    tokens_grad = tokens_grad.reshape(samples, seq, width)
    s_in.second()
    ff_share = s_ff.last()
    s_in.third()
    in_share = s_in.last()
    class_bias_grad = cb[0, :classes]

    half = cut + 128
    input_share = jnp.concatenate([in_share[:, :cut], in_share[:, half : half + cut]], axis=1)
    flat = lambda size: jax.ShapeDtypeStruct((1, size), F32)
    group = stu // devices
    outs = pl.pallas_call(
        functools.partial(finish_kernel, group=group, classes=classes, up_size=ff // devices),
        out_shape=[flat(shard)] * 8
        + [
            jax.ShapeDtypeStruct((group, 64), F32),
            jax.ShapeDtypeStruct((group, 64), F32),
            jax.ShapeDtypeStruct((group, classes), F32),
        ]
        + [flat(group)] * 3
        + [flat(ff // devices)],
        name="finish",
    )(in_share[:, half + cut :])
    qb, vb, ob, g1, s1, db, g2, s2 = (o.reshape(-1) for o in outs[:8])
    ff_half = (ff + width) // 2
    wo_share, wu_share = (
        jnp.concatenate([ff_share[:, b:e], ff_share[:, ff_half + b : ff_half + e]], axis=1)
        for b, e in ((0, width // 2), (width // 2, ff_half))
    )
    return (
        repacked,
        student_logits,
        tokens_grad,
        input_share,
        qb,
        vb,
        wo_share,
        ob,
        g1,
        s1,
        wu_share,
        outs[14].reshape(-1),
        wd_share.astype(F32),
        db,
        g2,
        s2,
        in_share[:, cut:half],
        outs[11].reshape(-1),
        outs[12].reshape(-1),
        jnp.concatenate(outs[8:10], axis=1),
        outs[13].reshape(-1),
        outs[10],
        class_bias_grad,
    )


def solution(mesh):
    both = P(AXES)
    matrix = P(AXES, None)
    cube = P(AXES, None, None)
    return jax.shard_map(
        body,
        mesh=mesh,
        in_specs=(
            cube,
            matrix,
            both,
            both,
            matrix,
            both,
            both,
            both,
            matrix,
            both,
            matrix,
            both,
            both,
            both,
            matrix,
            both,
            both,
            matrix,
            both,
            matrix,
            P(),
            both,
            both,
            P(),
            cube,
            matrix,
        ),
        out_specs=(
            cube,
            matrix,
            cube,
            matrix,
            both,
            both,
            matrix,
            both,
            both,
            both,
            matrix,
            both,
            matrix,
            both,
            both,
            both,
            matrix,
            both,
            both,
            matrix,
            both,
            matrix,
            P(),
        ),
        check_vma=False,
    )
```

```python
import functools
import itertools
import math

import jax
import jax.numpy as jnp
from jax import lax
from jax.experimental import pallas as pl
from jax.experimental.pallas import tpu as pltpu
from jax.sharding import PartitionSpec as P

HEADS = 12
HEAD_DIM = 64
STU_HEADS = 2
LAYER = 6
EPS = 1e-06
MASKED = -1e30
AXES = ("dp", "fsdp")
F32 = jnp.float32
BF16 = jnp.bfloat16
VMEM_LIMIT = 60 * 1024 * 1024

QB, VB, OB, G1, S1, DB, G2, S2 = range(8)


def dot(left, right):
    return jnp.dot(left, right, preferred_element_type=F32)


def dot_nt(left, right):
    return lax.dot_general(left, right, (((1,), (1,)), ((), ())), preferred_element_type=F32)


def dot_tn(left, right):
    return lax.dot_general(left, right, (((0,), (0,)), ((), ())), preferred_element_type=F32)


def params(limit=VMEM_LIMIT):
    return pltpu.CompilerParams(vmem_limit_bytes=limit, dimension_semantics=("arbitrary",))


def cost(flops, nbytes):
    return pl.CostEstimate(
        flops=int(0.3 * flops), bytes_accessed=int(0.3 * nbytes), transcendentals=0
    )


def whole(shape, index=None):
    index = index or (0,) * len(shape)
    return pl.BlockSpec(shape, lambda i, *_: index, pipeline_mode=pl.Buffered(1))


def rows_spec(rows, width):
    return pl.BlockSpec((rows, width), lambda i, *_: (i, 0))


def kept(shape):
    return pl.BlockSpec(shape, lambda i, *_: (0,) * len(shape))


def layer_norm(total):
    mean = jnp.mean(total, axis=-1, keepdims=True)
    centered = total - mean
    factor = lax.rsqrt(jnp.mean(centered * centered, axis=-1, keepdims=True) + EPS)
    return centered * factor, factor


def layer_norm_back(cot, gain, normed, factor):
    scaled = cot * gain
    inner = (
        scaled
        - jnp.mean(scaled, axis=-1, keepdims=True)
        - normed * jnp.mean(scaled * normed, axis=-1, keepdims=True)
    )
    return factor * inner


def gelu_parts(up):
    phi = 0.5 + 0.5 * lax.erf(up * (1.0 / math.sqrt(2.0)))
    bell = jnp.exp(up * up * -0.5) * (1.0 / math.sqrt(2.0 * math.pi))
    return up * phi, phi + up * bell


def column_sum(matrix):
    return jnp.sum(matrix, axis=0, keepdims=True)


def stack_rows(rows, count):
    width = rows[0].shape[1]
    pad = count - len(rows)
    if pad:
        rows = list(rows) + [jnp.zeros((pad, width), F32)]
    return jnp.concatenate(rows, axis=0)


def one_hot_rows(count, width, group, stride, skip):
    row = lax.broadcasted_iota(jnp.int32, (count, width), 0)
    column = lax.broadcasted_iota(jnp.int32, (count, width), 1)
    shift = group.bit_length() - 1
    wanted = (row >> shift) * stride + skip + (row & (group - 1))
    return jnp.where(column == wanted, 1.0, 0.0).astype(BF16)


def turn_lanes(matrix):
    return pltpu.roll(matrix, 64, 1)


def read_small(block, vec_ref, sv_ref, pw_ref, cw_ref, ub_ref, cb_ref, stu, classes, devices, up_size):
    width = block.shape[0]
    shard = width // devices
    group = stu // devices
    lane = lax.broadcasted_iota(jnp.int32, (stu, 128), 1)
    left, right, rest = (
        dot(one_hot_rows(stu, width, group, shard, n * group), block) for n in range(3)
    )
    pw_ref[...] = jnp.where(lane < 64, turn_lanes(left), right).astype(BF16)
    rest = turn_lanes(rest)
    cw_ref[...] = jnp.where(lane < classes, rest, 0.0).astype(BF16)
    sv_ref[...] = rest.T[classes : classes + 8]
    low, high = (
        dot(one_hot_rows(devices, width, 1, shard, 3 * group + n), block) for n in range(2)
    )
    lane = lax.broadcasted_iota(jnp.int32, (devices, 128), 1)
    ub_ref[...] = jnp.where(lane < 64, turn_lanes(low), high)
    vec_ref[...] = block.astype(F32).T[:8]
    skip = 3 * group + pl.cdiv(up_size, 64)
    high, low = (dot(one_hot_rows(devices, width, 1, shard, skip + n), block) for n in range(2))
    cb_ref[...] = jnp.broadcast_to(turn_lanes(column_sum(high + low)), cb_ref.shape)


def pack_kernel(here, *refs, classes, group):
    wi_ref, ws_ref, wo_ref, wu_ref, ub_ref, pw_ref, cw_ref, lg_ref = refs[:8]
    columns, vectors = refs[8:11], refs[11:19]
    in_mine, in_other, ff_mine, ff_other, held = refs[19:]
    shard = wi_ref.shape[0]
    held[...] = jnp.zeros_like(held)
    for n, vector in enumerate(vectors):
        held[n : n + 1, :shard] = vector[...].astype(F32)
    left = held[:128].T[:shard]
    held[:8] = jnp.zeros((8, 128), F32)
    for n, column in enumerate(columns):
        held[classes + n : classes + n + 1, :group] = column[...].astype(F32)
    held[128 : 128 + group, :classes] = cw_ref[...].astype(F32)
    rest = held[128 : 128 + group] + held[:128].T[:group]
    up_size = ub_ref.shape[1]
    held[136:137, :up_size] = ub_ref[...].astype(F32)
    up = held[136:137]
    total = column_sum(lg_ref[...].astype(F32))
    high = total.astype(BF16).astype(F32)
    held[144:145, :classes] = high
    held[145:146, :classes] = total - high
    pool = pw_ref[...].astype(F32)
    rows = [turn_lanes(pool), pool, turn_lanes(rest), turn_lanes(up)]
    if up_size > 64:
        rows.append(up)
    rows.append(turn_lanes(held[144:146]))
    spare = shard - sum(r.shape[0] for r in rows)
    if spare:
        rows.append(jnp.zeros((spare, 128), F32))
    lane = lax.broadcasted_iota(jnp.int32, (shard, 128), 1)
    small = jnp.where(lane < 64, left, jnp.concatenate(rows, axis=0)).astype(BF16)
    cut = wi_ref.shape[1] // 2
    width = wo_ref.shape[1]
    part = ff_mine.shape[1] - width
    for core, (a, b, c, d) in enumerate(
        ((in_mine, in_other, ff_mine, ff_other), (in_other, in_mine, ff_other, ff_mine))
    ):

        @pl.when(here[3] == core)
        def _():
            a[:, :cut] = wi_ref[:, :cut]
            a[:, cut:] = ws_ref[...]
            b[:, :cut] = wi_ref[:, cut:]
            b[:, cut:] = small
            c[:, :width] = wo_ref[...]
            c[:, width:] = wu_ref[:, :part]
            d[...] = wu_ref[:, part:]


def pack(here, wi, ws, wo, wu, ub, pw, cw, lg, columns, vectors):
    shard = wi.shape[0]
    group, classes = cw.shape
    flat = lambda v: v.reshape(1, -1)
    first = jax.ShapeDtypeStruct((shard, wi.shape[1] // 2 + 128), BF16)
    second = jax.ShapeDtypeStruct((shard, (wo.shape[1] + wu.shape[1]) // 2), BF16)
    args = (wi, ws, wo, wu, flat(ub), pw, cw, lg, *map(flat, columns), *map(flat, vectors))
    return pl.pallas_call(
        functools.partial(pack_kernel, classes=classes, group=group),
        grid_spec=pltpu.PrefetchScalarGridSpec(
            num_scalar_prefetch=1,
            grid=(1,),
            in_specs=[whole(a.shape) for a in args],
            out_specs=[kept(o.shape) for o in (first, first, second, second)],
            scratch_shapes=[pltpu.VMEM((152, 128), F32)],
        ),
        out_shape=[first, first, second, second],
        compiler_params=params(),
        cost_estimate=cost(1e6, 1e6),
        name="pack",
    )(here, *args)


def attend_kernel(lens, here, *refs, copies, size, seq, width, stu, classes, devices, up_size):
    x_ref = refs[0]
    pieces = refs[1:-14]
    qkv_ref, prob_ref, mixed_ref, turned_ref, vec_ref, sv_ref, pw_ref = refs[-14:-7]
    cw_ref, ub_ref, cb_ref, ws_ref, w_ref, held, sem = refs[-7:]
    step = pl.program_id(0)
    half = w_ref.shape[1] // 2
    cut = half - 128

    @pl.when(step == 0)
    def _():
        fetch(copies, here, size, pieces, w_ref, sem)
        ws_ref[...] = w_ref[:, cut:half]
        read_small(
            w_ref[:, half + cut :],
            vec_ref,
            sv_ref,
            pw_ref,
            cw_ref,
            ub_ref,
            cb_ref,
            stu,
            classes,
            devices,
            up_size,
        )

    rows = x_ref.shape[0]
    lines = line_rows(here, size, width // (size["y"] * size["z"]))
    turn_lines(x_ref[...], lines, held, turned_ref, slice(0, rows))
    x = x_ref[...]
    vec = vec_ref[...]
    query = dot(x, w_ref[:, :width]) + vec[QB : QB + 1]
    qkv_ref[:, :width] = query.astype(BF16)
    split = 2 * width - cut
    qkv_ref[:, width:cut] = dot(x, w_ref[:, width:cut]).astype(BF16)
    qkv_ref[:, cut : 2 * width] = dot(x, w_ref[:, half : half + split]).astype(BF16)
    value = dot(x, w_ref[:, half + split : half + cut]) + vec[VB : VB + 1]
    qkv_ref[:, 2 * width :] = value.astype(BF16)
    lane = lax.broadcasted_iota(jnp.int32, (seq, 128), 1)
    first_head = lane < HEAD_DIM
    place = lax.broadcasted_iota(jnp.int32, (seq, 2 * seq), 0)
    scale = jnp.asarray(1.0 / math.sqrt(HEAD_DIM), BF16)
    for s in range(rows // seq):
        valid = place < lens[step * (rows // seq) + s]
        at = slice(s * seq, (s + 1) * seq)
        for pair in range(width // 128):
            low = pair * 128
            q = qkv_ref[at, low : low + 128] * scale
            k = qkv_ref[at, width + low : width + low + 128]
            v = qkv_ref[at, 2 * width + low : 2 * width + low + 128]
            zero = jnp.zeros_like(q)
            both = jnp.concatenate(
                [jnp.where(first_head, q, zero), jnp.where(first_head, zero, q)], axis=0
            )
            scores = jnp.where(valid, dot_nt(k, both), MASKED)
            raised = jnp.exp(scores - jnp.max(scores, axis=0, keepdims=True))
            share = raised * (1.0 / jnp.sum(raised, axis=0, keepdims=True))
            share = share.astype(BF16)
            prob_ref[s, pair] = share
            out = dot_tn(share, v)
            mixed_ref[at, low : low + 128] = jnp.where(first_head, out[:seq], out[seq:]).astype(BF16)


def attend(lens, gather, rows, seq, block, stu, classes, devices, up_size):
    copies, here, size = gather.plan(), gather.grid.here, gather.grid.size
    pieces = gather.parts
    count, width = rows.shape
    pairs = width // 128
    samples = block // seq
    columns = gather.columns
    small = [
        jax.ShapeDtypeStruct((8, width), F32),
        jax.ShapeDtypeStruct((8, stu), F32),
        jax.ShapeDtypeStruct((stu, stu), BF16),
        jax.ShapeDtypeStruct((stu, 128), BF16),
        jax.ShapeDtypeStruct((devices, 128), F32),
        jax.ShapeDtypeStruct((8, 128), F32),
        jax.ShapeDtypeStruct((width, stu), BF16),
    ]
    return pl.pallas_call(
        functools.partial(
            attend_kernel,
            copies=copies,
            size=size,
            seq=seq,
            width=width,
            stu=stu,
            classes=classes,
            devices=devices,
            up_size=up_size,
        ),
        grid_spec=pltpu.PrefetchScalarGridSpec(
            num_scalar_prefetch=2,
            grid=(count // block,),
            in_specs=[rows_spec(block, width)] + [pl.BlockSpec(memory_space=pl.ANY)] * len(pieces),
            out_specs=[
                rows_spec(block, 3 * width),
                pl.BlockSpec((samples, pairs, seq, 2 * seq), lambda i, *_: (i, 0, 0, 0)),
                rows_spec(block, width),
                pl.BlockSpec((width, block), lambda i, *_: (0, i)),
            ]
            + [kept(s.shape) for s in small],
            scratch_shapes=[
                pltpu.VMEM((width, columns), BF16),
                pltpu.VMEM((width, block), BF16),
                pltpu.SemaphoreType.DMA((len(copies),)),
            ],
        ),
        out_shape=[
            jax.ShapeDtypeStruct((count, 3 * width), BF16),
            jax.ShapeDtypeStruct((count // seq, pairs, seq, 2 * seq), BF16),
            jax.ShapeDtypeStruct((count, width), BF16),
            jax.ShapeDtypeStruct((width, count), BF16),
        ]
        + small,
        compiler_params=params(),
        cost_estimate=cost(2 * count * width * 3 * width * 2, 30e6),
        name="attend",
    )(lens, here, rows, *pieces)


def first_rows(normed, vec):
    return normed.astype(F32) * vec[G1 : G1 + 1] + vec[S1 : S1 + 1]


def up_kernel(here, *refs, copies, size, chunk):
    mixed_ref, x_ref, vec_ref, ub_ref = refs[:4]
    pieces = refs[4:-6]
    norm_ref, factor_ref, act_ref, slope_ref, w_ref, sem = refs[-6:]
    width = x_ref.shape[1]

    @pl.when(pl.program_id(0) == 0)
    def _():
        fetch(copies, here, size, pieces, w_ref, sem)

    vec = vec_ref[...]
    total = dot(mixed_ref[...], w_ref[:, :width]) + vec[OB : OB + 1] + x_ref[...].astype(F32)
    normed, factor = layer_norm(total)
    norm_ref[...] = normed
    factor_ref[...] = jnp.broadcast_to(factor, factor_ref.shape)
    low = first_rows(norm_ref[...], vec).astype(BF16)
    for begin in range(0, act_ref.shape[1], chunk):
        at = slice(begin, begin + chunk)
        for first in range(0, low.shape[0], 128):
            rows = slice(first, first + 128)
            up = dot(low[rows], w_ref[:, width + begin : width + begin + chunk]) + ub_ref[0:1, at]
            act, slope = gelu_parts(up)
            act_ref[rows, at] = act.astype(BF16)
            slope_ref[rows, at] = slope.astype(BF16)


def up_part(gather, mixed, rows, vec, ub, block):
    copies, here, size = gather.plan(), gather.grid.here, gather.grid.size
    pieces = gather.parts
    count, width = rows.shape
    ff = gather.columns - width
    return pl.pallas_call(
        functools.partial(up_kernel, copies=copies, size=size, chunk=256),
        grid_spec=pltpu.PrefetchScalarGridSpec(
            num_scalar_prefetch=1,
            grid=(count // block,),
            in_specs=[
                rows_spec(block, width),
                rows_spec(block, width),
                whole(vec.shape),
                whole(ub.shape),
            ]
            + [pl.BlockSpec(memory_space=pl.ANY)] * len(pieces),
            out_specs=[
                rows_spec(block, width),
                rows_spec(block, 128),
                rows_spec(block, ff),
                rows_spec(block, ff),
            ],
            scratch_shapes=[
                pltpu.VMEM((width, gather.columns), BF16),
                pltpu.SemaphoreType.DMA((len(copies),)),
            ],
        ),
        out_shape=[
            jax.ShapeDtypeStruct((count, width), F32),
            jax.ShapeDtypeStruct((count, 128), F32),
            jax.ShapeDtypeStruct((count, ff), BF16),
            jax.ShapeDtypeStruct((count, ff), BF16),
        ],
        compiler_params=params(),
        cost_estimate=cost(2 * count * width * (ff + width) * 2, 50e6),
        name="up_part",
    )(here, mixed, rows, vec, ub, *pieces)


def down_kernel(lens, alive, *refs, seq, steps, tile):
    act_hbm, norm_ref, cot_ref, lg_ref, wd_ref, vec_ref, ws_ref, sv_ref, pw_ref, cw_ref = refs[:10]
    second_ref, dcot_ref, logits_ref, vgrad_ref, sgrad_ref = refs[10:15]
    wsgrad_ref, pwgrad_ref, cwgrad_ref, grad_ref, act_all, turned = refs[15:21]
    held, sem = refs[21:25], refs[25]
    step = pl.program_id(0)
    rows = norm_ref.shape[0]

    def load(n):
        at = pl.ds(pl.multiple_of(n * rows, rows), rows)
        return pltpu.make_async_copy(act_hbm.at[at], act_all.at[at], sem.at[n])

    @pl.when(step == 0)
    def _():
        load(0).start()
        for total_ref in (vgrad_ref, sgrad_ref, wsgrad_ref, pwgrad_ref, cwgrad_ref):
            total_ref[...] = jnp.zeros_like(total_ref)

    @pl.when(step + 1 < steps)
    def _():
        load(step + 1).start()

    @pl.when(step < steps)
    def _():
        load(step).wait()
        at = pl.ds(pl.multiple_of(step * rows, rows), rows)
        down_rows(
            lens,
            alive,
            (act_all.at[at], norm_ref, cot_ref, lg_ref, wd_ref, vec_ref, ws_ref, sv_ref, pw_ref, cw_ref),
            (second_ref, dcot_ref, logits_ref, vgrad_ref, sgrad_ref),
            (wsgrad_ref, pwgrad_ref, cwgrad_ref),
            held,
            seq,
        )
        turned[:, at] = dcot_ref[...].T

    @pl.when(step >= steps)
    def _():
        at = pl.ds(pl.multiple_of((step - steps) * tile, tile), tile)
        grad_ref[...] = dot(turned[...], act_all[:, at]).astype(BF16).T


SLICE = 32


def fold(matrix):
    return jnp.sum(matrix.reshape(matrix.shape[0] // 8, 8, matrix.shape[1]), axis=0)


def down_rows(lens, alive, ins, outs, sums, held, seq):
    act_ref, norm_ref, cot_ref, lg_ref, wd_ref, vec_ref, ws_ref, sv_ref, pw_ref, cw_ref = ins
    second_ref, dcot_ref, logits_ref, vgrad_ref, sgrad_ref = outs
    wsgrad_ref, pwgrad_ref, cwgrad_ref = sums
    wide_ref, back_ref, factor_ref, low_ref = held
    step = pl.program_id(0)
    rows = norm_ref.shape[0]
    samples = rows // seq
    vec = vec_ref[...]
    sv = sv_ref[...]
    stu = sv.shape[1]
    pool_width = stu // STU_HEADS
    pool_scale = 1.0 / math.sqrt(pool_width)

    wide_ref[...] = dot(act_ref[...], wd_ref[...])
    for begin in range(0, rows, SLICE):
        at = slice(begin, begin + SLICE)
        first = first_rows(norm_ref[at], vec)
        normed, factor = layer_norm(first + wide_ref[at] + vec[DB : DB + 1])
        wide_ref[at] = normed
        factor_ref[at] = jnp.broadcast_to(factor, (SLICE, 128))
        low_ref[at] = (normed * vec[G2 : G2 + 1] + vec[S2 : S2 + 1]).astype(BF16)
    second = low_ref[...]
    reduced = (dot(second, ws_ref[...]) + sv[0:1]).astype(BF16)
    head_of = lax.broadcasted_iota(jnp.int32, (stu, stu), 0) // pool_width
    same = head_of == lax.broadcasted_iota(jnp.int32, (stu, stu), 1) // pool_width
    pool_query = sv[1:2]
    query_table = jnp.where(same, jnp.broadcast_to(pool_query, (stu, stu)), 0.0).astype(BF16)
    scores = dot_nt(reduced, query_table) * pool_scale
    place = lax.broadcasted_iota(jnp.int32, (seq, stu), 0)
    cuts = [slice(s * seq, (s + 1) * seq) for s in range(samples)]
    wides = [reduced[at].astype(F32) for at in cuts]
    shares = [
        jnp.where(place < lens[step * samples + s], scores[at], MASKED) for s, at in enumerate(cuts)
    ]
    peaks = [jnp.max(part, axis=0, keepdims=True) for part in shares]
    shares = [jnp.exp(part - peak) for part, peak in zip(shares, peaks)]
    sums_of = [column_sum(part) for part in shares]
    shares = [part / total for part, total in zip(shares, sums_of)]
    pooled = stack_rows([column_sum(p * w) for p, w in zip(shares, wides)], 8).astype(BF16)
    squashed = jnp.tanh(dot(pooled, pw_ref[...]) + sv[2:3])
    squashed_low = squashed.astype(BF16)
    logits_ref[...] = dot(squashed_low, cw_ref[...])
    lg = lg_ref[...]
    cwgrad_ref[...] += dot_tn(squashed_low, lg)
    hidden_cot = (dot_nt(lg, cw_ref[...]) * (1.0 - squashed * squashed)).astype(BF16)
    pwgrad_ref[...] += dot_tn(pooled, hidden_cot)
    pooled_cot = dot_nt(hidden_cot, pw_ref[...]).astype(BF16).astype(F32)
    lines = [pooled_cot[s : s + 1] for s in range(samples)]
    tables = [
        jnp.where(same, jnp.broadcast_to(row, (stu, stu)), 0.0).astype(BF16) for row in lines
    ]
    share_cots = [dot_nt(reduced[at], table) for at, table in zip(cuts, tables)]
    inner = [column_sum(p * c) for p, c in zip(shares, share_cots)]
    score_cots = [p * (c - i) for p, c, i in zip(shares, share_cots, inner)]
    query_grad = sum(column_sum(c * w) for c, w in zip(score_cots, wides)) * pool_scale
    scaled_query = pool_query * pool_scale
    reduced_cot = jnp.concatenate(
        [
            (p * row + c * scaled_query).astype(BF16)
            for p, row, c in zip(shares, lines, score_cots)
        ],
        axis=0,
    )
    sgrad_ref[...] += stack_rows(
        [
            column_sum(reduced_cot.astype(F32)),
            query_grad,
            column_sum(hidden_cot.astype(F32)),
        ],
        8,
    )
    wsgrad_ref[...] += dot_tn(reduced_cot, second)
    back_ref[...] = dot_nt(reduced_cot, ws_ref[...])
    gain_sum = jnp.zeros((8, vec.shape[1]), F32)
    shift_sum, bias_sum = gain_sum, gain_sum
    for begin in range(0, rows, SLICE):
        at = slice(begin, begin + SLICE)
        live = alive[step * samples + begin // seq] > 0
        total = back_ref[at] + jnp.where(live, cot_ref[at].astype(F32), 0.0)
        low = low_ref[at]
        second_ref[at] = jnp.where(live, low, jnp.zeros_like(low))
        normed = wide_ref[at]
        sum_cot = layer_norm_back(total, vec[G2 : G2 + 1], normed, factor_ref[at, 0:1])
        dcot_ref[at] = sum_cot.astype(BF16)
        gain_sum += fold(total * normed)
        shift_sum += fold(total)
        bias_sum += fold(sum_cot)
    vgrad_ref[...] += stack_rows([column_sum(p) for p in (gain_sum, shift_sum, bias_sum)], 8)


def down_part(lens, alive, act, normed, cot, lg, wd, vec, ws, sv, pw, cw, seq, block, tile):
    count, ff = act.shape
    width = normed.shape[1]
    stu = ws.shape[1]
    steps = count // block

    def block_rows(height, columns):
        return pl.BlockSpec((height, columns), lambda i, *_: (jnp.minimum(i, steps - 1), 0))

    return pl.pallas_call(
        functools.partial(down_kernel, seq=seq, steps=steps, tile=tile),
        grid_spec=pltpu.PrefetchScalarGridSpec(
            num_scalar_prefetch=2,
            grid=(steps + ff // tile,),
            in_specs=[
                pl.BlockSpec(memory_space=pl.ANY),
                block_rows(block, width),
                block_rows(block, width),
                block_rows(8, 128),
                whole(wd.shape),
                whole(vec.shape),
                whole(ws.shape),
                whole(sv.shape),
                whole(pw.shape),
                whole(cw.shape),
            ],
            out_specs=[
                block_rows(block, width),
                block_rows(block, width),
                block_rows(8, 128),
                kept((8, width)),
                kept((8, stu)),
                kept((stu, width)),
                kept((stu, stu)),
                kept((stu, 128)),
                pl.BlockSpec((tile, width), lambda i, *_: (jnp.maximum(i - steps, 0), 0)),
            ],
            scratch_shapes=[
                pltpu.VMEM((count, ff), BF16),
                pltpu.VMEM((width, count), BF16),
                pltpu.VMEM((block, width), F32),
                pltpu.VMEM((block, width), F32),
                pltpu.VMEM((block, 128), F32),
                pltpu.VMEM((block, width), BF16),
                pltpu.SemaphoreType.DMA((steps,)),
            ],
        ),
        out_shape=[
            jax.ShapeDtypeStruct((count, width), BF16),
            jax.ShapeDtypeStruct((count, width), BF16),
            jax.ShapeDtypeStruct((steps * 8, 128), F32),
            jax.ShapeDtypeStruct((8, width), F32),
            jax.ShapeDtypeStruct((8, stu), F32),
            jax.ShapeDtypeStruct((stu, width), F32),
            jax.ShapeDtypeStruct((stu, stu), F32),
            jax.ShapeDtypeStruct((stu, 128), F32),
            jax.ShapeDtypeStruct((ff, width), BF16),
        ],
        compiler_params=params(),
        cost_estimate=cost(2 * count * width * ff * 4, 60e6),
        name="down_part",
    )(lens, alive, act, normed, cot, lg, wd, vec, ws, sv, pw, cw)


def turn_lines(block, lines, held, to, at):
    held[...] = block.T
    rows = to.shape[0] // len(lines)
    for n, line in enumerate(lines):
        to[n * rows : (n + 1) * rows, at] = held[pl.ds(line, rows)]


def up_back_kernel(here, *refs, copies, size, steps, chunk, tile):
    dcot_ref, slope_ref, norm_ref, factor_ref, mixed_ref, wd_ref, vec_ref = refs[:7]
    pieces = refs[7:-16]
    one_ref, mcot_ref, vgrad_ref, ugrad_ref = refs[-16:-12]
    up_other, up_mine, out_other, out_mine = refs[-12:-8]
    w_ref, ucot_all, acot_all, low_turned, mixed_turned, held, back_ref, sem = refs[-8:]
    step = pl.program_id(0)
    rows, width = dcot_ref.shape
    ff = slope_ref.shape[1]
    core = here[3]
    lines = line_rows(here, size, width // (size["y"] * size["z"]))

    @pl.when(step == 0)
    def _():
        fetch(copies, here, size, pieces, w_ref, sem)
        vgrad_ref[...] = jnp.zeros_like(vgrad_ref)
        ugrad_ref[...] = jnp.zeros_like(ugrad_ref)

    @pl.when(step < steps)
    def _():
        vec = vec_ref[...]
        at_rows = pl.ds(pl.multiple_of(step * rows, rows), rows)
        down_cot = dcot_ref[...]
        for begin in range(0, ff, chunk):
            at = slice(begin, begin + chunk)
            up_cot = dot_nt(down_cot, wd_ref[at, :]) * slope_ref[:, at].astype(F32)
            ugrad_ref[0:1, at] += column_sum(up_cot)
            ucot_all[at_rows, at] = up_cot.astype(BF16)
        turn_lines(first_rows(norm_ref[...], vec).astype(BF16), lines, held, low_turned, at_rows)
        turn_lines(mixed_ref[...], lines, held, mixed_turned, at_rows)
        back_ref[...] = dot_nt(ucot_all[at_rows, :], w_ref[:, width:])
        gain_sum = jnp.zeros((8, width), F32)
        shift_sum, bias_sum = gain_sum, gain_sum
        for begin in range(0, rows, SLICE):
            at = slice(begin, begin + SLICE)
            cot = dcot_ref[at].astype(F32) + back_ref[at]
            normed = norm_ref[at].astype(F32)
            one_cot = layer_norm_back(cot, vec[G1 : G1 + 1], normed, factor_ref[at, 0:1])
            one_ref[at] = one_cot.astype(BF16)
            gain_sum += fold(cot * normed)
            shift_sum += fold(cot)
            bias_sum += fold(one_cot)
        acot_all[at_rows, :] = one_ref[...]
        mcot_ref[...] = dot_nt(one_ref[...], w_ref[:, :width]).astype(BF16)
        vgrad_ref[...] += stack_rows([column_sum(p) for p in (gain_sum, shift_sum, bias_sum)], 8)

    per = ff // 2 // tile

    def up_tile(n, half):
        first = (half * per + n) * tile
        return dot(low_turned[...], ucot_all[:, pl.ds(pl.multiple_of(first, 128), tile)])

    def out_tile(half):
        first = half * (width // 2)
        return dot(mixed_turned[...], acot_all[:, pl.ds(pl.multiple_of(first, 128), width // 2)])

    @pl.when((step >= steps) & (step < steps + per))
    def _():
        up_other[...] = up_tile(step - steps, 1 - core).astype(BF16)

    @pl.when(step == steps + per)
    def _():
        out_other[...] = out_tile(1 - core).astype(BF16)
        out_mine[...] = out_tile(core).astype(BF16)

    @pl.when(step > steps + per)
    def _():
        up_mine[...] = up_tile(step - steps - per - 1, core).astype(BF16)


def up_back(gather, dcot, slope, normed, factor, mixed, wd, vec, block, tile):
    copies, here, size = gather.plan(), gather.grid.here, gather.grid.size
    pieces = gather.parts
    count, width = dcot.shape
    ff = slope.shape[1]
    steps = count // block
    per = ff // 2 // tile

    def block_rows(columns):
        return pl.BlockSpec((block, columns), lambda i, *_: (jnp.minimum(i, steps - 1), 0))

    def tiles(begin):
        return pl.BlockSpec(
            (width, tile), lambda i, *_: (0, jnp.clip(i - begin, 0, per - 1))
        )

    return pl.pallas_call(
        functools.partial(
            up_back_kernel, copies=copies, size=size, steps=steps, chunk=512, tile=tile
        ),
        grid_spec=pltpu.PrefetchScalarGridSpec(
            num_scalar_prefetch=1,
            grid=(steps + 2 * per + 1,),
            in_specs=[
                block_rows(width),
                block_rows(ff),
                block_rows(width),
                block_rows(128),
                block_rows(width),
                whole(wd.shape),
                whole(vec.shape),
            ]
            + [pl.BlockSpec(memory_space=pl.ANY)] * len(pieces),
            out_specs=[
                block_rows(width),
                block_rows(width),
                kept((8, width)),
                kept((8, ff)),
                tiles(steps),
                tiles(steps + per + 1),
                kept((width, width // 2)),
                kept((width, width // 2)),
            ],
            scratch_shapes=[
                pltpu.VMEM((width, gather.columns), BF16),
                pltpu.VMEM((count, ff), BF16),
                pltpu.VMEM((count, width), BF16),
                pltpu.VMEM((width, count), BF16),
                pltpu.VMEM((width, count), BF16),
                pltpu.VMEM((width, block), BF16),
                pltpu.VMEM((block, width), F32),
                pltpu.SemaphoreType.DMA((len(copies),)),
            ],
        ),
        out_shape=[
            jax.ShapeDtypeStruct((count, width), BF16),
            jax.ShapeDtypeStruct((count, width), BF16),
            jax.ShapeDtypeStruct((8, width), F32),
            jax.ShapeDtypeStruct((8, ff), F32),
            jax.ShapeDtypeStruct((width, ff // 2), BF16),
            jax.ShapeDtypeStruct((width, ff // 2), BF16),
            jax.ShapeDtypeStruct((width, width // 2), BF16),
            jax.ShapeDtypeStruct((width, width // 2), BF16),
        ],
        compiler_params=params(),
        cost_estimate=cost(2 * count * width * ff * 4, 60e6),
        name="up_back",
    )(here, dcot, slope, normed, factor, mixed, wd, vec, *pieces)


def attend_back_kernel(mcot_ref, qkv_ref, prob_ref, pcot_ref, vgrad_ref, *, seq, width):
    @pl.when(pl.program_id(0) == 0)
    def _():
        vgrad_ref[...] = jnp.zeros_like(vgrad_ref)

    attend_back_rows(mcot_ref, qkv_ref, prob_ref, pcot_ref, vgrad_ref, seq, width)


def input_grad_kernel(here, turned_ref, pcot_ref, other, mine, *, per):
    step = pl.program_id(0)
    grad = dot(turned_ref[...], pcot_ref[...]).astype(BF16)

    @pl.when(step < per)
    def _():
        other[...] = grad

    @pl.when(step >= per)
    def _():
        mine[...] = grad


def input_grad(here, turned, pcot, tile):
    width, count = turned.shape
    half = pcot.shape[1] // 2
    per = half // tile

    def columns(i, t):
        core = t[3]
        return (0, jnp.where(i < per, (1 - core) * per + i, core * per + i - per))

    return pl.pallas_call(
        functools.partial(input_grad_kernel, per=per),
        grid_spec=pltpu.PrefetchScalarGridSpec(
            num_scalar_prefetch=1,
            grid=(2 * per,),
            in_specs=[whole((width, count)), pl.BlockSpec((count, tile), columns)],
            out_specs=[
                pl.BlockSpec((width, tile), lambda i, t: (0, jnp.minimum(i, per - 1))),
                pl.BlockSpec((width, tile), lambda i, t: (0, jnp.maximum(i - per, 0))),
            ],
        ),
        out_shape=[jax.ShapeDtypeStruct((width, half), BF16)] * 2,
        compiler_params=params(),
        cost_estimate=cost(4 * count * width * half, 20e6),
        name="input_grad",
    )(here, turned, pcot)


def attend_back_rows(mcot_ref, qkv_ref, prob_ref, pcot_ref, vgrad_ref, seq, width):
    rows = mcot_ref.shape[0]
    lane = lax.broadcasted_iota(jnp.int32, (seq, 128), 1)
    first_head = lane < HEAD_DIM
    scale = 1.0 / math.sqrt(HEAD_DIM)

    def split(part):
        zero = jnp.zeros_like(part)
        return jnp.concatenate(
            [jnp.where(first_head, part, zero), jnp.where(first_head, zero, part)], axis=0
        )

    for s in range(rows // seq):
        at = slice(s * seq, (s + 1) * seq)
        lows = range(0, width, 128)
        cots = [split(mcot_ref[at, low : low + 128]) for low in lows]
        share_cots = [
            dot_nt(qkv_ref[at, 2 * width + low : 2 * width + low + 128], cot)
            for low, cot in zip(lows, cots)
        ]
        values = [dot(prob_ref[s, n], cot) for n, cot in enumerate(cots)]
        for low, value in zip(lows, values):
            pcot_ref[at, 2 * width + low : 2 * width + low + 128] = value.astype(BF16)
        score_cots = []
        for n, share_cot in enumerate(share_cots):
            wide = prob_ref[s, n].astype(F32)
            product = wide * share_cot
            score_cots.append((product - wide * column_sum(product)).astype(BF16))
        keys = [
            dot(score, split(qkv_ref[at, low : low + 128])) * scale
            for low, score in zip(lows, score_cots)
        ]
        queries = [
            dot_tn(score, qkv_ref[at, width + low : width + low + 128]) * scale
            for low, score in zip(lows, score_cots)
        ]
        for low, key, query in zip(lows, keys, queries):
            pcot_ref[at, width + low : width + low + 128] = key.astype(BF16)
            pcot_ref[at, low : low + 128] = jnp.where(
                first_head, query[:seq], query[seq:]
            ).astype(BF16)
    vgrad_ref[...] += stack_rows(
        [
            column_sum(pcot_ref[:, :width].astype(F32)),
            column_sum(pcot_ref[:, 2 * width :].astype(F32)),
        ],
        8,
    )


def attend_back(mcot, qkv, prob, seq, block):
    count, width = mcot.shape
    pairs = width // 128
    return pl.pallas_call(
        functools.partial(attend_back_kernel, seq=seq, width=width),
        grid_spec=pltpu.PrefetchScalarGridSpec(
            num_scalar_prefetch=0,
            grid=(count // block,),
            in_specs=[
                rows_spec(block, width),
                rows_spec(block, 3 * width),
                pl.BlockSpec((block // seq, pairs, seq, 2 * seq), lambda i: (i, 0, 0, 0)),
            ],
            out_specs=[rows_spec(block, 3 * width), kept((8, width))],
        ),
        out_shape=[
            jax.ShapeDtypeStruct((count, 3 * width), BF16),
            jax.ShapeDtypeStruct((8, width), F32),
        ],
        compiler_params=params(),
        cost_estimate=cost(2 * count * width * 3 * width * 2, 30e6),
        name="attend_back",
    )(mcot, qkv, prob)


def token_kernel(here, *refs, copies, size):
    pcot_ref, one_ref = refs[:2]
    pieces = refs[2:-3]
    out_ref, w_ref, sem = refs[-3:]

    @pl.when(pl.program_id(0) == 0)
    def _():
        fetch(copies, here, size, pieces, w_ref, sem)

    half = w_ref.shape[1] // 2
    cut = half - 128
    out_ref[...] = (
        one_ref[...].astype(F32)
        + dot_nt(pcot_ref[:, :cut], w_ref[:, :cut])
        + dot_nt(pcot_ref[:, cut:], w_ref[:, half : half + cut])
    )


def token_part(gather, pcot, one_cot, block):
    copies, here, size = gather.plan(), gather.grid.here, gather.grid.size
    pieces = gather.parts
    count, width = one_cot.shape
    return pl.pallas_call(
        functools.partial(token_kernel, copies=copies, size=size),
        grid_spec=pltpu.PrefetchScalarGridSpec(
            num_scalar_prefetch=1,
            grid=(count // block,),
            in_specs=[rows_spec(block, 3 * width), rows_spec(block, width)]
            + [pl.BlockSpec(memory_space=pl.ANY)] * len(pieces),
            out_specs=rows_spec(block, width),
            scratch_shapes=[
                pltpu.VMEM((width, gather.columns), BF16),
                pltpu.SemaphoreType.DMA((len(copies),)),
            ],
        ),
        out_shape=jax.ShapeDtypeStruct((count, width), F32),
        compiler_params=params(),
        cost_estimate=cost(2 * count * width * 3 * width, 25e6),
        name="token_part",
    )(here, pcot, one_cot, *pieces)


def small_kernel(here, *refs, size, classes, devices):
    vin_ref, vone_ref, vtwo_ref, ugrad_ref, sgrad_ref, wsgrad_ref, pwgrad_ref, cwgrad_ref = refs[:8]
    other_ref, mine_ref, halves = refs[8:]
    width = vin_ref.shape[1]
    stu = sgrad_ref.shape[1]
    shard = width // devices
    group = stu // devices
    halves[0] = wsgrad_ref[...].T
    vin, vone, vtwo = vin_ref[...], vone_ref[...], vtwo_ref[...]
    rows = [vin[0:1], vin[1:2], vone[2:3], vone[0:1], vone[1:2], vtwo[2:3], vtwo[0:1], vtwo[1:2]]
    block = stack_rows(rows, 128).T
    lane = lax.broadcasted_iota(jnp.int32, (stu, 128), 1)
    high = lane >= 64
    pwgrad = pwgrad_ref[...]
    spare = jnp.zeros((classes, stu), F32)
    rest = jnp.concatenate(
        [spare, sgrad_ref[0:3], jnp.zeros((128 - classes - 3, stu), F32)], axis=0
    ).T
    rest = rest + jnp.where(lane < classes, cwgrad_ref[...], 0.0)
    for n, part in enumerate((turn_lanes(pwgrad), pwgrad, turn_lanes(rest))):
        part = jnp.where(high, part, 0.0).astype(BF16)
        block = block + dot_tn(one_hot_rows(stu, width, group, shard, n * group), part)
    ugrad = ugrad_ref[...]
    high = lax.broadcasted_iota(jnp.int32, ugrad.shape, 1) >= 64
    for n, part in enumerate((turn_lanes(ugrad), ugrad)):
        part = jnp.where(high, part, 0.0).astype(BF16)
        block = block + dot_tn(one_hot_rows(devices, width, 1, shard, 3 * group + n), part)
    halves[1] = block
    core = here[3]
    rows = width // (size["y"] * size["z"])
    for n, line in enumerate(line_rows(here, size, rows)):
        at = pl.ds(line, rows)
        other_ref[n * rows : (n + 1) * rows] = halves[1 - core, at].astype(BF16)
        mine_ref[n * rows : (n + 1) * rows] = halves[core, at].astype(BF16)


def small_pieces(grid, grads, classes, devices):
    width = grads[0].shape[1]
    return pl.pallas_call(
        functools.partial(small_kernel, size=grid.size, classes=classes, devices=devices),
        grid_spec=pltpu.PrefetchScalarGridSpec(
            num_scalar_prefetch=1,
            grid=(1,),
            in_specs=[whole(g.shape) for g in grads],
            out_specs=[kept((width, 128))] * 2,
            scratch_shapes=[pltpu.VMEM((2, width, 128), F32)],
        ),
        out_shape=[jax.ShapeDtypeStruct((width, 128), BF16)] * 2,
        compiler_params=params(),
        cost_estimate=cost(1e8, 2e6),
        name="small_pieces",
    )(grid.here, *grads)


def finish_kernel(block_ref, *outs, group, classes, up_size):
    block = block_ref[...]
    shard = block.shape[0]
    columns = jnp.concatenate([block, jnp.zeros((128 - shard, 128), F32)], axis=0).T
    for n in range(8):
        outs[n][...] = columns[n : n + 1, :shard]
    outs[8][...] = block[:group, 64:]
    outs[9][...] = block[group : 2 * group, 64:]
    outs[10][...] = block[2 * group : 3 * group, 64 : 64 + classes]
    for n in range(3):
        row = columns[64 + classes + n : 64 + classes + n + 1]
        outs[11 + n][...] = row[:, 2 * group : 3 * group]
    first = min(64, up_size)
    outs[14][:, :first] = block[3 * group : 3 * group + 1, 64 : 64 + first]
    if up_size > first:
        outs[14][:, first:] = block[3 * group + 1 : 3 * group + 2, 64 : 64 + up_size - first]


def pick_kernel(table, source_ref, *refs, count):
    outs, held, sem_in, sem_out = refs[:-3], refs[-3], refs[-2], refs[-1]
    reads, writes = [], []
    for o, out in enumerate(outs):
        for j in range(count):
            n = o * count + j
            reads.append(pltpu.make_async_copy(source_ref.at[table[o, j]], held.at[n], sem_in.at[n]))
            writes.append(pltpu.make_async_copy(held.at[n], out.at[j], sem_out.at[n]))
    for copy in reads:
        copy.start()
    for read, write in zip(reads, writes):
        read.wait()
        write.start()
    for copy in writes:
        copy.wait()


def pick(table, source, outs, count):
    total = outs * count
    return pl.pallas_call(
        functools.partial(pick_kernel, count=count),
        grid_spec=pltpu.PrefetchScalarGridSpec(
            num_scalar_prefetch=1,
            grid=(1,),
            in_specs=[pl.BlockSpec(memory_space=pl.ANY)],
            out_specs=[pl.BlockSpec(memory_space=pl.ANY)] * outs,
            scratch_shapes=[
                pltpu.VMEM((total,) + source.shape[1:], source.dtype),
                pltpu.SemaphoreType.DMA((total,)),
                pltpu.SemaphoreType.DMA((total,)),
            ],
        ),
        out_shape=[jax.ShapeDtypeStruct((count,) + source.shape[1:], source.dtype)] * outs,
        compiler_params=params(),
        cost_estimate=cost(0, 2 * total * source[0].size * 2),
        name="pick",
    )(table, source)


def place_kernel(origin, position, *refs, samples):
    sources, out_ref, held, sem_in, sem_out = refs[:-4], refs[-4], refs[-3], refs[-2], refs[-1]
    for j in range(samples):
        for o, source in enumerate(sources):

            @pl.when(origin[j] == o)
            def _():
                pltpu.make_async_copy(source.at[position[j]], held.at[j], sem_in.at[j]).start()

    writes = []
    for j in range(samples):
        pltpu.make_async_copy(sources[0].at[0], held.at[j], sem_in.at[j]).wait()
        writes.append(pltpu.make_async_copy(held.at[j], out_ref.at[j], sem_out.at[j]))
        writes[-1].start()
    for copy in writes:
        copy.wait()


def place(origin, position, sources):
    samples = origin.shape[0]
    shape = sources[0].shape[1:]
    return pl.pallas_call(
        functools.partial(place_kernel, samples=samples),
        grid_spec=pltpu.PrefetchScalarGridSpec(
            num_scalar_prefetch=2,
            grid=(1,),
            in_specs=[pl.BlockSpec(memory_space=pl.ANY)] * len(sources),
            out_specs=pl.BlockSpec(memory_space=pl.ANY),
            scratch_shapes=[
                pltpu.VMEM((samples,) + shape, sources[0].dtype),
                pltpu.SemaphoreType.DMA((samples,)),
                pltpu.SemaphoreType.DMA((samples,)),
            ],
        ),
        out_shape=jax.ShapeDtypeStruct((samples,) + shape, sources[0].dtype),
        compiler_params=params(),
        cost_estimate=cost(0, 4 * samples * shape[0] * shape[1]),
        name="place",
    )(origin, position, *sources)


def routes(destination, samples, fsdp):
    group = lax.axis_index("dp")
    me = lax.axis_index("fsdp")
    capacity = 3 * samples // (2 * fsdp)
    span = fsdp * samples
    slots = lax.dynamic_slice_in_dim(destination, group * span, span).reshape(fsdp, samples)
    target = slots // samples - group * fsdp
    slot = slots % samples
    order = jnp.arange(samples, dtype=jnp.int32)
    before = order[None, :] < order[:, None]
    rank = jnp.sum(
        jnp.where((target[:, :, None] == target[:, None, :]) & before[None], 1, 0), axis=2
    ).astype(jnp.int32)
    offsets = (me + jnp.arange(1, fsdp, dtype=jnp.int32)) % fsdp
    places = jnp.arange(capacity, dtype=jnp.int32)

    def mine(table):
        return lax.dynamic_index_in_dim(table, me, 0, keepdims=False)

    my_target, my_slot, my_rank = mine(target), mine(slot), mine(rank)
    hit = (my_target[None, None, :] == offsets[:, None, None]) & (
        my_rank[None, None, :] == places[None, :, None]
    )
    out_pick = jnp.sum(jnp.where(hit, order[None, None, :], 0), axis=2).astype(jnp.int32)
    lands = (target == me)[:, :, None] & (slot[:, :, None] == order[None, None, :])
    origin_table = ((me - jnp.arange(fsdp, dtype=jnp.int32)) % fsdp)[:, None, None]
    in_origin = jnp.sum(jnp.where(lands, origin_table, 0), axis=(0, 1)).astype(jnp.int32)
    entry = jnp.where(origin_table == 0, order[None, :, None], rank[:, :, None])
    in_place = jnp.sum(jnp.where(lands, entry, 0), axis=(0, 1)).astype(jnp.int32)
    their_target = jnp.take(target, offsets, axis=0)
    their_slot = jnp.take(slot, offsets, axis=0)
    their_rank = jnp.take(rank, offsets, axis=0)
    hit = (their_target[:, None, :] == me) & (their_rank[:, None, :] == places[None, :, None])
    back_pick = jnp.sum(jnp.where(hit, their_slot[:, None, :], 0), axis=2).astype(jnp.int32)
    back_origin = ((me - my_target) % fsdp).astype(jnp.int32)
    back_place = jnp.where(back_origin == 0, my_slot, my_rank).astype(jnp.int32)
    return capacity, out_pick, in_origin, in_place, back_pick, back_origin, back_place


class Grid:
    def __init__(self, dp, fsdp, shard):
        self.size = {"c": 2, "x": fsdp // 2}
        self.size["z"] = 4 if dp % 4 == 0 else dp
        self.size["y"] = dp // self.size["z"]
        d, f = lax.axis_index("dp"), lax.axis_index("fsdp")
        self.at = {"z": d // self.size["y"], "y": d % self.size["y"], "x": f // 2, "c": f % 2}
        self.plain = 2 * shard % 16 != 0 or self.size["x"] != 2 or self.size["y"] != 2
        self.here = jnp.stack([self.at[a] for a in "zyxc"]).astype(jnp.int32)

    def number(self, at):
        dp = at["z"] * self.size["y"] + at["y"]
        return (dp * self.size["x"] + at["x"]) * 2 + at["c"]

    def send(self, array, axis, offset):
        pairs = []
        spans = [range(self.size[a]) for a in "zyxc"]
        for place in itertools.product(*spans):
            here = dict(zip("zyxc", place))
            there = dict(here)
            there[axis] = (here[axis] + offset) % self.size[axis]
            pairs.append((self.number(here), self.number(there)))
        return lax.ppermute(array, AXES, pairs)

    def spread(self, array, axis):
        return [array] + [self.send(array, axis, o) for o in range(1, self.size[axis])]

    def ordered(self, parts, axis):
        n, at = self.size[axis], self.at[axis]
        out = []
        for j in range(n):
            pick = parts[0]
            for o in range(1, n):
                pick = jnp.where((at - o) % n == j, parts[o], pick)
            out.append(pick)
        return jnp.concatenate(out, axis=0)


def tie(*values):
    return lax.optimization_barrier(values)


class Gather:
    def __init__(self, grid, mine, other, split):
        self.grid, self.mine, self.other, self.split = grid, mine, other, split
        self.rows, self.columns = 2 * mine.shape[0], 2 * mine.shape[1]
        self.plain = grid.plain
        self.parts = []

    def chips(self):
        if not self.plain:
            grid = self.grid
            self.chip = grid.ordered([self.mine, grid.send(self.other, "c", 1)], "c")

    def along_z(self):
        grid = self.grid
        if self.plain:
            shard = jnp.concatenate([self.mine, self.other], axis=1)
            self.parts = [lax.all_gather(shard, AXES, axis=0, tiled=True)]
            return
        self.line = grid.spread(self.chip, "z")

    def stack_z(self):
        if not self.plain:
            self.stack = jnp.concatenate(self.line, axis=0)

    def along_xy(self):
        if not self.plain:
            self.from_x = self.grid.send(self.stack, "x", 1)
            self.from_y = self.grid.send(self.stack, "y", 1)
            self.near = self.grid.send(self.stack, "c", 1)

    def diagonal(self):
        if not self.plain:
            self.one = self.grid.send(self.from_x[:, : self.split], "y", 1)
            self.two = self.grid.send(self.from_y[:, self.split :], "x", 1)
            self.near_x = self.grid.send(self.from_x, "c", 1)
            self.near_y = self.grid.send(self.from_y, "c", 1)

    def finish(self):
        if not self.plain:
            own = [self.stack, self.from_x, self.from_y, self.one, self.two]
            far = [self.near, self.near_x, self.near_y]
            far += [self.grid.send(self.one, "c", 1), self.grid.send(self.two, "c", 1)]
            self.parts = own + far

    def plan(self):
        if self.plain:
            return [(0, 0, self.parts[0].shape[0], self.columns, None, 0, 0, 0, 0)]
        copies = []
        steps = [(0, 0, 0), (0, 1, 0), (1, 0, 0), (1, 1, 0), (1, 1, self.split)]
        for n, part in enumerate(self.parts):
            dy, dx, begin = steps[n % 5]
            for k in range(self.grid.size["z"]):
                copies.append(
                    (n, k * self.rows, self.rows, part.shape[1], dy, dx, k, n // 5, begin)
                )
        return copies


def fetch(copies, here, size, parts, w_ref, sem):
    z, y, x, c = (here[n] for n in range(4))
    half = w_ref.shape[1] // 2
    started = []
    for n, (part, first, rows, columns, dy, dx, dz, far, begin) in enumerate(copies):
        if dy is None:
            to = w_ref
        else:
            line = (lax.rem(z + size["z"] - dz, size["z"]) * size["y"]) + lax.rem(y + dy, size["y"])
            row = (line * size["x"] + lax.rem(x + dx, size["x"])) * rows
            core = 1 - c if far else c
            to = w_ref.at[
                pl.ds(pl.multiple_of(row, 16), rows),
                pl.ds(pl.multiple_of(core * half + begin, 128), columns),
            ]
        started.append(
            pltpu.make_async_copy(parts[part].at[pl.ds(first, rows)], to, sem.at[n])
        )
    for copy in started:
        copy.start()
    for copy in started:
        copy.wait()


def line_rows(here, size, rows):
    z, y = here[0], here[1]
    return [
        pl.multiple_of(
            (lax.rem(z + oz, size["z"]) * size["y"] + lax.rem(y + oy, size["y"])) * rows, 16
        )
        for oy in range(size["y"])
        for oz in range(size["z"])
    ]


def tie_lists(*lists):
    flat = tie(*[value for part in lists for value in part])
    out = []
    for part in lists:
        out.append(list(flat[: len(part)]))
        flat = flat[len(part) :]
    return out


def add(*parts):
    total = parts[0].astype(F32)
    for part in parts[1:]:
        total = total + part.astype(F32)
    return total


class Scatter:
    def __init__(self, grid, mine, split):
        self.grid, self.mine, self.split = grid, mine, split

    def core(self, others):
        self.got = [self.grid.send(other, "c", 1) for other in others]

    def line(self, array, offset, axis):
        at = (self.grid.at["x"] + offset) % self.grid.size["x"]
        return lax.dynamic_index_in_dim(array, at, axis, keepdims=False)

    def begin(self):
        grid = self.grid
        total = jnp.concatenate([add(m, g) for m, g in zip(self.mine, self.got)], axis=1)
        sizes = [grid.size[a] for a in "yzx"]
        chip = total.shape[0] // math.prod(sizes)
        total = total.reshape(*sizes, chip, total.shape[1])
        left, right = total[..., : self.split], total[..., self.split :]
        self.keep_one, self.keep_two = left[0], self.line(right, 0, 2)
        self.out_one = [left[o].astype(BF16) for o in range(1, grid.size["y"])]
        self.out_two = [self.line(right, o, 2).astype(BF16) for o in range(1, grid.size["x"])]

    def first(self):
        grid = self.grid
        self.in_one = [grid.send(p, "y", o + 1) for o, p in enumerate(self.out_one)]
        self.in_two = [grid.send(p, "x", o + 1) for o, p in enumerate(self.out_two)]

    def second(self):
        grid = self.grid
        one, two = add(self.keep_one, *self.in_one), add(self.keep_two, *self.in_two)
        self.keep_one, self.keep_two = self.line(one, 0, 1), two[0]
        self.out_one = [self.line(one, o, 1).astype(BF16) for o in range(1, grid.size["x"])]
        self.out_two = [two[o].astype(BF16) for o in range(1, grid.size["y"])]

    def second_sends(self):
        grid = self.grid
        self.in_one = [grid.send(p, "x", o + 1) for o, p in enumerate(self.out_one)]
        self.in_two = [grid.send(p, "y", o + 1) for o, p in enumerate(self.out_two)]

    def third(self):
        grid = self.grid
        total = jnp.concatenate(
            [add(self.keep_one, *self.in_one), add(self.keep_two, *self.in_two)], axis=2
        )
        self.keep = total[0]
        self.came = [grid.send(total[o].astype(BF16), "z", o) for o in range(1, grid.size["z"])]

    def last(self):
        grid = self.grid
        total = add(self.keep, *self.came)
        c = grid.at["c"]
        share = total.shape[0] // 2
        mine = lax.dynamic_slice_in_dim(total, c * share, share, 0)
        far = lax.dynamic_slice_in_dim(total, (1 - c) * share, share, 0).astype(BF16)
        far = grid.send(far, "c", 1).astype(F32)
        return jnp.concatenate([jnp.where(c == 0, mine, far), jnp.where(c == 0, far, mine)], axis=1)


def exchange(part, fsdp, offset):
    return lax.ppermute(part, "fsdp", [(m, (m + offset) % fsdp) for m in range(fsdp)])


def body(
    tokens,
    input_weight,
    query_bias,
    value_bias,
    output_weight,
    output_bias,
    first_gain,
    first_shift,
    up_weight,
    up_bias,
    down_weight,
    down_bias,
    second_gain,
    second_shift,
    student_weight,
    student_bias,
    pool_query,
    pool_weight,
    pool_bias,
    class_weight,
    class_bias,
    lengths,
    exit_layer,
    destination,
    repacked_grad,
    logits_grad,
):
    samples, seq, width = tokens.shape
    count = samples * seq
    devices = lax.axis_size("dp") * lax.axis_size("fsdp")
    fsdp = lax.axis_size("fsdp")
    ff = up_weight.shape[1]
    stu = student_weight.shape[1]
    classes = class_weight.shape[1]
    block = min(count, 256)
    wide_block = min(count, 512)
    shard = width // devices
    grid = Grid(lax.axis_size("dp"), fsdp, shard)
    vectors = (
        query_bias,
        value_bias,
        output_bias,
        first_gain,
        first_shift,
        down_bias,
        second_gain,
        second_shift,
    )
    cut = 3 * width // 2
    here = grid.here
    if grid.plain:
        here = here * jnp.array([1, 1, 1, 0], jnp.int32)
    in_mine, in_other, ff_mine, ff_other = pack(
        here,
        input_weight,
        student_weight,
        output_weight,
        up_weight,
        up_bias,
        pool_weight,
        class_weight,
        logits_grad,
        (student_bias, pool_query, pool_bias),
        vectors,
    )
    wd = lax.all_gather(down_weight, AXES, axis=0, tiled=True)
    g_in = Gather(grid, in_mine, in_other, (cut + 128) // 256 * 128)
    g_in.chips()
    if not grid.plain:
        g_in.chip, destination = tie(g_in.chip, destination)
    g_in.along_z()
    capacity, out_pick, in_origin, in_place, back_pick, back_origin, back_place = routes(
        destination, samples, fsdp
    )
    alive = (exit_layer > LAYER).astype(jnp.int32)
    outgoing = pick(back_pick, repacked_grad, fsdp - 1, capacity)
    g_in.stack_z()
    returned = [exchange(outgoing[0], fsdp, 1)]
    if not grid.plain:
        g_in.stack, ff_mine, returned[0] = tie(g_in.stack, ff_mine, returned[0])
    g_ff = Gather(grid, ff_mine, ff_other, (ff + width) // 512 * 128 + 128)
    g_in.along_xy()
    g_in.diagonal()
    g_ff.chips()
    g_ff.along_z()
    g_ff.stack_z()
    g_in.finish()
    if not grid.plain:
        *g_in.parts, g_ff.stack = tie(*g_in.parts, g_ff.stack)
    last = exchange(outgoing[-1], fsdp, fsdp - 1)
    outgoing = outgoing[:-1]
    g_ff.along_xy()
    rows = tokens.reshape(count, width)
    qkv, prob, mixed, turned, vec, sv, pw, cw, ubm, cb, ws = attend(
        lengths, g_in, rows, seq, wide_block, stu, classes, devices, ff // devices
    )
    rest = list(outgoing[1:])
    if not grid.plain:
        mixed, g_ff.from_x, g_ff.from_y, g_ff.near, *rest = tie(
            mixed, g_ff.from_x, g_ff.from_y, g_ff.near, *rest
        )
    g_ff.diagonal()
    returned += [exchange(part, fsdp, o + 2) for o, part in enumerate(rest)] + [last]
    g_ff.finish()
    ub = jnp.broadcast_to(ubm[:, : ff // devices].reshape(1, ff), (8, ff))
    normed, factor, act, slope = up_part(g_ff, mixed, rows, vec, ub, block)
    act, *returned = tie(act, *returned)
    second_cot = place(back_origin, back_place, [repacked_grad] + returned)
    steps = count // wide_block
    lg = jnp.pad(
        logits_grad.reshape(steps, samples // steps, classes),
        ((0, 0), (0, 8 - samples // steps), (0, 128 - classes)),
    ).reshape(steps * 8, 128)
    second, dcot, logits, vgrad_two, sgrad, wsgrad, pwgrad, cwgrad, wd_grad = down_part(
        lengths,
        alive,
        act,
        normed,
        second_cot.reshape(count, width),
        lg,
        wd,
        vec,
        ws,
        sv,
        pw,
        cw,
        seq,
        wide_block,
        ff // 6,
    )
    student_logits = logits.reshape(steps, 8, 128)[:, : samples // steps, :classes].reshape(
        samples, classes
    ) + class_bias.astype(F32)
    second = second.reshape(samples, seq, width)
    wd_share = lax.psum_scatter(wd_grad, AXES, scatter_dimension=0, tiled=True)
    leaving = pick(out_pick, second, fsdp - 1, capacity)
    dcot, *leaving = tie(dcot, *leaving)
    arrived = [exchange(part, fsdp, o + 1) for o, part in enumerate(leaving)]
    one_cot, mcot, vgrad_one, ugrad, wu_other, wu_mine, wo_other, wo_mine = up_back(
        g_ff, dcot, slope, normed, factor, mixed, wd, vec, wide_block, ff // 6
    )
    mcot, wu_other, wo_other, *arrived = tie(mcot, wu_other, wo_other, *arrived)
    s_ff = Scatter(grid, [wo_mine, wu_mine], (ff + width) // 512 * 128 + 128)
    s_ff.core([wo_other, wu_other])
    repacked = place(in_origin, in_place, [second] + arrived)
    s_ff.begin()
    (mcot, repacked), s_ff.out_one, s_ff.out_two = tie_lists(
        (mcot, repacked), s_ff.out_one, s_ff.out_two
    )
    s_ff.first()
    pcot, vgrad_in = attend_back(mcot, qkv, prob, seq, wide_block)
    wi_other, wi_mine = input_grad(grid.here, turned, pcot, width // 2)
    wi_got = grid.send(wi_other, "c", 1)
    (wi_mine, vgrad_in, wd_share), s_ff.in_one, s_ff.in_two = tie_lists(
        (wi_mine, vgrad_in, wd_share), s_ff.in_one, s_ff.in_two
    )
    s_ff.second()
    s_ff.second_sends()
    ugm = jnp.pad(ugrad[0].reshape(devices, -1), ((0, 0), (0, 128 - ff // devices)))
    small_other, small_mine = small_pieces(
        grid,
        (vgrad_in, vgrad_one, vgrad_two, ugm, sgrad, wsgrad, pwgrad, cwgrad),
        classes,
        devices,
    )
    s_in = Scatter(grid, [wi_mine, small_mine], (cut + 128) // 2)
    s_in.got = [wi_got, grid.send(small_other, "c", 1)]
    s_in.begin()
    (pcot,), s_in.out_one, s_in.out_two, s_ff.in_one, s_ff.in_two = tie_lists(
        (pcot,), s_in.out_one, s_in.out_two, s_ff.in_one, s_ff.in_two
    )
    s_ff.third()
    s_in.first()
    tokens_grad = token_part(g_in, pcot, one_cot, wide_block)
    (tokens_grad,), s_in.in_one, s_in.in_two, s_ff.came = tie_lists(
        (tokens_grad,), s_in.in_one, s_in.in_two, s_ff.came
    )
    tokens_grad = tokens_grad.reshape(samples, seq, width)
    s_in.second()
    s_ff.came, s_in.out_one, s_in.out_two = tie_lists(s_ff.came, s_in.out_one, s_in.out_two)
    s_in.second_sends()
    ff_share = s_ff.last()
    s_in.third()
    in_share = s_in.last()
    class_bias_grad = cb[0, :classes]

    half = cut + 128
    input_share = jnp.concatenate([in_share[:, :cut], in_share[:, half : half + cut]], axis=1)
    flat = lambda size: jax.ShapeDtypeStruct((1, size), F32)
    group = stu // devices
    outs = pl.pallas_call(
        functools.partial(finish_kernel, group=group, classes=classes, up_size=ff // devices),
        out_shape=[flat(shard)] * 8
        + [
            jax.ShapeDtypeStruct((group, 64), F32),
            jax.ShapeDtypeStruct((group, 64), F32),
            jax.ShapeDtypeStruct((group, classes), F32),
        ]
        + [flat(group)] * 3
        + [flat(ff // devices)],
        name="finish",
    )(in_share[:, half + cut :])
    qb, vb, ob, g1, s1, db, g2, s2 = (o.reshape(-1) for o in outs[:8])
    ff_half = (ff + width) // 2
    wo_share, wu_share = (
        jnp.concatenate([ff_share[:, b:e], ff_share[:, ff_half + b : ff_half + e]], axis=1)
        for b, e in ((0, width // 2), (width // 2, ff_half))
    )
    return (
        repacked,
        student_logits,
        tokens_grad,
        input_share,
        qb,
        vb,
        wo_share,
        ob,
        g1,
        s1,
        wu_share,
        outs[14].reshape(-1),
        wd_share.astype(F32),
        db,
        g2,
        s2,
        in_share[:, cut:half],
        outs[11].reshape(-1),
        outs[12].reshape(-1),
        jnp.concatenate(outs[8:10], axis=1),
        outs[13].reshape(-1),
        outs[10],
        class_bias_grad,
    )


def solution(mesh):
    both = P(AXES)
    matrix = P(AXES, None)
    cube = P(AXES, None, None)
    return jax.shard_map(
        body,
        mesh=mesh,
        in_specs=(
            cube,
            matrix,
            both,
            both,
            matrix,
            both,
            both,
            both,
            matrix,
            both,
            matrix,
            both,
            both,
            both,
            matrix,
            both,
            both,
            matrix,
            both,
            matrix,
            P(),
            both,
            both,
            P(),
            cube,
            matrix,
        ),
        out_specs=(
            cube,
            matrix,
            cube,
            matrix,
            both,
            both,
            matrix,
            both,
            both,
            both,
            matrix,
            both,
            matrix,
            both,
            both,
            both,
            matrix,
            both,
            both,
            matrix,
            both,
            matrix,
            P(),
        ),
        check_vma=False,
    )
```

```python
import functools
import itertools
import math

import jax
import jax.numpy as jnp
from jax import lax
from jax.experimental import pallas as pl
from jax.experimental.pallas import tpu as pltpu
from jax.sharding import PartitionSpec as P

HEADS = 12
HEAD_DIM = 64
STU_HEADS = 2
LAYER = 6
EPS = 1e-06
MASKED = -1e30
AXES = ("dp", "fsdp")
F32 = jnp.float32
BF16 = jnp.bfloat16
VMEM_LIMIT = 60 * 1024 * 1024

QB, VB, OB, G1, S1, DB, G2, S2 = range(8)


def dot(left, right):
    return jnp.dot(left, right, preferred_element_type=F32)


def dot_nt(left, right):
    return lax.dot_general(left, right, (((1,), (1,)), ((), ())), preferred_element_type=F32)


def dot_tn(left, right):
    return lax.dot_general(left, right, (((0,), (0,)), ((), ())), preferred_element_type=F32)


def params(limit=VMEM_LIMIT):
    return pltpu.CompilerParams(vmem_limit_bytes=limit, dimension_semantics=("arbitrary",))


def cost(flops, nbytes):
    return pl.CostEstimate(
        flops=int(0.3 * flops), bytes_accessed=int(0.3 * nbytes), transcendentals=0
    )


def whole(shape, index=None):
    index = index or (0,) * len(shape)
    return pl.BlockSpec(shape, lambda i, *_: index, pipeline_mode=pl.Buffered(1))


def rows_spec(rows, width):
    return pl.BlockSpec((rows, width), lambda i, *_: (i, 0))


def kept(shape):
    return pl.BlockSpec(shape, lambda i, *_: (0,) * len(shape))


def layer_norm(total):
    mean = jnp.mean(total, axis=-1, keepdims=True)
    centered = total - mean
    factor = lax.rsqrt(jnp.mean(centered * centered, axis=-1, keepdims=True) + EPS)
    return centered * factor, factor


def layer_norm_back(cot, gain, normed, factor):
    scaled = cot * gain
    inner = (
        scaled
        - jnp.mean(scaled, axis=-1, keepdims=True)
        - normed * jnp.mean(scaled * normed, axis=-1, keepdims=True)
    )
    return factor * inner


def gelu_parts(up):
    phi = 0.5 + 0.5 * lax.erf(up * (1.0 / math.sqrt(2.0)))
    bell = jnp.exp(up * up * -0.5) * (1.0 / math.sqrt(2.0 * math.pi))
    return up * phi, phi + up * bell


def column_sum(matrix):
    return jnp.sum(matrix, axis=0, keepdims=True)


def stack_rows(rows, count):
    width = rows[0].shape[1]
    pad = count - len(rows)
    if pad:
        rows = list(rows) + [jnp.zeros((pad, width), F32)]
    return jnp.concatenate(rows, axis=0)


def one_hot_rows(count, width, group, stride, skip):
    row = lax.broadcasted_iota(jnp.int32, (count, width), 0)
    column = lax.broadcasted_iota(jnp.int32, (count, width), 1)
    shift = group.bit_length() - 1
    wanted = (row >> shift) * stride + skip + (row & (group - 1))
    return jnp.where(column == wanted, 1.0, 0.0).astype(BF16)


def turn_lanes(matrix):
    return pltpu.roll(matrix, 64, 1)


def read_small(block, vec_ref, sv_ref, pw_ref, cw_ref, ub_ref, cb_ref, stu, classes, devices, up_size):
    width = block.shape[0]
    shard = width // devices
    group = stu // devices
    lane = lax.broadcasted_iota(jnp.int32, (stu, 128), 1)
    left, right, rest = (
        dot(one_hot_rows(stu, width, group, shard, n * group), block) for n in range(3)
    )
    pw_ref[...] = jnp.where(lane < 64, turn_lanes(left), right).astype(BF16)
    rest = turn_lanes(rest)
    cw_ref[...] = jnp.where(lane < classes, rest, 0.0).astype(BF16)
    sv_ref[...] = rest.T[classes : classes + 8]
    low, high = (
        dot(one_hot_rows(devices, width, 1, shard, 3 * group + n), block) for n in range(2)
    )
    lane = lax.broadcasted_iota(jnp.int32, (devices, 128), 1)
    ub_ref[...] = jnp.where(lane < 64, turn_lanes(low), high)
    vec_ref[...] = block.astype(F32).T[:8]
    skip = 3 * group + pl.cdiv(up_size, 64)
    high, low = (dot(one_hot_rows(devices, width, 1, shard, skip + n), block) for n in range(2))
    cb_ref[...] = jnp.broadcast_to(turn_lanes(column_sum(high + low)), cb_ref.shape)


def pack_kernel(here, *refs, classes, group):
    wi_ref, ws_ref, wo_ref, wu_ref, ub_ref, pw_ref, cw_ref, lg_ref = refs[:8]
    columns, vectors = refs[8:11], refs[11:19]
    in_mine, in_other, ff_mine, ff_other, held = refs[19:]
    shard = wi_ref.shape[0]
    held[...] = jnp.zeros_like(held)
    for n, vector in enumerate(vectors):
        held[n : n + 1, :shard] = vector[...].astype(F32)
    left = held[:128].T[:shard]
    held[:8] = jnp.zeros((8, 128), F32)
    for n, column in enumerate(columns):
        held[classes + n : classes + n + 1, :group] = column[...].astype(F32)
    held[128 : 128 + group, :classes] = cw_ref[...].astype(F32)
    rest = held[128 : 128 + group] + held[:128].T[:group]
    up_size = ub_ref.shape[1]
    held[136:137, :up_size] = ub_ref[...].astype(F32)
    up = held[136:137]
    total = column_sum(lg_ref[...].astype(F32))
    high = total.astype(BF16).astype(F32)
    held[144:145, :classes] = high
    held[145:146, :classes] = total - high
    pool = pw_ref[...].astype(F32)
    rows = [turn_lanes(pool), pool, turn_lanes(rest), turn_lanes(up)]
    if up_size > 64:
        rows.append(up)
    rows.append(turn_lanes(held[144:146]))
    spare = shard - sum(r.shape[0] for r in rows)
    if spare:
        rows.append(jnp.zeros((spare, 128), F32))
    lane = lax.broadcasted_iota(jnp.int32, (shard, 128), 1)
    small = jnp.where(lane < 64, left, jnp.concatenate(rows, axis=0)).astype(BF16)
    cut = wi_ref.shape[1] // 2
    width = wo_ref.shape[1]
    part = ff_mine.shape[1] - width
    for core, (a, b, c, d) in enumerate(
        ((in_mine, in_other, ff_mine, ff_other), (in_other, in_mine, ff_other, ff_mine))
    ):

        @pl.when(here[3] == core)
        def _():
            a[:, :cut] = wi_ref[:, :cut]
            a[:, cut:] = ws_ref[...]
            b[:, :cut] = wi_ref[:, cut:]
            b[:, cut:] = small
            c[:, :width] = wo_ref[...]
            c[:, width:] = wu_ref[:, :part]
            d[...] = wu_ref[:, part:]


def pack(here, wi, ws, wo, wu, ub, pw, cw, lg, columns, vectors):
    shard = wi.shape[0]
    group, classes = cw.shape
    flat = lambda v: v.reshape(1, -1)
    first = jax.ShapeDtypeStruct((shard, wi.shape[1] // 2 + 128), BF16)
    second = jax.ShapeDtypeStruct((shard, (wo.shape[1] + wu.shape[1]) // 2), BF16)
    args = (wi, ws, wo, wu, flat(ub), pw, cw, lg, *map(flat, columns), *map(flat, vectors))
    return pl.pallas_call(
        functools.partial(pack_kernel, classes=classes, group=group),
        grid_spec=pltpu.PrefetchScalarGridSpec(
            num_scalar_prefetch=1,
            grid=(1,),
            in_specs=[whole(a.shape) for a in args],
            out_specs=[kept(o.shape) for o in (first, first, second, second)],
            scratch_shapes=[pltpu.VMEM((152, 128), F32)],
        ),
        out_shape=[first, first, second, second],
        compiler_params=params(),
        cost_estimate=cost(1e6, 1e6),
        name="pack",
    )(here, *args)


def attend_kernel(lens, here, *refs, copies, size, seq, width, stu, classes, devices, up_size):
    x_ref = refs[0]
    pieces = refs[1:-14]
    qkv_ref, prob_ref, mixed_ref, turned_ref, vec_ref, sv_ref, pw_ref = refs[-14:-7]
    cw_ref, ub_ref, cb_ref, ws_ref, w_ref, held, sem = refs[-7:]
    step = pl.program_id(0)
    half = w_ref.shape[1] // 2
    cut = half - 128

    @pl.when(step == 0)
    def _():
        fetch(copies, here, size, pieces, w_ref, sem)
        ws_ref[...] = w_ref[:, cut:half]
        read_small(
            w_ref[:, half + cut :],
            vec_ref,
            sv_ref,
            pw_ref,
            cw_ref,
            ub_ref,
            cb_ref,
            stu,
            classes,
            devices,
            up_size,
        )

    rows = x_ref.shape[0]
    lines = line_rows(here, size, width // (size["y"] * size["z"]))
    turn_lines(x_ref[...], lines, held, turned_ref, slice(0, rows))
    x = x_ref[...]
    vec = vec_ref[...]
    query = dot(x, w_ref[:, :width]) + vec[QB : QB + 1]
    qkv_ref[:, :width] = query.astype(BF16)
    split = 2 * width - cut
    qkv_ref[:, width:cut] = dot(x, w_ref[:, width:cut]).astype(BF16)
    qkv_ref[:, cut : 2 * width] = dot(x, w_ref[:, half : half + split]).astype(BF16)
    value = dot(x, w_ref[:, half + split : half + cut]) + vec[VB : VB + 1]
    qkv_ref[:, 2 * width :] = value.astype(BF16)
    lane = lax.broadcasted_iota(jnp.int32, (seq, 128), 1)
    first_head = lane < HEAD_DIM
    place = lax.broadcasted_iota(jnp.int32, (seq, 2 * seq), 0)
    scale = jnp.asarray(1.0 / math.sqrt(HEAD_DIM), BF16)
    for s in range(rows // seq):
        valid = place < lens[step * (rows // seq) + s]
        at = slice(s * seq, (s + 1) * seq)
        for pair in range(width // 128):
            low = pair * 128
            q = qkv_ref[at, low : low + 128] * scale
            k = qkv_ref[at, width + low : width + low + 128]
            v = qkv_ref[at, 2 * width + low : 2 * width + low + 128]
            zero = jnp.zeros_like(q)
            both = jnp.concatenate(
                [jnp.where(first_head, q, zero), jnp.where(first_head, zero, q)], axis=0
            )
            scores = jnp.where(valid, dot_nt(k, both), MASKED)
            raised = jnp.exp(scores - jnp.max(scores, axis=0, keepdims=True))
            share = raised * (1.0 / jnp.sum(raised, axis=0, keepdims=True))
            share = share.astype(BF16)
            prob_ref[s, pair] = share
            out = dot_tn(share, v)
            mixed_ref[at, low : low + 128] = jnp.where(first_head, out[:seq], out[seq:]).astype(BF16)


def attend(lens, gather, rows, seq, block, stu, classes, devices, up_size):
    copies, here, size = gather.plan(), gather.grid.here, gather.grid.size
    pieces = gather.parts
    count, width = rows.shape
    pairs = width // 128
    samples = block // seq
    columns = gather.columns
    small = [
        jax.ShapeDtypeStruct((8, width), F32),
        jax.ShapeDtypeStruct((8, stu), F32),
        jax.ShapeDtypeStruct((stu, stu), BF16),
        jax.ShapeDtypeStruct((stu, 128), BF16),
        jax.ShapeDtypeStruct((devices, 128), F32),
        jax.ShapeDtypeStruct((8, 128), F32),
        jax.ShapeDtypeStruct((width, stu), BF16),
    ]
    return pl.pallas_call(
        functools.partial(
            attend_kernel,
            copies=copies,
            size=size,
            seq=seq,
            width=width,
            stu=stu,
            classes=classes,
            devices=devices,
            up_size=up_size,
        ),
        grid_spec=pltpu.PrefetchScalarGridSpec(
            num_scalar_prefetch=2,
            grid=(count // block,),
            in_specs=[rows_spec(block, width)] + [pl.BlockSpec(memory_space=pl.ANY)] * len(pieces),
            out_specs=[
                rows_spec(block, 3 * width),
                pl.BlockSpec((samples, pairs, seq, 2 * seq), lambda i, *_: (i, 0, 0, 0)),
                rows_spec(block, width),
                pl.BlockSpec((width, block), lambda i, *_: (0, i)),
            ]
            + [kept(s.shape) for s in small],
            scratch_shapes=[
                pltpu.VMEM((width, columns), BF16),
                pltpu.VMEM((width, block), BF16),
                pltpu.SemaphoreType.DMA((len(copies),)),
            ],
        ),
        out_shape=[
            jax.ShapeDtypeStruct((count, 3 * width), BF16),
            jax.ShapeDtypeStruct((count // seq, pairs, seq, 2 * seq), BF16),
            jax.ShapeDtypeStruct((count, width), BF16),
            jax.ShapeDtypeStruct((width, count), BF16),
        ]
        + small,
        compiler_params=params(),
        cost_estimate=cost(2 * count * width * 3 * width * 2, 30e6),
        name="attend",
    )(lens, here, rows, *pieces)


def up_kernel(here, *refs, copies, size, chunk):
    mixed_ref, x_ref, vec_ref, ub_ref = refs[:4]
    pieces = refs[4:-7]
    norm_ref, factor_ref, low_ref, act_ref, slope_ref, w_ref, sem = refs[-7:]
    width = x_ref.shape[1]

    @pl.when(pl.program_id(0) == 0)
    def _():
        fetch(copies, here, size, pieces, w_ref, sem)

    vec = vec_ref[...]
    total = dot(mixed_ref[...], w_ref[:, :width]) + vec[OB : OB + 1] + x_ref[...].astype(F32)
    normed, factor = layer_norm(total)
    norm_ref[...] = normed
    factor_ref[...] = jnp.broadcast_to(factor, factor_ref.shape)
    low_ref[...] = (normed * vec[G1 : G1 + 1] + vec[S1 : S1 + 1]).astype(BF16)
    low = low_ref[...]
    for begin in range(0, act_ref.shape[1], chunk):
        at = slice(begin, begin + chunk)
        for first in range(0, low.shape[0], 128):
            rows = slice(first, first + 128)
            up = dot(low[rows], w_ref[:, width + begin : width + begin + chunk]) + ub_ref[0:1, at]
            act, slope = gelu_parts(up)
            act_ref[rows, at] = act.astype(BF16)
            slope_ref[rows, at] = slope.astype(BF16)


def up_part(gather, mixed, rows, vec, ub, block):
    copies, here, size = gather.plan(), gather.grid.here, gather.grid.size
    pieces = gather.parts
    count, width = rows.shape
    ff = gather.columns - width
    return pl.pallas_call(
        functools.partial(up_kernel, copies=copies, size=size, chunk=256),
        grid_spec=pltpu.PrefetchScalarGridSpec(
            num_scalar_prefetch=1,
            grid=(count // block,),
            in_specs=[
                rows_spec(block, width),
                rows_spec(block, width),
                whole(vec.shape),
                whole(ub.shape),
            ]
            + [pl.BlockSpec(memory_space=pl.ANY)] * len(pieces),
            out_specs=[
                rows_spec(block, width),
                rows_spec(block, 128),
                rows_spec(block, width),
                rows_spec(block, ff),
                rows_spec(block, ff),
            ],
            scratch_shapes=[
                pltpu.VMEM((width, gather.columns), BF16),
                pltpu.SemaphoreType.DMA((len(copies),)),
            ],
        ),
        out_shape=[
            jax.ShapeDtypeStruct((count, width), F32),
            jax.ShapeDtypeStruct((count, 128), F32),
            jax.ShapeDtypeStruct((count, width), BF16),
            jax.ShapeDtypeStruct((count, ff), BF16),
            jax.ShapeDtypeStruct((count, ff), BF16),
        ],
        compiler_params=params(),
        cost_estimate=cost(2 * count * width * (ff + width) * 2, 50e6),
        name="up_part",
    )(here, mixed, rows, vec, ub, *pieces)


def down_kernel(lens, alive, *refs, seq, steps, tile):
    act_hbm, norm_ref, cot_ref, lg_ref, wd_ref, vec_ref, ws_ref, sv_ref, pw_ref, cw_ref = refs[:10]
    second_ref, sum_ref, dcot_ref, logits_ref, vgrad_ref, sgrad_ref = refs[10:16]
    wsgrad_ref, pwgrad_ref, cwgrad_ref, grad_ref, act_all, turned, sem = refs[16:]
    step = pl.program_id(0)
    rows = norm_ref.shape[0]

    def load(n):
        at = pl.ds(pl.multiple_of(n * rows, rows), rows)
        return pltpu.make_async_copy(act_hbm.at[at], act_all.at[at], sem.at[n])

    @pl.when(step == 0)
    def _():
        load(0).start()

    @pl.when(step + 1 < steps)
    def _():
        load(step + 1).start()

    @pl.when(step < steps)
    def _():
        load(step).wait()
        at = pl.ds(pl.multiple_of(step * rows, rows), rows)
        down_rows(
            lens,
            alive,
            (act_all.at[at], norm_ref, cot_ref, lg_ref, wd_ref, vec_ref, ws_ref, sv_ref, pw_ref, cw_ref),
            (second_ref, sum_ref, dcot_ref, logits_ref, vgrad_ref, sgrad_ref),
            (wsgrad_ref, pwgrad_ref, cwgrad_ref),
            seq,
        )
        turned[:, at] = dcot_ref[...].T

    @pl.when(step >= steps)
    def _():
        at = pl.ds(pl.multiple_of((step - steps) * tile, tile), tile)
        grad_ref[...] = dot(turned[...], act_all[:, at]).astype(BF16).T


def down_rows(lens, alive, ins, outs, sums, seq):
    act_ref, norm_ref, cot_ref, lg_ref, wd_ref, vec_ref, ws_ref, sv_ref, pw_ref, cw_ref = ins
    second_ref, sum_ref, dcot_ref, logits_ref, vgrad_ref, sgrad_ref = outs
    wsgrad_ref, pwgrad_ref, cwgrad_ref = sums
    step = pl.program_id(0)
    rows = norm_ref.shape[0]
    samples = rows // seq
    vec = vec_ref[...]
    sv = sv_ref[...]
    stu = sv.shape[1]
    pool_width = stu // STU_HEADS
    pool_scale = 1.0 / math.sqrt(pool_width)

    @pl.when(step == 0)
    def _():
        vgrad_ref[...] = jnp.zeros_like(vgrad_ref)
        sgrad_ref[...] = jnp.zeros_like(sgrad_ref)
        wsgrad_ref[...] = jnp.zeros_like(wsgrad_ref)
        pwgrad_ref[...] = jnp.zeros_like(pwgrad_ref)
        cwgrad_ref[...] = jnp.zeros_like(cwgrad_ref)

    first = norm_ref[...] * vec[G1 : G1 + 1] + vec[S1 : S1 + 1]
    down = dot(act_ref[...], wd_ref[...]) + vec[DB : DB + 1]
    normed, factor = layer_norm(first + down)
    second = (normed * vec[G2 : G2 + 1] + vec[S2 : S2 + 1]).astype(BF16)
    reduced = (dot(second, ws_ref[...]) + sv[0:1]).astype(BF16)
    head_of = lax.broadcasted_iota(jnp.int32, (stu, stu), 0) // pool_width
    same = head_of == lax.broadcasted_iota(jnp.int32, (stu, stu), 1) // pool_width
    pool_query = sv[1:2]
    query_table = jnp.where(same, jnp.broadcast_to(pool_query, (stu, stu)), 0.0).astype(BF16)
    scores = dot_nt(reduced, query_table) * pool_scale
    place = lax.broadcasted_iota(jnp.int32, (seq, stu), 0)
    shares = []
    pooled_rows = []
    for s in range(samples):
        at = slice(s * seq, (s + 1) * seq)
        part = jnp.where(place < lens[step * samples + s], scores[at], MASKED)
        raised = jnp.exp(part - jnp.max(part, axis=0, keepdims=True))
        share = raised / jnp.sum(raised, axis=0, keepdims=True)
        shares.append(share)
        pooled_rows.append(column_sum(share * reduced[at].astype(F32)))
    pooled = stack_rows(pooled_rows, 8).astype(BF16)
    squashed = jnp.tanh(dot(pooled, pw_ref[...]) + sv[2:3])
    squashed_low = squashed.astype(BF16)
    logits_ref[...] = dot(squashed_low, cw_ref[...])
    lg = lg_ref[...]
    cwgrad_ref[...] += dot_tn(squashed_low, lg)
    hidden_cot = (dot_nt(lg, cw_ref[...]) * (1.0 - squashed * squashed)).astype(BF16)
    pwgrad_ref[...] += dot_tn(pooled, hidden_cot)
    pooled_cot = dot_nt(hidden_cot, pw_ref[...]).astype(BF16).astype(F32)
    query_grad = jnp.zeros((1, stu), F32)
    cots = []
    for s in range(samples):
        at = slice(s * seq, (s + 1) * seq)
        row = pooled_cot[s : s + 1]
        table = jnp.where(same, jnp.broadcast_to(row, (stu, stu)), 0.0).astype(BF16)
        share_cot = dot_nt(reduced[at], table)
        share = shares[s]
        score_cot = share * (share_cot - column_sum(share * share_cot))
        query_grad += column_sum(score_cot * reduced[at].astype(F32)) * pool_scale
        cots.append((share * row + score_cot * (pool_query * pool_scale)).astype(BF16))
    reduced_cot = jnp.concatenate(cots, axis=0)
    sgrad_ref[...] += stack_rows(
        [
            column_sum(reduced_cot.astype(F32)),
            query_grad,
            column_sum(hidden_cot.astype(F32)),
        ],
        8,
    )
    wsgrad_ref[...] += dot_tn(reduced_cot, second)
    back = dot_nt(reduced_cot, ws_ref[...])
    parts = []
    for s in range(samples):
        at = slice(s * seq, (s + 1) * seq)
        live = alive[step * samples + s] > 0
        parts.append(back[at] + jnp.where(live, cot_ref[at].astype(F32), 0.0))
        second_ref[at] = jnp.where(live, second[at], jnp.zeros_like(second[at]))
    total = jnp.concatenate(parts, axis=0)
    sum_cot = layer_norm_back(total, vec[G2 : G2 + 1], normed, factor)
    sum_ref[...] = sum_cot
    down_cot = sum_cot.astype(BF16)
    dcot_ref[...] = down_cot
    vgrad_ref[...] += stack_rows(
        [column_sum(total * normed), column_sum(total), column_sum(down_cot.astype(F32))], 8
    )


def down_part(lens, alive, act, normed, cot, lg, wd, vec, ws, sv, pw, cw, seq, block, tile):
    count, ff = act.shape
    width = normed.shape[1]
    stu = ws.shape[1]
    steps = count // block

    def block_rows(height, columns):
        return pl.BlockSpec((height, columns), lambda i, *_: (jnp.minimum(i, steps - 1), 0))

    return pl.pallas_call(
        functools.partial(down_kernel, seq=seq, steps=steps, tile=tile),
        grid_spec=pltpu.PrefetchScalarGridSpec(
            num_scalar_prefetch=2,
            grid=(steps + ff // tile,),
            in_specs=[
                pl.BlockSpec(memory_space=pl.ANY),
                block_rows(block, width),
                block_rows(block, width),
                block_rows(8, 128),
                whole(wd.shape),
                whole(vec.shape),
                whole(ws.shape),
                whole(sv.shape),
                whole(pw.shape),
                whole(cw.shape),
            ],
            out_specs=[
                block_rows(block, width),
                block_rows(block, width),
                block_rows(block, width),
                block_rows(8, 128),
                kept((8, width)),
                kept((8, stu)),
                kept((stu, width)),
                kept((stu, stu)),
                kept((stu, 128)),
                pl.BlockSpec((tile, width), lambda i, *_: (jnp.maximum(i - steps, 0), 0)),
            ],
            scratch_shapes=[
                pltpu.VMEM((count, ff), BF16),
                pltpu.VMEM((width, count), BF16),
                pltpu.SemaphoreType.DMA((steps,)),
            ],
        ),
        out_shape=[
            jax.ShapeDtypeStruct((count, width), BF16),
            jax.ShapeDtypeStruct((count, width), F32),
            jax.ShapeDtypeStruct((count, width), BF16),
            jax.ShapeDtypeStruct((steps * 8, 128), F32),
            jax.ShapeDtypeStruct((8, width), F32),
            jax.ShapeDtypeStruct((8, stu), F32),
            jax.ShapeDtypeStruct((stu, width), F32),
            jax.ShapeDtypeStruct((stu, stu), F32),
            jax.ShapeDtypeStruct((stu, 128), F32),
            jax.ShapeDtypeStruct((ff, width), BF16),
        ],
        compiler_params=params(),
        cost_estimate=cost(2 * count * width * ff * 4, 60e6),
        name="down_part",
    )(lens, alive, act, normed, cot, lg, wd, vec, ws, sv, pw, cw)


def turn_lines(block, lines, held, to, at):
    held[...] = block.T
    rows = to.shape[0] // len(lines)
    for n, line in enumerate(lines):
        to[n * rows : (n + 1) * rows, at] = held[pl.ds(line, rows)]


def up_back_kernel(here, *refs, copies, size, steps, chunk, tile):
    dcot_ref, slope_ref, sum_ref, norm_ref, factor_ref, low_ref, mixed_ref, wd_ref, vec_ref = refs[:9]
    pieces = refs[9:-15]
    one_ref, mcot_ref, vgrad_ref, ugrad_ref = refs[-15:-11]
    up_other, up_mine, out_other, out_mine = refs[-11:-7]
    w_ref, ucot_all, acot_all, low_turned, mixed_turned, held, sem = refs[-7:]
    step = pl.program_id(0)
    rows, width = dcot_ref.shape
    ff = slope_ref.shape[1]
    core = here[3]
    lines = line_rows(here, size, width // (size["y"] * size["z"]))

    @pl.when(step == 0)
    def _():
        fetch(copies, here, size, pieces, w_ref, sem)
        vgrad_ref[...] = jnp.zeros_like(vgrad_ref)
        ugrad_ref[...] = jnp.zeros_like(ugrad_ref)

    @pl.when(step < steps)
    def _():
        vec = vec_ref[...]
        at_rows = pl.ds(pl.multiple_of(step * rows, rows), rows)
        down_cot = dcot_ref[...]
        for begin in range(0, ff, chunk):
            at = slice(begin, begin + chunk)
            up_cot = dot_nt(down_cot, wd_ref[at, :]) * slope_ref[:, at].astype(F32)
            ugrad_ref[0:1, at] += column_sum(up_cot)
            ucot_all[at_rows, at] = up_cot.astype(BF16)
        turn_lines(low_ref[...], lines, held, low_turned, at_rows)
        turn_lines(mixed_ref[...], lines, held, mixed_turned, at_rows)
        cot = sum_ref[...] + dot_nt(ucot_all[at_rows, :], w_ref[:, width:])
        normed = norm_ref[...]
        one_cot = layer_norm_back(cot, vec[G1 : G1 + 1], normed, factor_ref[:, 0:1])
        one_ref[...] = one_cot
        low = one_cot.astype(BF16)
        acot_all[at_rows, :] = low
        mcot_ref[...] = dot_nt(low, w_ref[:, :width]).astype(BF16)
        vgrad_ref[...] += stack_rows(
            [column_sum(cot * normed), column_sum(cot), column_sum(one_cot)], 8
        )

    per = ff // 2 // tile

    def up_tile(n, half):
        first = (half * per + n) * tile
        return dot(low_turned[...], ucot_all[:, pl.ds(pl.multiple_of(first, 128), tile)])

    def out_tile(half):
        first = half * (width // 2)
        return dot(mixed_turned[...], acot_all[:, pl.ds(pl.multiple_of(first, 128), width // 2)])

    @pl.when((step >= steps) & (step < steps + per))
    def _():
        up_other[...] = up_tile(step - steps, 1 - core).astype(BF16)

    @pl.when(step == steps + per)
    def _():
        out_other[...] = out_tile(1 - core).astype(BF16)
        out_mine[...] = out_tile(core).astype(BF16)

    @pl.when(step > steps + per)
    def _():
        up_mine[...] = up_tile(step - steps - per - 1, core).astype(BF16)


def up_back(gather, dcot, slope, sum_two, normed, factor, low, mixed, wd, vec, block, tile):
    copies, here, size = gather.plan(), gather.grid.here, gather.grid.size
    pieces = gather.parts
    count, width = dcot.shape
    ff = slope.shape[1]
    steps = count // block
    per = ff // 2 // tile

    def block_rows(columns):
        return pl.BlockSpec((block, columns), lambda i, *_: (jnp.minimum(i, steps - 1), 0))

    def tiles(begin):
        return pl.BlockSpec(
            (width, tile), lambda i, *_: (0, jnp.clip(i - begin, 0, per - 1))
        )

    return pl.pallas_call(
        functools.partial(
            up_back_kernel, copies=copies, size=size, steps=steps, chunk=512, tile=tile
        ),
        grid_spec=pltpu.PrefetchScalarGridSpec(
            num_scalar_prefetch=1,
            grid=(steps + 2 * per + 1,),
            in_specs=[
                block_rows(width),
                block_rows(ff),
                block_rows(width),
                block_rows(width),
                block_rows(128),
                block_rows(width),
                block_rows(width),
                whole(wd.shape),
                whole(vec.shape),
            ]
            + [pl.BlockSpec(memory_space=pl.ANY)] * len(pieces),
            out_specs=[
                block_rows(width),
                block_rows(width),
                kept((8, width)),
                kept((8, ff)),
                tiles(steps),
                tiles(steps + per + 1),
                kept((width, width // 2)),
                kept((width, width // 2)),
            ],
            scratch_shapes=[
                pltpu.VMEM((width, gather.columns), BF16),
                pltpu.VMEM((count, ff), BF16),
                pltpu.VMEM((count, width), BF16),
                pltpu.VMEM((width, count), BF16),
                pltpu.VMEM((width, count), BF16),
                pltpu.VMEM((width, block), BF16),
                pltpu.SemaphoreType.DMA((len(copies),)),
            ],
        ),
        out_shape=[
            jax.ShapeDtypeStruct((count, width), F32),
            jax.ShapeDtypeStruct((count, width), BF16),
            jax.ShapeDtypeStruct((8, width), F32),
            jax.ShapeDtypeStruct((8, ff), F32),
            jax.ShapeDtypeStruct((width, ff // 2), BF16),
            jax.ShapeDtypeStruct((width, ff // 2), BF16),
            jax.ShapeDtypeStruct((width, width // 2), BF16),
            jax.ShapeDtypeStruct((width, width // 2), BF16),
        ],
        compiler_params=params(),
        cost_estimate=cost(2 * count * width * ff * 4, 60e6),
        name="up_back",
    )(here, dcot, slope, sum_two, normed, factor, low, mixed, wd, vec, *pieces)


def attend_back_kernel(mcot_ref, qkv_ref, prob_ref, pcot_ref, vgrad_ref, *, seq, width):
    @pl.when(pl.program_id(0) == 0)
    def _():
        vgrad_ref[...] = jnp.zeros_like(vgrad_ref)

    attend_back_rows(mcot_ref, qkv_ref, prob_ref, pcot_ref, vgrad_ref, seq, width)


def input_grad_kernel(here, turned_ref, pcot_ref, other, mine, *, per):
    step = pl.program_id(0)
    grad = dot(turned_ref[...], pcot_ref[...]).astype(BF16)

    @pl.when(step < per)
    def _():
        other[...] = grad

    @pl.when(step >= per)
    def _():
        mine[...] = grad


def input_grad(here, turned, pcot, tile):
    width, count = turned.shape
    half = pcot.shape[1] // 2
    per = half // tile

    def columns(i, t):
        core = t[3]
        return (0, jnp.where(i < per, (1 - core) * per + i, core * per + i - per))

    return pl.pallas_call(
        functools.partial(input_grad_kernel, per=per),
        grid_spec=pltpu.PrefetchScalarGridSpec(
            num_scalar_prefetch=1,
            grid=(2 * per,),
            in_specs=[whole((width, count)), pl.BlockSpec((count, tile), columns)],
            out_specs=[
                pl.BlockSpec((width, tile), lambda i, t: (0, jnp.minimum(i, per - 1))),
                pl.BlockSpec((width, tile), lambda i, t: (0, jnp.maximum(i - per, 0))),
            ],
        ),
        out_shape=[jax.ShapeDtypeStruct((width, half), BF16)] * 2,
        compiler_params=params(),
        cost_estimate=cost(4 * count * width * half, 20e6),
        name="input_grad",
    )(here, turned, pcot)


def attend_back_rows(mcot_ref, qkv_ref, prob_ref, pcot_ref, vgrad_ref, seq, width):
    rows = mcot_ref.shape[0]
    lane = lax.broadcasted_iota(jnp.int32, (seq, 128), 1)
    first_head = lane < HEAD_DIM
    scale = 1.0 / math.sqrt(HEAD_DIM)

    def split(part):
        zero = jnp.zeros_like(part)
        return jnp.concatenate(
            [jnp.where(first_head, part, zero), jnp.where(first_head, zero, part)], axis=0
        )

    for s in range(rows // seq):
        at = slice(s * seq, (s + 1) * seq)
        lows = range(0, width, 128)
        cots = [split(mcot_ref[at, low : low + 128]) for low in lows]
        share_cots = [
            dot_nt(qkv_ref[at, 2 * width + low : 2 * width + low + 128], cot)
            for low, cot in zip(lows, cots)
        ]
        values = [dot(prob_ref[s, n], cot) for n, cot in enumerate(cots)]
        for low, value in zip(lows, values):
            pcot_ref[at, 2 * width + low : 2 * width + low + 128] = value.astype(BF16)
        score_cots = []
        for n, share_cot in enumerate(share_cots):
            wide = prob_ref[s, n].astype(F32)
            product = wide * share_cot
            score_cots.append((product - wide * column_sum(product)).astype(BF16))
        keys = [
            dot(score, split(qkv_ref[at, low : low + 128])) * scale
            for low, score in zip(lows, score_cots)
        ]
        queries = [
            dot_tn(score, qkv_ref[at, width + low : width + low + 128]) * scale
            for low, score in zip(lows, score_cots)
        ]
        for low, key, query in zip(lows, keys, queries):
            pcot_ref[at, width + low : width + low + 128] = key.astype(BF16)
            pcot_ref[at, low : low + 128] = jnp.where(
                first_head, query[:seq], query[seq:]
            ).astype(BF16)
    vgrad_ref[...] += stack_rows(
        [
            column_sum(pcot_ref[:, :width].astype(F32)),
            column_sum(pcot_ref[:, 2 * width :].astype(F32)),
        ],
        8,
    )


def attend_back(mcot, qkv, prob, seq, block):
    count, width = mcot.shape
    pairs = width // 128
    return pl.pallas_call(
        functools.partial(attend_back_kernel, seq=seq, width=width),
        grid_spec=pltpu.PrefetchScalarGridSpec(
            num_scalar_prefetch=0,
            grid=(count // block,),
            in_specs=[
                rows_spec(block, width),
                rows_spec(block, 3 * width),
                pl.BlockSpec((block // seq, pairs, seq, 2 * seq), lambda i: (i, 0, 0, 0)),
            ],
            out_specs=[rows_spec(block, 3 * width), kept((8, width))],
        ),
        out_shape=[
            jax.ShapeDtypeStruct((count, 3 * width), BF16),
            jax.ShapeDtypeStruct((8, width), F32),
        ],
        compiler_params=params(),
        cost_estimate=cost(2 * count * width * 3 * width * 2, 30e6),
        name="attend_back",
    )(mcot, qkv, prob)


def token_kernel(here, *refs, copies, size):
    pcot_ref, one_ref = refs[:2]
    pieces = refs[2:-3]
    out_ref, w_ref, sem = refs[-3:]

    @pl.when(pl.program_id(0) == 0)
    def _():
        fetch(copies, here, size, pieces, w_ref, sem)

    half = w_ref.shape[1] // 2
    cut = half - 128
    out_ref[...] = (
        one_ref[...]
        + dot_nt(pcot_ref[:, :cut], w_ref[:, :cut])
        + dot_nt(pcot_ref[:, cut:], w_ref[:, half : half + cut])
    )


def token_part(gather, pcot, one_cot, block):
    copies, here, size = gather.plan(), gather.grid.here, gather.grid.size
    pieces = gather.parts
    count, width = one_cot.shape
    return pl.pallas_call(
        functools.partial(token_kernel, copies=copies, size=size),
        grid_spec=pltpu.PrefetchScalarGridSpec(
            num_scalar_prefetch=1,
            grid=(count // block,),
            in_specs=[rows_spec(block, 3 * width), rows_spec(block, width)]
            + [pl.BlockSpec(memory_space=pl.ANY)] * len(pieces),
            out_specs=rows_spec(block, width),
            scratch_shapes=[
                pltpu.VMEM((width, gather.columns), BF16),
                pltpu.SemaphoreType.DMA((len(copies),)),
            ],
        ),
        out_shape=jax.ShapeDtypeStruct((count, width), F32),
        compiler_params=params(),
        cost_estimate=cost(2 * count * width * 3 * width, 25e6),
        name="token_part",
    )(here, pcot, one_cot, *pieces)


def small_kernel(here, *refs, size, classes, devices):
    vin_ref, vone_ref, vtwo_ref, ugrad_ref, sgrad_ref, wsgrad_ref, pwgrad_ref, cwgrad_ref = refs[:8]
    other_ref, mine_ref, halves = refs[8:]
    width = vin_ref.shape[1]
    stu = sgrad_ref.shape[1]
    shard = width // devices
    group = stu // devices
    halves[0] = wsgrad_ref[...].T
    vin, vone, vtwo = vin_ref[...], vone_ref[...], vtwo_ref[...]
    rows = [vin[0:1], vin[1:2], vone[2:3], vone[0:1], vone[1:2], vtwo[2:3], vtwo[0:1], vtwo[1:2]]
    block = stack_rows(rows, 128).T
    lane = lax.broadcasted_iota(jnp.int32, (stu, 128), 1)
    high = lane >= 64
    pwgrad = pwgrad_ref[...]
    spare = jnp.zeros((classes, stu), F32)
    rest = jnp.concatenate(
        [spare, sgrad_ref[0:3], jnp.zeros((128 - classes - 3, stu), F32)], axis=0
    ).T
    rest = rest + jnp.where(lane < classes, cwgrad_ref[...], 0.0)
    for n, part in enumerate((turn_lanes(pwgrad), pwgrad, turn_lanes(rest))):
        part = jnp.where(high, part, 0.0).astype(BF16)
        block = block + dot_tn(one_hot_rows(stu, width, group, shard, n * group), part)
    ugrad = ugrad_ref[...]
    high = lax.broadcasted_iota(jnp.int32, ugrad.shape, 1) >= 64
    for n, part in enumerate((turn_lanes(ugrad), ugrad)):
        part = jnp.where(high, part, 0.0).astype(BF16)
        block = block + dot_tn(one_hot_rows(devices, width, 1, shard, 3 * group + n), part)
    halves[1] = block
    core = here[3]
    rows = width // (size["y"] * size["z"])
    for n, line in enumerate(line_rows(here, size, rows)):
        at = pl.ds(line, rows)
        other_ref[n * rows : (n + 1) * rows] = halves[1 - core, at].astype(BF16)
        mine_ref[n * rows : (n + 1) * rows] = halves[core, at].astype(BF16)


def small_pieces(grid, grads, classes, devices):
    width = grads[0].shape[1]
    return pl.pallas_call(
        functools.partial(small_kernel, size=grid.size, classes=classes, devices=devices),
        grid_spec=pltpu.PrefetchScalarGridSpec(
            num_scalar_prefetch=1,
            grid=(1,),
            in_specs=[whole(g.shape) for g in grads],
            out_specs=[kept((width, 128))] * 2,
            scratch_shapes=[pltpu.VMEM((2, width, 128), F32)],
        ),
        out_shape=[jax.ShapeDtypeStruct((width, 128), BF16)] * 2,
        compiler_params=params(),
        cost_estimate=cost(1e8, 2e6),
        name="small_pieces",
    )(grid.here, *grads)


def finish_kernel(block_ref, *outs, group, classes, up_size):
    block = block_ref[...]
    shard = block.shape[0]
    columns = jnp.concatenate([block, jnp.zeros((128 - shard, 128), F32)], axis=0).T
    for n in range(8):
        outs[n][...] = columns[n : n + 1, :shard]
    outs[8][...] = block[:group, 64:]
    outs[9][...] = block[group : 2 * group, 64:]
    outs[10][...] = block[2 * group : 3 * group, 64 : 64 + classes]
    for n in range(3):
        row = columns[64 + classes + n : 64 + classes + n + 1]
        outs[11 + n][...] = row[:, 2 * group : 3 * group]
    first = min(64, up_size)
    outs[14][:, :first] = block[3 * group : 3 * group + 1, 64 : 64 + first]
    if up_size > first:
        outs[14][:, first:] = block[3 * group + 1 : 3 * group + 2, 64 : 64 + up_size - first]


def pick_kernel(table, source_ref, *refs, count):
    outs, held, sem_in, sem_out = refs[:-3], refs[-3], refs[-2], refs[-1]
    reads, writes = [], []
    for o, out in enumerate(outs):
        for j in range(count):
            n = o * count + j
            reads.append(pltpu.make_async_copy(source_ref.at[table[o, j]], held.at[n], sem_in.at[n]))
            writes.append(pltpu.make_async_copy(held.at[n], out.at[j], sem_out.at[n]))
    for copy in reads:
        copy.start()
    for read, write in zip(reads, writes):
        read.wait()
        write.start()
    for copy in writes:
        copy.wait()


def pick(table, source, outs, count):
    total = outs * count
    return pl.pallas_call(
        functools.partial(pick_kernel, count=count),
        grid_spec=pltpu.PrefetchScalarGridSpec(
            num_scalar_prefetch=1,
            grid=(1,),
            in_specs=[pl.BlockSpec(memory_space=pl.ANY)],
            out_specs=[pl.BlockSpec(memory_space=pl.ANY)] * outs,
            scratch_shapes=[
                pltpu.VMEM((total,) + source.shape[1:], source.dtype),
                pltpu.SemaphoreType.DMA((total,)),
                pltpu.SemaphoreType.DMA((total,)),
            ],
        ),
        out_shape=[jax.ShapeDtypeStruct((count,) + source.shape[1:], source.dtype)] * outs,
        compiler_params=params(),
        cost_estimate=cost(0, 2 * total * source[0].size * 2),
        name="pick",
    )(table, source)


def place_kernel(origin, position, *refs, samples):
    sources, out_ref, held, sem_in, sem_out = refs[:-4], refs[-4], refs[-3], refs[-2], refs[-1]
    for j in range(samples):
        for o, source in enumerate(sources):

            @pl.when(origin[j] == o)
            def _():
                pltpu.make_async_copy(source.at[position[j]], held.at[j], sem_in.at[j]).start()

    writes = []
    for j in range(samples):
        pltpu.make_async_copy(sources[0].at[0], held.at[j], sem_in.at[j]).wait()
        writes.append(pltpu.make_async_copy(held.at[j], out_ref.at[j], sem_out.at[j]))
        writes[-1].start()
    for copy in writes:
        copy.wait()


def place(origin, position, sources):
    samples = origin.shape[0]
    shape = sources[0].shape[1:]
    return pl.pallas_call(
        functools.partial(place_kernel, samples=samples),
        grid_spec=pltpu.PrefetchScalarGridSpec(
            num_scalar_prefetch=2,
            grid=(1,),
            in_specs=[pl.BlockSpec(memory_space=pl.ANY)] * len(sources),
            out_specs=pl.BlockSpec(memory_space=pl.ANY),
            scratch_shapes=[
                pltpu.VMEM((samples,) + shape, sources[0].dtype),
                pltpu.SemaphoreType.DMA((samples,)),
                pltpu.SemaphoreType.DMA((samples,)),
            ],
        ),
        out_shape=jax.ShapeDtypeStruct((samples,) + shape, sources[0].dtype),
        compiler_params=params(),
        cost_estimate=cost(0, 4 * samples * shape[0] * shape[1]),
        name="place",
    )(origin, position, *sources)


def routes(destination, samples, fsdp):
    group = lax.axis_index("dp")
    me = lax.axis_index("fsdp")
    capacity = 3 * samples // (2 * fsdp)
    span = fsdp * samples
    slots = lax.dynamic_slice_in_dim(destination, group * span, span).reshape(fsdp, samples)
    target = slots // samples - group * fsdp
    slot = slots % samples
    order = jnp.arange(samples, dtype=jnp.int32)
    before = order[None, :] < order[:, None]
    rank = jnp.sum(
        jnp.where((target[:, :, None] == target[:, None, :]) & before[None], 1, 0), axis=2
    ).astype(jnp.int32)
    offsets = (me + jnp.arange(1, fsdp, dtype=jnp.int32)) % fsdp
    places = jnp.arange(capacity, dtype=jnp.int32)

    def mine(table):
        return lax.dynamic_index_in_dim(table, me, 0, keepdims=False)

    my_target, my_slot, my_rank = mine(target), mine(slot), mine(rank)
    hit = (my_target[None, None, :] == offsets[:, None, None]) & (
        my_rank[None, None, :] == places[None, :, None]
    )
    out_pick = jnp.sum(jnp.where(hit, order[None, None, :], 0), axis=2).astype(jnp.int32)
    lands = (target == me)[:, :, None] & (slot[:, :, None] == order[None, None, :])
    origin_table = ((me - jnp.arange(fsdp, dtype=jnp.int32)) % fsdp)[:, None, None]
    in_origin = jnp.sum(jnp.where(lands, origin_table, 0), axis=(0, 1)).astype(jnp.int32)
    entry = jnp.where(origin_table == 0, order[None, :, None], rank[:, :, None])
    in_place = jnp.sum(jnp.where(lands, entry, 0), axis=(0, 1)).astype(jnp.int32)
    their_target = jnp.take(target, offsets, axis=0)
    their_slot = jnp.take(slot, offsets, axis=0)
    their_rank = jnp.take(rank, offsets, axis=0)
    hit = (their_target[:, None, :] == me) & (their_rank[:, None, :] == places[None, :, None])
    back_pick = jnp.sum(jnp.where(hit, their_slot[:, None, :], 0), axis=2).astype(jnp.int32)
    back_origin = ((me - my_target) % fsdp).astype(jnp.int32)
    back_place = jnp.where(back_origin == 0, my_slot, my_rank).astype(jnp.int32)
    return capacity, out_pick, in_origin, in_place, back_pick, back_origin, back_place


class Grid:
    def __init__(self, dp, fsdp, shard):
        self.size = {"c": 2, "x": fsdp // 2}
        self.size["z"] = 4 if dp % 4 == 0 else dp
        self.size["y"] = dp // self.size["z"]
        d, f = lax.axis_index("dp"), lax.axis_index("fsdp")
        self.at = {"z": d // self.size["y"], "y": d % self.size["y"], "x": f // 2, "c": f % 2}
        self.plain = 2 * shard % 16 != 0 or self.size["x"] != 2 or self.size["y"] != 2
        self.here = jnp.stack([self.at[a] for a in "zyxc"]).astype(jnp.int32)

    def number(self, at):
        dp = at["z"] * self.size["y"] + at["y"]
        return (dp * self.size["x"] + at["x"]) * 2 + at["c"]

    def send(self, array, axis, offset):
        pairs = []
        spans = [range(self.size[a]) for a in "zyxc"]
        for place in itertools.product(*spans):
            here = dict(zip("zyxc", place))
            there = dict(here)
            there[axis] = (here[axis] + offset) % self.size[axis]
            pairs.append((self.number(here), self.number(there)))
        return lax.ppermute(array, AXES, pairs)

    def spread(self, array, axis):
        return [array] + [self.send(array, axis, o) for o in range(1, self.size[axis])]

    def ordered(self, parts, axis):
        n, at = self.size[axis], self.at[axis]
        out = []
        for j in range(n):
            pick = parts[0]
            for o in range(1, n):
                pick = jnp.where((at - o) % n == j, parts[o], pick)
            out.append(pick)
        return jnp.concatenate(out, axis=0)


def tie(*values):
    return lax.optimization_barrier(values)


class Gather:
    def __init__(self, grid, mine, other, split):
        self.grid, self.mine, self.other, self.split = grid, mine, other, split
        self.rows, self.columns = 2 * mine.shape[0], 2 * mine.shape[1]
        self.plain = grid.plain
        self.parts = []

    def along_z(self):
        grid = self.grid
        if self.plain:
            shard = jnp.concatenate([self.mine, self.other], axis=1)
            self.parts = [lax.all_gather(shard, AXES, axis=0, tiled=True)]
            return
        chip = grid.ordered([self.mine, grid.send(self.other, "c", 1)], "c")
        self.stack = jnp.concatenate(grid.spread(chip, "z"), axis=0)

    def along_xy(self):
        if not self.plain:
            self.from_x = self.grid.send(self.stack, "x", 1)
            self.from_y = self.grid.send(self.stack, "y", 1)
            self.near = self.grid.send(self.stack, "c", 1)

    def diagonal(self):
        if not self.plain:
            self.one = self.grid.send(self.from_x[:, : self.split], "y", 1)
            self.two = self.grid.send(self.from_y[:, self.split :], "x", 1)
            self.near_x = self.grid.send(self.from_x, "c", 1)
            self.near_y = self.grid.send(self.from_y, "c", 1)

    def finish(self):
        if not self.plain:
            own = [self.stack, self.from_x, self.from_y, self.one, self.two]
            far = [self.near, self.near_x, self.near_y]
            far += [self.grid.send(self.one, "c", 1), self.grid.send(self.two, "c", 1)]
            self.parts = own + far

    def plan(self):
        if self.plain:
            return [(0, 0, self.parts[0].shape[0], self.columns, None, 0, 0, 0, 0)]
        copies = []
        steps = [(0, 0, 0), (0, 1, 0), (1, 0, 0), (1, 1, 0), (1, 1, self.split)]
        for n, part in enumerate(self.parts):
            dy, dx, begin = steps[n % 5]
            for k in range(self.grid.size["z"]):
                copies.append(
                    (n, k * self.rows, self.rows, part.shape[1], dy, dx, k, n // 5, begin)
                )
        return copies


def fetch(copies, here, size, parts, w_ref, sem):
    z, y, x, c = (here[n] for n in range(4))
    half = w_ref.shape[1] // 2
    started = []
    for n, (part, first, rows, columns, dy, dx, dz, far, begin) in enumerate(copies):
        if dy is None:
            to = w_ref
        else:
            line = (lax.rem(z + size["z"] - dz, size["z"]) * size["y"]) + lax.rem(y + dy, size["y"])
            row = (line * size["x"] + lax.rem(x + dx, size["x"])) * rows
            core = 1 - c if far else c
            to = w_ref.at[
                pl.ds(pl.multiple_of(row, 16), rows),
                pl.ds(pl.multiple_of(core * half + begin, 128), columns),
            ]
        started.append(
            pltpu.make_async_copy(parts[part].at[pl.ds(first, rows)], to, sem.at[n])
        )
    for copy in started:
        copy.start()
    for copy in started:
        copy.wait()


def line_rows(here, size, rows):
    z, y = here[0], here[1]
    return [
        pl.multiple_of(
            (lax.rem(z + oz, size["z"]) * size["y"] + lax.rem(y + oy, size["y"])) * rows, 16
        )
        for oy in range(size["y"])
        for oz in range(size["z"])
    ]


def tie_lists(*lists):
    flat = tie(*[value for part in lists for value in part])
    out = []
    for part in lists:
        out.append(list(flat[: len(part)]))
        flat = flat[len(part) :]
    return out


def add(*parts):
    total = parts[0].astype(F32)
    for part in parts[1:]:
        total = total + part.astype(F32)
    return total


class Scatter:
    def __init__(self, grid, mine, split):
        self.grid, self.mine, self.split = grid, mine, split

    def core(self, others):
        self.got = [self.grid.send(other, "c", 1) for other in others]

    def line(self, array, offset, axis):
        at = (self.grid.at["x"] + offset) % self.grid.size["x"]
        return lax.dynamic_index_in_dim(array, at, axis, keepdims=False)

    def begin(self):
        grid = self.grid
        total = jnp.concatenate([add(m, g) for m, g in zip(self.mine, self.got)], axis=1)
        sizes = [grid.size[a] for a in "yzx"]
        chip = total.shape[0] // math.prod(sizes)
        total = total.reshape(*sizes, chip, total.shape[1])
        left, right = total[..., : self.split], total[..., self.split :]
        self.keep_one, self.keep_two = left[0], self.line(right, 0, 2)
        self.out_one = [left[o].astype(BF16) for o in range(1, grid.size["y"])]
        self.out_two = [self.line(right, o, 2).astype(BF16) for o in range(1, grid.size["x"])]

    def first(self):
        grid = self.grid
        self.in_one = [grid.send(p, "y", o + 1) for o, p in enumerate(self.out_one)]
        self.in_two = [grid.send(p, "x", o + 1) for o, p in enumerate(self.out_two)]

    def second(self):
        grid = self.grid
        one, two = add(self.keep_one, *self.in_one), add(self.keep_two, *self.in_two)
        self.keep_one, self.keep_two = self.line(one, 0, 1), two[0]
        self.in_one = [
            grid.send(self.line(one, o, 1).astype(BF16), "x", o) for o in range(1, grid.size["x"])
        ]
        self.in_two = [grid.send(two[o].astype(BF16), "y", o) for o in range(1, grid.size["y"])]

    def third(self):
        grid = self.grid
        total = jnp.concatenate(
            [add(self.keep_one, *self.in_one), add(self.keep_two, *self.in_two)], axis=2
        )
        self.keep = total[0]
        self.came = [grid.send(total[o].astype(BF16), "z", o) for o in range(1, grid.size["z"])]

    def last(self):
        grid = self.grid
        total = add(self.keep, *self.came)
        c = grid.at["c"]
        share = total.shape[0] // 2
        mine = lax.dynamic_slice_in_dim(total, c * share, share, 0)
        far = lax.dynamic_slice_in_dim(total, (1 - c) * share, share, 0).astype(BF16)
        far = grid.send(far, "c", 1).astype(F32)
        return jnp.concatenate([jnp.where(c == 0, mine, far), jnp.where(c == 0, far, mine)], axis=1)


def exchange(part, fsdp, offset):
    return lax.ppermute(part, "fsdp", [(m, (m + offset) % fsdp) for m in range(fsdp)])


def body(
    tokens,
    input_weight,
    query_bias,
    value_bias,
    output_weight,
    output_bias,
    first_gain,
    first_shift,
    up_weight,
    up_bias,
    down_weight,
    down_bias,
    second_gain,
    second_shift,
    student_weight,
    student_bias,
    pool_query,
    pool_weight,
    pool_bias,
    class_weight,
    class_bias,
    lengths,
    exit_layer,
    destination,
    repacked_grad,
    logits_grad,
):
    samples, seq, width = tokens.shape
    count = samples * seq
    devices = lax.axis_size("dp") * lax.axis_size("fsdp")
    fsdp = lax.axis_size("fsdp")
    ff = up_weight.shape[1]
    stu = student_weight.shape[1]
    classes = class_weight.shape[1]
    block = min(count, 256)
    wide_block = min(count, 512)
    shard = width // devices
    grid = Grid(lax.axis_size("dp"), fsdp, shard)
    vectors = (
        query_bias,
        value_bias,
        output_bias,
        first_gain,
        first_shift,
        down_bias,
        second_gain,
        second_shift,
    )
    cut = 3 * width // 2
    here = grid.here
    if grid.plain:
        here = here * jnp.array([1, 1, 1, 0], jnp.int32)
    in_mine, in_other, ff_mine, ff_other = pack(
        here,
        input_weight,
        student_weight,
        output_weight,
        up_weight,
        up_bias,
        pool_weight,
        class_weight,
        logits_grad,
        (student_bias, pool_query, pool_bias),
        vectors,
    )
    capacity, out_pick, in_origin, in_place, back_pick, back_origin, back_place = routes(
        destination, samples, fsdp
    )
    alive = (exit_layer > LAYER).astype(jnp.int32)

    wd = lax.all_gather(down_weight, AXES, axis=0, tiled=True)
    g_in = Gather(grid, in_mine, in_other, (cut + 128) // 256 * 128)
    g_in.along_z()
    outgoing = pick(back_pick, repacked_grad, fsdp - 1, capacity)
    returned = [exchange(outgoing[0], fsdp, 1)]
    if not grid.plain:
        g_in.stack, ff_mine, returned[0] = tie(g_in.stack, ff_mine, returned[0])
    g_ff = Gather(grid, ff_mine, ff_other, (ff + width) // 512 * 128 + 128)
    g_in.along_xy()
    g_in.diagonal()
    g_ff.along_z()
    g_in.finish()
    if not grid.plain:
        *g_in.parts, g_ff.stack = tie(*g_in.parts, g_ff.stack)
    g_ff.along_xy()
    rows = tokens.reshape(count, width)
    qkv, prob, mixed, turned, vec, sv, pw, cw, ubm, cb, ws = attend(
        lengths, g_in, rows, seq, wide_block, stu, classes, devices, ff // devices
    )
    rest = list(outgoing[1:])
    if not grid.plain:
        mixed, g_ff.from_x, g_ff.from_y, g_ff.near, *rest = tie(
            mixed, g_ff.from_x, g_ff.from_y, g_ff.near, *rest
        )
    g_ff.diagonal()
    returned += [exchange(part, fsdp, o + 2) for o, part in enumerate(rest)]
    g_ff.finish()
    ub = jnp.broadcast_to(ubm[:, : ff // devices].reshape(1, ff), (8, ff))
    normed, factor, low, act, slope = up_part(g_ff, mixed, rows, vec, ub, block)
    act, *returned = tie(act, *returned)
    second_cot = place(back_origin, back_place, [repacked_grad] + returned)
    steps = count // wide_block
    lg = jnp.pad(
        logits_grad.reshape(steps, samples // steps, classes),
        ((0, 0), (0, 8 - samples // steps), (0, 128 - classes)),
    ).reshape(steps * 8, 128)
    second, sum_two, dcot, logits, vgrad_two, sgrad, wsgrad, pwgrad, cwgrad, wd_grad = down_part(
        lengths,
        alive,
        act,
        normed,
        second_cot.reshape(count, width),
        lg,
        wd,
        vec,
        ws,
        sv,
        pw,
        cw,
        seq,
        wide_block,
        ff // 6,
    )
    student_logits = logits.reshape(steps, 8, 128)[:, : samples // steps, :classes].reshape(
        samples, classes
    ) + class_bias.astype(F32)
    second = second.reshape(samples, seq, width)
    wd_share = lax.psum_scatter(wd_grad, AXES, scatter_dimension=0, tiled=True)
    leaving = pick(out_pick, second, fsdp - 1, capacity)
    dcot, *leaving = tie(dcot, *leaving)
    arrived = [exchange(part, fsdp, o + 1) for o, part in enumerate(leaving)]
    one_cot, mcot, vgrad_one, ugrad, wu_other, wu_mine, wo_other, wo_mine = up_back(
        g_ff, dcot, slope, sum_two, normed, factor, low, mixed, wd, vec, block, ff // 6
    )
    mcot, wu_other, wo_other, *arrived = tie(mcot, wu_other, wo_other, *arrived)
    s_ff = Scatter(grid, [wo_mine, wu_mine], (ff + width) // 512 * 128 + 128)
    s_ff.core([wo_other, wu_other])
    s_ff.begin()
    mcot, *out = tie(mcot, *s_ff.out_one, *s_ff.out_two)
    s_ff.out_one, s_ff.out_two = out[: len(s_ff.out_one)], out[len(s_ff.out_one) :]
    s_ff.first()
    pcot, vgrad_in = attend_back(mcot, qkv, prob, seq, wide_block)
    (pcot, vgrad_in), s_ff.in_one, s_ff.in_two = tie_lists(
        (pcot, vgrad_in), s_ff.in_one, s_ff.in_two
    )
    s_ff.second()
    ugm = jnp.pad(ugrad[0].reshape(devices, -1), ((0, 0), (0, 128 - ff // devices)))
    small_other, small_mine = small_pieces(
        grid,
        (vgrad_in, vgrad_one, vgrad_two, ugm, sgrad, wsgrad, pwgrad, cwgrad),
        classes,
        devices,
    )
    wi_other, wi_mine = input_grad(grid.here, turned, pcot, width // 2)
    (wi_other, small_other, wd_share), s_ff.in_one, s_ff.in_two, arrived = tie_lists(
        (wi_other, small_other, wd_share), s_ff.in_one, s_ff.in_two, arrived
    )
    s_in = Scatter(grid, [wi_mine, small_mine], (cut + 128) // 2)
    s_in.core([wi_other, small_other])
    s_ff.third()
    repacked = place(in_origin, in_place, [second] + arrived)
    s_in.begin()
    (pcot, repacked), s_in.out_one, s_in.out_two = tie_lists(
        (pcot, repacked), s_in.out_one, s_in.out_two
    )
    s_in.first()
    tokens_grad = token_part(g_in, pcot, one_cot, wide_block)
    (tokens_grad,), s_in.in_one, s_in.in_two, s_ff.came = tie_lists(
        (tokens_grad,), s_in.in_one, s_in.in_two, s_ff.came
    )
    tokens_grad = tokens_grad.reshape(samples, seq, width)
    s_in.second()
    ff_share = s_ff.last()
    s_in.third()
    in_share = s_in.last()
    class_bias_grad = cb[0, :classes]

    half = cut + 128
    input_share = jnp.concatenate([in_share[:, :cut], in_share[:, half : half + cut]], axis=1)
    flat = lambda size: jax.ShapeDtypeStruct((1, size), F32)
    group = stu // devices
    outs = pl.pallas_call(
        functools.partial(finish_kernel, group=group, classes=classes, up_size=ff // devices),
        out_shape=[flat(shard)] * 8
        + [
            jax.ShapeDtypeStruct((group, 64), F32),
            jax.ShapeDtypeStruct((group, 64), F32),
            jax.ShapeDtypeStruct((group, classes), F32),
        ]
        + [flat(group)] * 3
        + [flat(ff // devices)],
        name="finish",
    )(in_share[:, half + cut :])
    qb, vb, ob, g1, s1, db, g2, s2 = (o.reshape(-1) for o in outs[:8])
    ff_half = (ff + width) // 2
    wo_share, wu_share = (
        jnp.concatenate([ff_share[:, b:e], ff_share[:, ff_half + b : ff_half + e]], axis=1)
        for b, e in ((0, width // 2), (width // 2, ff_half))
    )
    return (
        repacked,
        student_logits,
        tokens_grad,
        input_share,
        qb,
        vb,
        wo_share,
        ob,
        g1,
        s1,
        wu_share,
        outs[14].reshape(-1),
        wd_share.astype(F32),
        db,
        g2,
        s2,
        in_share[:, cut:half],
        outs[11].reshape(-1),
        outs[12].reshape(-1),
        jnp.concatenate(outs[8:10], axis=1),
        outs[13].reshape(-1),
        outs[10],
        class_bias_grad,
    )


def solution(mesh):
    both = P(AXES)
    matrix = P(AXES, None)
    cube = P(AXES, None, None)
    return jax.shard_map(
        body,
        mesh=mesh,
        in_specs=(
            cube,
            matrix,
            both,
            both,
            matrix,
            both,
            both,
            both,
            matrix,
            both,
            matrix,
            both,
            both,
            both,
            matrix,
            both,
            both,
            matrix,
            both,
            matrix,
            P(),
            both,
            both,
            P(),
            cube,
            matrix,
        ),
        out_specs=(
            cube,
            matrix,
            cube,
            matrix,
            both,
            both,
            matrix,
            both,
            both,
            both,
            matrix,
            both,
            matrix,
            both,
            both,
            both,
            matrix,
            both,
            both,
            matrix,
            both,
            matrix,
            P(),
        ),
        check_vma=False,
    )
```
